128 devices in a mesh: inst: 8 (over z, x_lo), space: 16 (over x_hi, y, core).
Axes of the slice: x: 4 (x_hi: 2, x_lo: 2; x = x_hi * 2 + x_lo), y: 4, z: 4, core: 2. Of those that a mesh axis runs over, the one named last changes fastest.
Arguments:
- basis: float32 [8, 8, 7, 131072], P(None, 'inst', None, 'space'), may hold values from -13 to 13
- flux_adjoint: bfloat16 [8, 7, 7, 7, 131072], P('inst', None, None, None, 'space'), may hold values from -0.875 to 0.875
- recon_adjoint: bfloat16 [8, 7, 7, 7, 131072], P('inst', None, None, None, 'space'), may hold values from -0.875 to 0.875
- pseudo_time: float32 [131072], P('space'), may hold values from 0.5 to 2
- vol_omega: float32 [131072], P('space'), may hold values from 0.25 to 1
- block_ids: int32 [32], replicated, may hold values from 0 to 31, each once
- neighbour: int32 [32, 6], replicated, may hold values from -1 to 191, as said below
- orient: int32 [32, 6], replicated, may hold values from 0 to 7, as said below
Outputs:
- next_vector: float32 [8, 7, 131072], P('inst', None, 'space')
- hessenberg: float32 [9], replicated
The draws below stay inside these ranges and needn't reach their ends.
Inputs may be any that keep to these rules, and one draw needn't show every extreme that they name: `block_ids`: a permutation of the block numbers. `neighbour`: exactly 32 faces are walls; every other face touches one different face, the pairing is mutual. `orient`: walls have 0; the codes of the two sides of a connection undo each other.
All inputs are finite; a program needn't handle non-finite values.
Results may differ from the reference program's by a relative error of at most 0.0003.
Values sent between devices are 32-bit elements; how exact they have to be, the bound alone decides.
No kernel may reach another device: no remote copies, remote signals or barrier semaphores. Data moves between devices by JAX's collectives and lax.ppermute only.
A program may use at most 128 MiB of HBM per device.

```python
import math
import jax
import jax.numpy as jnp
from jax import lax

VARS = 7
BLOCK_EDGE = 16
KRYLOV = 8
INST = 8
BLOCKS = 32
CELLS = 131072
WALL_FACES = 32


def paired_faces(key):
    total = BLOCKS * 6
    shuffled = jax.random.permutation(jax.random.fold_in(key, 11), total - 1).astype(jnp.int32)
    order = jnp.concatenate([shuffled, jnp.full((1,), total - 1, jnp.int32)])
    paired = order[WALL_FACES:].reshape(-1, 2)
    first = paired[:, 0]
    second = paired[:, 1]
    codes = jax.random.randint(jax.random.fold_in(key, 12), (first.shape[0],), 0, 8).astype(jnp.int32)
    codes = codes.at[0].set(7)
    swapped = (codes & 1) + (codes & 2) * 2 + (codes & 4) // 2
    undoing = jnp.where(codes & 1 == 1, swapped, codes)
    partner = jnp.full((total,), -1, jnp.int32).at[first].set(second).at[second].set(first)
    turned = jnp.zeros((total,), jnp.int32).at[first].set(codes).at[second].set(undoing)
    return (partner.reshape(BLOCKS, 6), turned.reshape(BLOCKS, 6))


def draw_neighbour(key, part):
    shared = paired_faces(key)
    return shared[0]


def draw_orient(key, part):
    shared = paired_faces(key)
    return shared[1]


def draw_basis(key, part):
    key = jax.random.fold_in(key, 5)
    inst_ramp = jnp.arange(INST, dtype=jnp.float32) / max(INST - 1, 1)
    cell_ramp = jnp.arange(CELLS, dtype=jnp.float32) / (CELLS - 1)
    ramp = 0.6 + 0.6 * inst_ramp[:, None, None] + 0.6 * cell_ramp[None, None, :]
    first_key = jax.random.fold_in(key, 21)
    second_key = jax.random.fold_in(key, 22)
    common = jnp.clip(jax.random.normal(first_key, (INST, VARS, CELLS), jnp.float32), -5.0, 5.0)
    own = jnp.clip(jax.random.normal(second_key, (KRYLOV, INST, VARS, CELLS), jnp.float32), -5.0, 5.0)
    mixed = 0.6 * common[None] + 0.8 * own
    return (ramp[None] * mixed).astype(jnp.float32)


def block_scale(key, dims, cuts, low, top_value):
    def one(dim, blocks):
        heights = jax.random.uniform(jax.random.fold_in(jax.random.fold_in(key, 6), dim), (blocks,), jnp.float32, low / len(cuts), top_value / len(cuts))
        return jnp.repeat(jnp.exp(heights), dims[dim] // blocks).reshape((-1,) + (1,) * (len(dims) - dim - 1))

    factor_of = one(*cuts[0])
    for cut in cuts[1:]:
        factor_of = factor_of * one(*cut)
    return factor_of


def centred(stream_key, dims, width, limit, cuts=(), kind=jnp.bfloat16):
    gain = block_scale(stream_key, dims, cuts, -0.22, 0.18) if cuts else 1.0
    values = jax.random.normal(stream_key, dims, jnp.float32) * width * gain
    return jnp.minimum(jnp.maximum(values, -limit), limit).astype(kind)


def setup_inputs(seed: int = 0) -> dict:
    splits = jax.random.split(jax.random.key(seed), 9)
    return {
        "basis": draw_basis(jax.random.fold_in(splits[8], 71), 0),
        "flux_adjoint": centred(splits[1], (INST, 7, VARS, VARS, CELLS), 49 ** -0.5, 0.875, ((0, 8), (4, 16))),
        "recon_adjoint": centred(splits[2], (INST, 7, VARS, VARS, CELLS), 49 ** -0.5, 0.875, ((0, 8), (4, 16))),
        "pseudo_time": jnp.clip(jnp.exp(math.log(2.0) - 1.3862944 * jax.random.uniform(splits[3], (CELLS,), jnp.float32) ** block_scale(splits[3], (CELLS,), ((0, 16),), -0.2, 0.2)), 0.5, 2.0),
        "vol_omega": jnp.clip(jnp.exp(math.log(1.0) - 1.3862944 * jax.random.uniform(splits[4], (CELLS,), jnp.float32) ** block_scale(splits[4], (CELLS,), ((0, 16),), -0.2, 0.2)), 0.25, 1.0),
        "block_ids": jax.random.permutation(splits[5], BLOCKS).astype(jnp.int32),
        "neighbour": draw_neighbour(jax.random.fold_in(splits[8], 71), 0),
        "orient": draw_orient(jax.random.fold_in(splits[8], 71), 0),
    }


def spectral_weight(offsets, count):
    angle = jnp.pi * offsets.astype(jnp.float32) / count
    parity = (offsets % 2).astype(jnp.float32)
    on_diagonal = offsets % count == 0
    sine = jnp.where(on_diagonal, 1.0, jnp.sin(angle))
    signed = 1.0 - 2.0 * parity
    first = 0.5 * signed * jnp.cos(angle) / sine
    second = -0.5 * signed / (sine * sine)
    centre = -0.25 * (count * count + 2) / 12.0
    return jnp.where(on_diagonal, centre, first + 0.25 * second)

def table_lookup(table, index):
    numbers = jnp.arange(table.shape[0], dtype=jnp.int32)
    matches = index[:, None] == numbers[None, :]
    return lax.optimization_barrier(jnp.sum(jnp.where(matches, table[None, :], 0), axis=1)).astype(jnp.int32)

def row_lookup(table, index):
    numbers = jnp.arange(table.shape[0], dtype=jnp.int32)
    matches = index[:, None, None] == numbers[None, :, None]
    return lax.optimization_barrier(jnp.sum(jnp.where(matches, table[None, :, :], 0), axis=1)).astype(jnp.int32)

def face_sources(block_ids, neighbour, orient, slots):
    numbers = jnp.arange(block_ids.shape[0], dtype=jnp.int32)
    position = lax.optimization_barrier(jnp.sum(jnp.where(block_ids[None, :] == numbers[:, None], numbers[None, :], 0), axis=1)).astype(jnp.int32)
    owners = table_lookup(block_ids, slots)
    partner = row_lookup(neighbour, owners).reshape(-1)
    codes = row_lookup(orient, owners).reshape(-1)
    is_wall = partner < 0
    target = jnp.maximum(partner, 0)
    source_row = table_lookup(position, target // 6) * 6 + target % 6
    return (source_row, is_wall, codes)

def block_faces(blocks, edge):
    variables, count = (blocks.shape[0], blocks.shape[1])
    square = edge * edge
    parts = [blocks[:, :, 0, :], blocks[:, :, edge - 1, :], blocks[..., :edge].reshape(variables, count, square), blocks[..., square - edge:].reshape(variables, count, square), blocks[..., 0::edge].reshape(variables, count, square), blocks[..., edge - 1::edge].reshape(variables, count, square)]
    stacked = jnp.stack(parts, axis=2)
    return jnp.moveaxis(stacked, 0, 2).reshape(count * 6, variables, square)

def turn_faces(faces, codes, edge):
    grid = faces.reshape(faces.shape[0], faces.shape[1], edge, edge)
    grid = jnp.where((codes & 1 == 1)[:, None, None, None], jnp.swapaxes(grid, 2, 3), grid)
    grid = jnp.where((codes & 2 == 2)[:, None, None, None], jnp.flip(grid, 2), grid)
    grid = jnp.where((codes & 4 == 4)[:, None, None, None], jnp.flip(grid, 3), grid)
    return grid.reshape(faces.shape)

def section_halos(all_faces, source_row, is_wall, codes, edge, count, variables):
    picked = jnp.take(all_faces, source_row, axis=0)
    turned = turn_faces(picked, codes, edge)
    turned = jnp.where(is_wall[:, None, None], 0.0, turned)
    grouped = turned.reshape(count, 6, variables, edge * edge)
    return [jnp.moveaxis(grouped[:, facing], 1, 0) for facing in range(6)]

def neighbour_fields(blocks, halos, edge):
    variables, count = (blocks.shape[0], blocks.shape[1])
    grid_shape = (variables, count, edge, edge)
    lower_x = jnp.concatenate([halos[0][:, :, None, :], blocks[:, :, :-1, :]], axis=2)
    upper_x = jnp.concatenate([blocks[:, :, 1:, :], halos[1][:, :, None, :]], axis=2)
    lower_y = jnp.concatenate([halos[2].reshape(grid_shape), blocks[..., :-edge]], axis=3)
    upper_y = jnp.concatenate([blocks[..., edge:], halos[3].reshape(grid_shape)], axis=3)
    column = jnp.arange(edge * edge, dtype=jnp.int32) % edge
    lower_z = jnp.where(column == 0, jnp.repeat(halos[4].reshape(grid_shape), edge, axis=3), jnp.roll(blocks, 1, axis=3))
    upper_z = jnp.where(column == edge - 1, jnp.repeat(halos[5].reshape(grid_shape), edge, axis=3), jnp.roll(blocks, -1, axis=3))
    return [blocks, lower_x, upper_x, lower_y, upper_y, lower_z, upper_z]

def apply_section(coeffs, blocks, halos, edge):
    result = jnp.zeros(blocks.shape, jnp.float32)
    for stencil_pos, values in enumerate(neighbour_fields(blocks, halos, edge)):
        result = result + lax.optimization_barrier(jnp.sum(coeffs[stencil_pos].astype(jnp.float32) * values[None], axis=1))
    return result

def reference(basis, flux_adjoint, recon_adjoint, pseudo_time, vol_omega, block_ids, neighbour, orient):
    edge = BLOCK_EDGE
    count = BLOCKS
    square = edge * edge
    slots = jnp.arange(count, dtype=jnp.int32)
    source_row, is_wall, codes = face_sources(block_ids, neighbour, orient, slots)
    vector = basis[KRYLOV - 1]
    numbers = jnp.arange(INST, dtype=jnp.int32)
    mixing = spectral_weight(numbers[:, None] - numbers[None, :], INST)
    spectral = jnp.einsum('mn,mvc->nvc', mixing, vector, precision=lax.Precision.HIGHEST)
    results = []
    for instance in range(INST):
        blocks = vector[instance].reshape(VARS, count, edge, square)
        halos = section_halos(block_faces(blocks, edge), source_row, is_wall, codes, edge, count, VARS)
        first = apply_section(flux_adjoint[instance].reshape(7, VARS, VARS, count, edge, square), blocks, halos, edge)
        halos = section_halos(block_faces(first, edge), source_row, is_wall, codes, edge, count, VARS)
        second = apply_section(recon_adjoint[instance].reshape(7, VARS, VARS, count, edge, square), first, halos, edge)
        results.append(second.reshape(VARS, CELLS))
    stencil = jnp.stack(results)
    image = pseudo_time * vector + stencil + vol_omega * spectral
    entries = float(INST * VARS * CELLS)
    flat_basis = basis.reshape(KRYLOV, -1)
    coeffs = jnp.dot(flat_basis, image.reshape(-1), precision=lax.Precision.HIGHEST) / entries
    ortho = image - jnp.einsum('k,knvc->nvc', coeffs, basis, precision=lax.Precision.HIGHEST)
    norm = jnp.sqrt(jnp.sum(ortho * ortho) / entries + 1e-06)
    return (ortho / norm, jnp.concatenate([coeffs, norm[None]]))
```

```python
import functools
import math

import jax
import jax.numpy as jnp
import numpy as np
from jax import lax
from jax.experimental import pallas as pl
from jax.experimental.pallas import tpu as pltpu
from jax.sharding import Mesh, PartitionSpec as P

EDGE = 16
SQUARE = EDGE * EDGE
CUBE = EDGE * SQUARE
VARS = 7
KRYLOV = 8
INST = 8
BLOCKS = 32
SPACE = 16
CELLS = 8192
PER = CELLS // CUBE
FACES = 6 * PER
SLABS = CELLS // SQUARE
ENTRIES = float(INST * VARS * CELLS * SPACE)
ALL = ("z", "xl", "xh", "y", "core")
CHIPS = ("xh", "y")
HALF = 128
VMEM = pltpu.VMEM
SMEM = pltpu.SMEM
GUARD = 0.02


def mixing_weights():
    k = np.arange(INST)
    parity = np.where(k % 2 == 0, 1.0, -1.0)
    weight = np.empty(INST)
    weight[0] = -0.25 * (INST * INST + 2) / 12.0
    angle = np.pi * k[1:] / INST
    weight[1:] = 0.5 * parity[1:] / np.tan(angle) - 0.125 * parity[1:] / np.sin(angle) ** 2
    return weight.astype(np.float32)


def lanes(shape):
    return lax.broadcasted_iota(jnp.int32, shape, len(shape) - 1)


def pick(values, index):
    return jnp.take_along_axis(values, index, axis=1)


def collect_faces(slab, block, x, faces):
    lane = lanes((8, HALF))
    low, high = (slab[:, :HALF], slab[:, HALF:])
    within = lane % 8
    own = lane // EDGE == x % 8
    upper_half = lane % EDGE >= 8
    strips = (
        pick(low, lane % EDGE),
        pick(high, lane % EDGE + (HALF - EDGE)),
        jnp.where(upper_half, pick(high, within * EDGE), pick(low, within * EDGE)),
        jnp.where(upper_half, pick(high, within * EDGE + 15), pick(low, within * EDGE + 15)),
    )
    start = pl.multiple_of((x // 8) * HALF, HALF)
    for number, strip in enumerate(strips):
        spot = (block * 6 + 2 + number, slice(None), pl.ds(start, HALF))
        faces[spot] = jnp.where(own, strip, faces[spot])

    @pl.when(x == 0)
    def _():
        faces[block * 6] = slab

    @pl.when(x == EDGE - 1)
    def _():
        faces[block * 6 + 1] = slab


def copy_out(faces, sent_ref):
    for number in range(FACES):
        face = faces[number]
        for chip in range(sent_ref.shape[0]):
            sent_ref[chip, number] = face


def first_faces_kernel(which_ref, vector_ref, sent_ref, mine_ref, other_ref, faces):
    faces[...] = jnp.zeros_like(faces)

    def step(k, carry):
        start = pl.multiple_of(k * SQUARE, SQUARE)
        slab = vector_ref[0, 0, :, pl.ds(start, SQUARE)]
        slab = jnp.concatenate([slab, jnp.zeros((1, SQUARE), jnp.float32)], axis=0)
        collect_faces(slab, k // EDGE, k % EDGE, faces)
        return carry

    lax.fori_loop(0, SLABS, step, 0)
    copy_out(faces, sent_ref)
    mine = pl.multiple_of(which_ref[0] * CUBE, CUBE)
    other = pl.multiple_of((1 - which_ref[0]) * CUBE, CUBE)
    mine_ref[...] = vector_ref[0, 0, :, pl.ds(mine, CUBE)]
    other_ref[...] = vector_ref[0, 0, :, pl.ds(other, CUBE)]


def fetch_halos(tables_ref, own_ref, swapped_ref, position, halos):
    rank = tables_ref[BLOCKS * 13]

    def place(slot, carry):
        position[tables_ref[slot]] = slot
        return carry

    lax.fori_loop(0, BLOCKS, place, 0)
    lane = lanes((8, HALF))

    def face(number, carry):
        owner = tables_ref[rank * PER + number // 6]
        entry = owner * 6 + number % 6
        partner = tables_ref[BLOCKS + entry]
        code = tables_ref[BLOCKS * 7 + entry]
        target = jnp.maximum(partner, 0)
        slot = position[target // 6]
        device = slot // PER
        row = (slot % PER) * 6 + target % 6
        own = own_ref[device // 2, row]
        swapped = swapped_ref[device // 2, row]
        source = jnp.where(device % 2 == rank % 2, own, swapped)
        source = jnp.where(partner < 0, 0.0, source)
        low, high = (source[:, :HALF], source[:, HALF:])
        transposed = code % 2 == 1
        flip_a = (code // 2) % 2 * (EDGE - 1)
        flip_b = (code // 4) * (EDGE - 1)
        for half in range(2):
            a = lane // EDGE + half * 8
            b = lane % EDGE
            a = jnp.abs(a - flip_a)
            b = jnp.abs(b - flip_b)
            index = jnp.where(transposed, b * EDGE + a, a * EDGE + b)
            inside = index % HALF
            halos[number, :, half * HALF : (half + 1) * HALF] = jnp.where(
                index < HALF, pick(low, inside), pick(high, inside)
            )
        return carry

    lax.fori_loop(0, FACES, face, 0)


def slab_neighbours(load, halos, k):
    block, x = (k // EDGE, k % EDGE)
    centre = load(k)
    below = jnp.where(x == 0, halos[block * 6, :VARS], load(jnp.maximum(k - 1, 0)))
    above = jnp.where(x == EDGE - 1, halos[block * 6 + 1, :VARS], load(jnp.minimum(k + 1, SLABS - 1)))
    lane = lanes((8, HALF))
    start = pl.multiple_of((x // 8) * HALF, HALF)
    offset = (x % 8) * EDGE

    def strip(face):
        return halos[block * 6 + face, :, pl.ds(start, HALF)]

    def spread_y(face):
        piece = pick(strip(face), lane % EDGE + offset)
        return jnp.concatenate([piece, piece], axis=1)[:VARS]

    def spread_z(face):
        source = strip(face)
        return jnp.concatenate(
            [pick(source, lane // EDGE + offset), pick(source, lane // EDGE + (offset + 8))], axis=1
        )[:VARS]

    column = lanes((VARS, SQUARE))
    z = column % EDGE
    y_low = jnp.where(column < EDGE, spread_y(2), pltpu.roll(centre, EDGE, 1))
    y_high = jnp.where(column >= SQUARE - EDGE, spread_y(3), pltpu.roll(centre, SQUARE - EDGE, 1))
    z_low = jnp.where(z == 0, spread_z(4), pltpu.roll(centre, 1, 1))
    z_high = jnp.where(z == EDGE - 1, spread_z(5), pltpu.roll(centre, SQUARE - 1, 1))
    return [centre, below, above, y_low, y_high, z_low, z_high]


def section_slab(coeff_ref, operands, start):
    totals = [None] * VARS
    for s, operand in enumerate(operands):
        for o in range(VARS):
            term = coeff_ref[0, s, o, :, pl.ds(start, SQUARE)].astype(jnp.float32) * operand
            totals[o] = term if totals[o] is None else totals[o] + term
    empty = jnp.zeros((1, SQUARE), jnp.float32)
    padded = [jnp.concatenate([total, empty], axis=0) for total in totals]
    padded.append(jnp.zeros((8, SQUARE), jnp.float32))
    row = lax.broadcasted_iota(jnp.int32, (8, SQUARE), 0)

    quarter = [fold4(padded[i], padded[i + 4], row) for i in range(4)]
    pair = [fold2(quarter[i], quarter[i + 2], row) for i in range(2)]
    return fold1(pair[0], pair[1], row)


def fold4(a, b, row):
    first = row < 4
    return jnp.where(first, a, b) + pltpu.roll(jnp.where(first, b, a), 4, 0)


def fold2(a, b, row):
    first = row % 4 < 2
    other = jnp.where(first, b, a)
    moved = jnp.where(first, pltpu.roll(other, 6, 0), pltpu.roll(other, 2, 0))
    return jnp.where(first, a, b) + moved


def fold1(a, b, row):
    first = row % 2 == 0
    other = jnp.where(first, b, a)
    moved = jnp.where(first, pltpu.roll(other, 7, 0), pltpu.roll(other, 1, 0))
    return jnp.where(first, a, b) + moved


def flux_kernel(tables_ref, own_ref, swapped_ref, vector_ref, coeff_ref, first_ref, sent_ref, halos, faces, position):
    fetch_halos(tables_ref, own_ref, swapped_ref, position, halos)
    faces[...] = jnp.zeros_like(faces)

    def load(k):
        return vector_ref[0, 0, :, pl.ds(pl.multiple_of(k * SQUARE, SQUARE), SQUARE)]

    def step(k, carry):
        start = pl.multiple_of(k * SQUARE, SQUARE)
        slab = section_slab(coeff_ref, slab_neighbours(load, halos, k), start)
        first_ref[:, pl.ds(start, SQUARE)] = slab[:VARS]
        collect_faces(slab, k // EDGE, k % EDGE, faces)
        return carry

    lax.fori_loop(0, SLABS, step, 0)
    copy_out(faces, sent_ref)


def gram_kernel(basis_ref, gram_ref):
    rows = []

    def step(k, totals):
        start = pl.multiple_of(k * SQUARE, SQUARE)
        fields = [basis_ref[j, 0, :, pl.ds(start, SQUARE)] for j in range(KRYLOV)]
        out = []
        number = 0
        for i in range(KRYLOV):
            for j in range(i, KRYLOV):
                term = fields[i] * fields[j]
                out.append(totals[number] + term[:, :HALF] + term[:, HALF:])
                number += 1
        return tuple(out)

    zero = jnp.zeros((VARS, HALF), jnp.float32)
    totals = lax.fori_loop(0, SLABS, step, (zero,) * (KRYLOV * (KRYLOV + 1) // 2))
    number = 0
    for i in range(KRYLOV):
        for j in range(i, KRYLOV):
            line = jnp.sum(totals[number], axis=0, keepdims=True)
            gram_ref[i * KRYLOV + j : i * KRYLOV + j + 1] = line
            if i != j:
                gram_ref[j * KRYLOV + i : j * KRYLOV + i + 1] = line
            number += 1


def image_kernel(
    tables_ref, own_ref, swapped_ref, first_ref, coeff_ref, basis_ref, pseudo_ref, omega_ref,
    mixed_ref, returned_ref, gram_ref, image_ref, sums_ref, halos, position, lines
):
    fetch_halos(tables_ref, own_ref, swapped_ref, position, halos)
    which = tables_ref[BLOCKS * 13 + 1]

    def load(k):
        return first_ref[:, pl.ds(pl.multiple_of(k * SQUARE, SQUARE), SQUARE)]

    def step(k, totals):
        start = pl.multiple_of(k * SQUARE, SQUARE)
        inner = pl.multiple_of((k % EDGE) * SQUARE, SQUARE)
        slab = section_slab(coeff_ref, slab_neighbours(load, halos, k), start)[:VARS]
        spectral = jnp.where(
            k // EDGE == which, mixed_ref[:, pl.ds(inner, SQUARE)], returned_ref[:, pl.ds(inner, SQUARE)]
        )
        vector = basis_ref[KRYLOV - 1, 0, :, pl.ds(start, SQUARE)]
        image = pseudo_ref[:, pl.ds(start, SQUARE)] * vector + slab + omega_ref[:, pl.ds(start, SQUARE)] * spectral
        image_ref[:, pl.ds(start, SQUARE)] = image
        out = []
        for j in range(KRYLOV + 1):
            field = image if j == KRYLOV else basis_ref[j, 0, :, pl.ds(start, SQUARE)]
            term = field * image
            out.append(totals[j] + term[:, :HALF] + term[:, HALF:])
        return tuple(out)

    zero = jnp.zeros((VARS, HALF), jnp.float32)
    totals = lax.fori_loop(0, SLABS, step, (zero,) * (KRYLOV + 1))
    lines[...] = jnp.zeros_like(lines)
    for j in range(KRYLOV + 1):
        lines[j : j + 1] = jnp.sum(totals[j], axis=0, keepdims=True)
    lines[64:] = gram_ref[...]
    ones = jnp.ones((8, HALF), jnp.float32)
    sums = lax.dot_general(
        ones, lines[...], (((1,), (1,)), ((), ())),
        precision=lax.Precision.HIGHEST, preferred_element_type=jnp.float32,
    )
    for group in range(16):
        sums_ref[group * 8 : group * 8 + 8] = sums


def finish_kernel(received_ref, image_ref, basis_ref, next_ref, column_ref):
    sums = jnp.sum(received_ref[...], axis=0, keepdims=True)
    sums = jnp.broadcast_to(sums, (8, HALF)) / ENTRIES
    lane = lanes((8, HALF))
    left = pick(sums, jnp.maximum(lane - 64, 0) // 8)
    right = pick(sums, lane % 8)
    quadratic = jnp.sum(jnp.where(lane >= 64, sums * left * right, 0.0), axis=1, keepdims=True)
    linear = jnp.sum(jnp.where(lane < KRYLOV, sums * sums, 0.0), axis=1, keepdims=True)
    whole = sums[:, KRYLOV : KRYLOV + 1]
    squares = whole - 2.0 * linear + quadratic
    size = whole + 2.0 * linear + jnp.abs(quadratic)
    norm = jnp.sqrt(jnp.maximum(squares, 0.0) + 1e-06)
    inverse = 1.0 / norm
    column = jnp.where(lane < KRYLOV, sums, jnp.where(lane == KRYLOV, norm, 0.0))
    column_ref[...] = jnp.where(lane == KRYLOV + 1, jnp.where(squares < GUARD * size, 1.0, 0.0), column)
    coeffs = [jnp.broadcast_to(sums[:VARS, j : j + 1], (VARS, SQUARE)) for j in range(KRYLOV)]
    scale = jnp.broadcast_to(inverse[:VARS], (VARS, SQUARE))

    def step(k, carry):
        start = pl.multiple_of(k * SQUARE, SQUARE)
        ortho = image_ref[:, pl.ds(start, SQUARE)]
        for j in range(KRYLOV):
            ortho = ortho - coeffs[j] * basis_ref[j, 0, :, pl.ds(start, SQUARE)]
        next_ref[0, :, pl.ds(start, SQUARE)] = ortho * scale
        return carry

    lax.fori_loop(0, SLABS, step, 0)


def whole(memory=VMEM):
    return pl.BlockSpec(memory_space=memory)


def last_vector():
    return pl.BlockSpec((1, 1, VARS, CELLS), lambda i: (KRYLOV - 1, 0, 0, 0))


def whole_in_grid(shape):
    return pl.BlockSpec(shape, lambda i: (0,) * len(shape))


def f32(*shape):
    return jax.ShapeDtypeStruct(shape, jnp.float32)


PARAMS = pltpu.CompilerParams(vmem_limit_bytes=24 * 2**20)


def swap(size, bit):
    return [(i, i ^ bit) for i in range(size)]


def exchange(sent):
    own = lax.all_to_all(sent, CHIPS, 0, 0)
    return own, lax.ppermute(own, "core", swap(2, 1))


def mix(mine, other, z):
    received = lax.ppermute(other, "xl", swap(2, 1))
    xl = lax.axis_index("xl")
    even = jnp.where(xl == 0, mine, received)
    odd = jnp.where(xl == 0, received, mine)
    pair = jnp.stack([even, odd])
    parts = [pair] + [lax.ppermute(pair, "z", swap(4, k)) for k in (1, 2, 3)]
    weights = jnp.asarray(mixing_weights())
    results = []
    for target in (xl, 1 - xl):
        total = 0.0
        for k, part in enumerate(parts):
            source = (z ^ k) * 2
            for offset in range(2):
                weight = weights[(source + offset - (2 * z + target)) % INST]
                total = total + weight * part[offset]
        results.append(total)
    return results[0], lax.ppermute(results[1], "xl", swap(2, 1))


def local(basis, flux, recon, pseudo_time, vol_omega, block_ids, neighbour, orient):
    z = lax.axis_index("z")
    xl = lax.axis_index("xl").astype(jnp.int32)
    rank = lax.axis_index(("xh", "y", "core")).astype(jnp.int32)
    tables = jnp.concatenate(
        [block_ids, neighbour.reshape(-1), orient.reshape(-1), rank[None], xl[None]]
    )
    sent, mine, other = pl.pallas_call(
        first_faces_kernel,
        grid=(1,),
        in_specs=[whole(SMEM), last_vector()],
        out_specs=[whole_in_grid((8, FACES, 8, SQUARE)), whole_in_grid((VARS, CUBE)), whole_in_grid((VARS, CUBE))],
        out_shape=[f32(8, FACES, 8, SQUARE), f32(VARS, CUBE), f32(VARS, CUBE)],
        scratch_shapes=[VMEM((FACES, 8, SQUARE), jnp.float32)],
        compiler_params=PARAMS,
        name="first_faces",
    )(xl[None], basis)
    own, swapped = exchange(sent)
    mixed, returned = mix(mine, other, z)
    gram = pl.pallas_call(
        gram_kernel,
        in_specs=[whole()],
        out_specs=whole(),
        out_shape=f32(KRYLOV * KRYLOV, HALF),
        compiler_params=PARAMS,
        cost_estimate=pl.CostEstimate(flops=2 * 36 * 7 * 8192, bytes_accessed=2 * 2**20, transcendentals=0),
        name="gram",
    )(basis)
    first, sent = pl.pallas_call(
        flux_kernel,
        grid=(1,),
        in_specs=[
            whole(SMEM), whole(), whole(), last_vector(), whole(),
        ],
        out_specs=[whole_in_grid((VARS, CELLS)), whole_in_grid((8, FACES, 8, SQUARE))],
        out_shape=[f32(VARS, CELLS), f32(8, FACES, 8, SQUARE)],
        scratch_shapes=[
            VMEM((FACES, 8, SQUARE), jnp.float32),
            VMEM((FACES, 8, SQUARE), jnp.float32),
            SMEM((BLOCKS,), jnp.int32),
        ],
        compiler_params=PARAMS,
        name="flux_section",
    )(tables, own, swapped, basis, flux)
    own, swapped = exchange(sent)
    image, sums = pl.pallas_call(
        image_kernel,
        in_specs=[whole(SMEM)] + [whole()] * 10,
        out_specs=[whole(), whole()],
        out_shape=[f32(VARS, CELLS), f32(HALF, HALF)],
        scratch_shapes=[
            VMEM((FACES, 8, SQUARE), jnp.float32),
            SMEM((BLOCKS,), jnp.int32),
            VMEM((HALF, HALF), jnp.float32),
        ],
        compiler_params=PARAMS,
        name="image",
    )(
        tables, own, swapped, first, recon, basis, pseudo_time[None], vol_omega[None],
        mixed, returned, gram,
    )
    received = lax.all_to_all(sums, ALL, 0, 0)
    following, column = pl.pallas_call(
        finish_kernel,
        in_specs=[whole()] * 3,
        out_specs=[whole(), whole()],
        out_shape=[f32(1, VARS, CELLS), f32(8, HALF)],
        compiler_params=PARAMS,
        name="finish",
    )(received, image, basis)
    coeffs = column[0, :KRYLOV]
    hessenberg = column[0, : KRYLOV + 1]

    def direct(state):
        ortho = image - jnp.einsum("k,kvc->vc", coeffs, basis[:, 0], precision=lax.Precision.HIGHEST)
        squares = lax.psum(jnp.sum(ortho * ortho), ALL) / ENTRIES
        norm = jnp.sqrt(squares + 1e-06)
        return ((ortho / norm)[None], jnp.concatenate([coeffs, norm[None]]), 0.0 * norm)

    following, hessenberg, _ = lax.while_loop(
        lambda state: state[2] > 0.5, direct, (following, hessenberg, column[0, KRYLOV + 1])
    )
    return following, hessenberg


def solution(mesh):
    fine = Mesh(mesh.devices.reshape(4, 2, 2, 4, 2), ALL)
    inst, space = (("z", "xl"), ("xh", "y", "core"))
    placed = (
        P(None, inst, None, space),
        P(inst, None, None, None, space),
        P(inst, None, None, None, space),
        P(space),
        P(space),
        P(),
        P(),
        P(),
    )
    return jax.shard_map(
        local,
        mesh=fine,
        in_specs=placed,
        out_specs=(P(inst, None, space), P()),
        check_vma=False,
    )
```

```python
import jax
import jax.numpy as jnp
import numpy as np
from jax import lax
from jax.experimental import pallas as pl
from jax.experimental.pallas import tpu as pltpu
from jax.sharding import Mesh, PartitionSpec as P

EDGE = 16
SQUARE = EDGE * EDGE
CUBE = EDGE * SQUARE
VARS = 7
KRYLOV = 8
INST = 8
BLOCKS = 32
SPACE = 16
CHIP_COUNT = 8
CELLS = 8192
PER = CELLS // CUBE
FACES = 6 * PER
SLABS = CELLS // SQUARE
ENTRIES = float(INST * VARS * CELLS * SPACE)
LANES = 128
GROUPS = CELLS // LANES
ROWS = VARS * GROUPS
ALL = ("z", "xl", "xh", "y", "core")
CHIPS = ("xh", "y")
VMEM = pltpu.VMEM
SMEM = pltpu.SMEM
GUARD = 0.02
CHUNK = 4


def mixing_weights():
    k = np.arange(1, INST)
    parity = np.where(k % 2 == 0, 1.0, -1.0)
    angle = np.pi * k / INST
    rest = 0.5 * parity / np.tan(angle) - 0.125 * parity / np.sin(angle) ** 2
    return [-0.25 * (INST * INST + 2) / 12.0] + [float(v) for v in rest]


def lanes(shape):
    return lax.broadcasted_iota(jnp.int32, shape, len(shape) - 1)


def sublanes(shape):
    return lax.broadcasted_iota(jnp.int32, shape, len(shape) - 2)


def pick(values, index):
    return jnp.take_along_axis(values, index, axis=1)


def fold(totals):
    row = sublanes(totals[0].shape)
    for width in (1, 2, 4):
        first = row % (2 * width) < width
        totals = [
            jnp.where(first, a, b) + pltpu.roll(jnp.where(first, b, a), width, 0)
            for a, b in zip(totals[::2], totals[1::2])
        ]
    return totals[0]


def strips_of(slab, x, strips):
    lane = lanes((8, LANES))
    low, high = (slab[:, :LANES], slab[:, LANES:])
    own = lane // EDGE == x
    upper = lane % EDGE >= 8
    source = lane % 8 * EDGE
    found = (
        pick(low, lane % EDGE),
        pick(high, lane % EDGE + (LANES - EDGE)),
        jnp.where(upper, pick(high, source), pick(low, source)),
        jnp.where(upper, pick(high, source + 15), pick(low, source + 15)),
    )
    if strips is None:
        return list(found)
    return [jnp.where(own, new, old) for new, old in zip(found, strips)]


def store_strips(faces, block, half, strips):
    for number, strip in enumerate(strips):
        faces[block * 6 + 2 + number, :, half * LANES : (half + 1) * LANES] = strip


def send_faces(faces, sent_ref, arrived):
    copies = [
        pltpu.make_async_copy(faces, sent_ref.at[chip], arrived.at[chip]) for chip in range(CHIP_COUNT)
    ]
    for copy in copies:
        copy.start()
    for copy in copies:
        copy.wait()


def first_faces_kernel(basis_ref, sent_ref, padded_ref, dense_ref, field, faces, arrived):
    fetch = pltpu.make_async_copy(
        basis_ref.at[pl.ds((KRYLOV - 1) * ROWS, ROWS)], field.at[pl.ds(0, ROWS)], arrived.at[0]
    )
    fetch.start()
    field[ROWS:] = jnp.zeros((GROUPS, LANES), jnp.float32)
    fetch.wait()
    dense_ref[...] = field[:ROWS]
    for block in range(PER):
        for half in range(2):
            strips = None
            for inner in range(8):
                k = block * EDGE + half * 8 + inner
                slab = jnp.concatenate(
                    [field[pl.ds(2 * k, 8, stride=GROUPS), :], field[pl.ds(2 * k + 1, 8, stride=GROUPS), :]],
                    axis=1,
                )
                padded_ref[:, k * SQUARE : (k + 1) * SQUARE] = slab
                strips = strips_of(slab, inner, strips)
                if half == 0 and inner == 0:
                    faces[block * 6] = slab
                if half == 1 and inner == 7:
                    faces[block * 6 + 1] = slab
            store_strips(faces, block, half, strips)
    send_faces(faces, sent_ref, arrived)


def tables_kernel(ids_ref, neighbour_ref, orient_ref, table_ref, position):
    core = lax.axis_index("core")
    rank = (lax.axis_index("xh") * 4 + lax.axis_index("y")) * 2 + core

    def place(slot, carry):
        position[ids_ref[slot]] = slot
        return carry

    lax.fori_loop(0, BLOCKS, place, 0)
    for number in range(FACES):
        owner = ids_ref[rank * PER + number // 6]
        partner = neighbour_ref[number % 6, owner]
        code = orient_ref[number % 6, owner]
        target = jnp.maximum(partner, 0)
        slot = position[target // 6]
        device = slot // PER
        table_ref[number * 4] = device // 2
        table_ref[number * 4 + 1] = jnp.where(device % 2 == core, 1, 0)
        table_ref[number * 4 + 2] = (slot % PER) * 6 + target % 6
        table_ref[number * 4 + 3] = jnp.where(partner < 0, -1, code)


def fetch_halos(table_ref, own_ref, swapped_ref, halos):
    lane = lanes((8, LANES))
    for number in range(FACES):
        chip = table_ref[number * 4]
        here = table_ref[number * 4 + 1] == 1
        row = table_ref[number * 4 + 2]
        code = table_ref[number * 4 + 3]
        wall = code < 0
        code = jnp.maximum(code, 0)
        source = jnp.where(here, own_ref[chip, row], swapped_ref[chip, row])
        source = jnp.where(wall, 0.0, source)
        low, high = (source[:, :LANES], source[:, LANES:])
        transposed = code % 2 == 1
        flip_a = code // 2 % 2 * (EDGE - 1)
        flip_b = code // 4 * (EDGE - 1)
        for half in range(2):
            a = (lane // EDGE + half * 8) ^ flip_a
            b = (lane % EDGE) ^ flip_b
            index = jnp.where(transposed, b * EDGE + a, a * EDGE + b)
            inside = index % LANES
            halos[number, :, half * LANES : (half + 1) * LANES] = jnp.where(
                index < LANES, pick(low, inside), pick(high, inside)
            )


def inner_kernel(field_ref, coeff_ref, part_ref, across_z_ref, across_y_ref, across_x_ref):
    column = lanes((8, SQUARE))
    z = column % EDGE
    below_zero = jnp.zeros((1, SQUARE), jnp.float32)

    def coeff(s, o, inner):
        value = coeff_ref[0, s, o, :, inner * SQUARE : (inner + 1) * SQUARE].astype(jnp.float32)
        return jnp.concatenate([value, below_zero], axis=0)

    def load(k):
        return field_ref[:, pl.ds(pl.multiple_of(k * SQUARE, SQUARE), SQUARE)]

    for inner in range(CHUNK):
        k = pl.program_id(0) * CHUNK + inner
        block, x = (k // EDGE, k % EDGE)
        place = slice(inner * SQUARE, (inner + 1) * SQUARE)
        centre = load(k)
        operands = [
            centre,
            jnp.where(x == 0, 0.0, load(jnp.maximum(k - 1, 0))),
            jnp.where(x == EDGE - 1, 0.0, load(jnp.minimum(k + 1, SLABS - 1))),
            jnp.where(column < EDGE, 0.0, pltpu.roll(centre, EDGE, 1)),
            jnp.where(column >= SQUARE - EDGE, 0.0, pltpu.roll(centre, SQUARE - EDGE, 1)),
            jnp.where(z == 0, 0.0, pltpu.roll(centre, 1, 1)),
            jnp.where(z == EDGE - 1, 0.0, pltpu.roll(centre, SQUARE - 1, 1)),
        ]
        totals = []
        for o in range(VARS):
            values = [coeff(s, o, inner) for s in range(7)]
            total = values[0] * operands[0]
            for s in range(1, 7):
                total = total + values[s] * operands[s]
            totals.append(total)
            across_z_ref[o, :, place] = jnp.where(
                z == 0, values[5], jnp.where(z == EDGE - 1, values[6], 0.0)
            )
            across_y_ref[o, :, place] = jnp.where(
                column < EDGE, values[3], jnp.where(column >= SQUARE - EDGE, values[4], 0.0)
            )
        part_ref[:, place] = fold(totals + [jnp.zeros((8, SQUARE), jnp.float32)])

        if inner == 0:

            @pl.when(x == 0)
            def _():
                for o in range(VARS):
                    across_x_ref[block * 2, o] = coeff(1, o, inner)

        if inner == CHUNK - 1:

            @pl.when(x == EDGE - 1)
            def _():
                for o in range(VARS):
                    across_x_ref[block * 2 + 1, o] = coeff(2, o, inner)


def outer_slab(part_ref, across_z_ref, across_y_ref, halos, block, half, inner):
    lane = lanes((8, LANES))
    offset = inner * EDGE
    place = pl.ds(pl.multiple_of(block * CUBE + (half * 8 + inner) * SQUARE, SQUARE), SQUARE)
    start = half * LANES

    def strip(face):
        return halos[block * 6 + face, :, start : start + LANES]

    y = lane % EDGE + offset
    z = lane // EDGE + offset
    at_low = lane % EDGE == 0
    across_y = jnp.concatenate([pick(strip(2), y), pick(strip(3), y)], axis=1)
    z_low, z_high = (strip(4), strip(5))
    across_z = jnp.concatenate(
        [
            jnp.where(at_low, pick(z_low, z), pick(z_high, z)),
            jnp.where(at_low, pick(z_low, z + 8), pick(z_high, z + 8)),
        ],
        axis=1,
    )
    totals = [
        across_z_ref[o, :, place] * across_z + across_y_ref[o, :, place] * across_y for o in range(VARS)
    ]
    return part_ref[:, place] + fold(totals + [jnp.zeros((8, SQUARE), jnp.float32)])


def outer_x(across_x_ref, halos, block, side):
    halo = halos[block * 6 + side]
    totals = [across_x_ref[block * 2 + side, o] * halo for o in range(VARS)]
    return fold(totals + [jnp.zeros((8, SQUARE), jnp.float32)])


def outer_blocks(across_x_ref, part_ref, across_z_ref, across_y_ref, halos, each):
    for block in range(PER):
        for half in range(2):
            for inner in range(8):
                slab = outer_slab(part_ref, across_z_ref, across_y_ref, halos, block, half, inner)
                if half == 0 and inner == 0:
                    slab = slab + outer_x(across_x_ref, halos, block, 0)
                if half == 1 and inner == 7:
                    slab = slab + outer_x(across_x_ref, halos, block, 1)
                each(block, half, inner, slab)


def flux_kernel(
    table_ref, own_ref, swapped_ref, part_ref, across_z_ref, across_y_ref, across_x_ref,
    first_ref, sent_ref, halos, faces, arrived
):
    fetch_halos(table_ref, own_ref, swapped_ref, halos)
    held = {}

    def each(block, half, inner, slab):
        k = block * EDGE + half * 8 + inner
        first_ref[:, k * SQUARE : (k + 1) * SQUARE] = slab
        held["strips"] = strips_of(slab, inner, held["strips"] if inner else None)
        if half == 0 and inner == 0:
            faces[block * 6] = slab
        if half == 1 and inner == 7:
            faces[block * 6 + 1] = slab
        if inner == 7:
            store_strips(faces, block, half, held["strips"])

    outer_blocks(across_x_ref, part_ref, across_z_ref, across_y_ref, halos, each)
    send_faces(faces, sent_ref, arrived)


def mix_kernel(own_ref, one_ref, two_ref, three_ref, kept_ref, given_ref):
    z = lax.axis_index("z")
    xl = lax.axis_index("xl")
    table = mixing_weights()

    def weight(offset):
        offset = lax.rem(offset + 2 * INST, INST)
        value = jnp.float32(table[0])
        for k in range(1, INST):
            value = jnp.where(offset == k, jnp.float32(table[k]), value)
        return value

    fields = (own_ref, one_ref, two_ref, three_ref)
    sources = [2 * (z ^ k) + xl for k in range(4)]
    kept = [weight(source - (2 * z + xl)) for source in sources]
    given = [weight(source - (2 * z + 1 - xl)) for source in sources]

    def step(k, carry):
        rows = pl.ds(pl.multiple_of(k * 64, 64), 64)
        values = [field[rows] for field in fields]
        kept_ref[rows] = sum(w * v for w, v in zip(kept, values))
        given_ref[rows] = sum(w * v for w, v in zip(given, values))
        return carry

    lax.fori_loop(0, ROWS // 64, step, 0)


def lane_sums(rows, first_lane):
    totals = jnp.broadcast_to(jnp.sum(rows, axis=1, keepdims=True), rows.shape)
    spot = lanes(rows.shape) == sublanes(rows.shape) + first_lane
    return jnp.sum(jnp.where(spot, totals, 0.0), axis=0, keepdims=True)


def gram_kernel(basis_ref, gram_ref, lines):
    def step(k, totals):
        fields = [
            basis_ref[pl.ds(pl.multiple_of(j * ROWS + k * 8, 8), 8)] for j in range(KRYLOV)
        ]
        out = []
        for i in range(KRYLOV):
            for j in range(i, KRYLOV):
                out.append(totals[len(out)] + fields[i] * fields[j])
        return tuple(out)

    zero = jnp.zeros((8, LANES), jnp.float32)
    totals = lax.fori_loop(0, ROWS // 8, step, (zero,) * (KRYLOV * (KRYLOV + 1) // 2))
    number = 0
    for i in range(KRYLOV):
        for j in range(i, KRYLOV):
            line = jnp.sum(totals[number], axis=0, keepdims=True)
            lines[i * KRYLOV + j : i * KRYLOV + j + 1] = line
            lines[j * KRYLOV + i : j * KRYLOV + i + 1] = line
            number += 1
    gram_ref[...] = jnp.broadcast_to(lane_sums(lines[...], 64), (8, LANES))


def image_kernel(
    table_ref, own_ref, swapped_ref, part_ref, across_z_ref, across_y_ref, across_x_ref,
    basis_ref, pseudo_ref, omega_ref, kept_ref, returned_ref, gram_ref,
    image_ref, sums_ref, halos, section
):
    fetch_halos(table_ref, own_ref, swapped_ref, halos)

    def each(block, half, inner, slab):
        k = block * EDGE + half * 8 + inner
        section[pl.ds(2 * k, 8, stride=GROUPS), :] = slab[:, :LANES]
        section[pl.ds(2 * k + 1, 8, stride=GROUPS), :] = slab[:, LANES:]

    outer_blocks(across_x_ref, part_ref, across_z_ref, across_y_ref, halos, each)

    def step(k, totals):
        start = k * 8
        cells = pl.ds(pl.multiple_of(start % GROUPS, 8), 8)
        rows = pl.ds(pl.multiple_of(start, 8), 8)
        fields = [basis_ref[pl.ds(pl.multiple_of(j * ROWS + start, 8), 8)] for j in range(KRYLOV)]
        spectral = kept_ref[rows] + returned_ref[rows]
        image = pseudo_ref[cells] * fields[KRYLOV - 1] + section[rows] + omega_ref[cells] * spectral
        image_ref[rows] = image
        return tuple(total + field * image for total, field in zip(totals, fields + [image]))

    zero = jnp.zeros((8, LANES), jnp.float32)
    totals = lax.fori_loop(0, ROWS // 8, step, (zero,) * (KRYLOV + 1), unroll=8)
    lines = [jnp.sum(total, axis=0, keepdims=True) for total in totals]
    lines += [jnp.zeros((16 - len(lines), LANES), jnp.float32)]
    sums = jnp.broadcast_to(lane_sums(jnp.concatenate(lines, axis=0), 0), (8, LANES)) + gram_ref[...]
    for group in range(16):
        sums_ref[group * 8 : group * 8 + 8] = sums


def finish_kernel(received_ref, image_ref, basis_ref, next_ref, column_ref):
    sums = jnp.sum(received_ref[...], axis=0, keepdims=True)
    sums = jnp.broadcast_to(sums, (8, LANES)) / ENTRIES
    lane = lanes((8, LANES))
    left = pick(sums, jnp.maximum(lane - 64, 0) // 8)
    right = pick(sums, lane % 8)
    quadratic = jnp.sum(jnp.where(lane >= 64, sums * left * right, 0.0), axis=1, keepdims=True)
    linear = jnp.sum(jnp.where(lane < KRYLOV, sums * sums, 0.0), axis=1, keepdims=True)
    whole_square = sums[:, KRYLOV : KRYLOV + 1]
    squares = whole_square - 2.0 * linear + quadratic
    size = whole_square + 2.0 * linear + jnp.abs(quadratic)
    norm = jnp.sqrt(jnp.maximum(squares, 0.0) + 1e-06)
    column = jnp.where(lane < KRYLOV, sums, jnp.where(lane == KRYLOV, norm, 0.0))
    column_ref[...] = jnp.where(lane == KRYLOV + 1, jnp.where(squares < GUARD * size, 1.0, 0.0), column)
    coeffs = [jnp.broadcast_to(sums[:, j : j + 1], (8, LANES)) for j in range(KRYLOV)]
    scale = jnp.broadcast_to(1.0 / norm, (8, LANES))

    def step(k, carry):
        start = k * 8
        rows = pl.ds(pl.multiple_of(start, 8), 8)
        ortho = image_ref[rows]
        for j in range(KRYLOV):
            ortho = ortho - coeffs[j] * basis_ref[pl.ds(pl.multiple_of(j * ROWS + start, 8), 8)]
        next_ref[rows] = ortho * scale
        return carry

    lax.fori_loop(0, ROWS // 8, step, 0, unroll=8)


def whole(memory=VMEM):
    return pl.BlockSpec(memory_space=memory)


def f32(*shape):
    return jax.ShapeDtypeStruct(shape, jnp.float32)


def params(mib):
    return pltpu.CompilerParams(vmem_limit_bytes=mib * 2**20)


def cost(flops, moved):
    return pl.CostEstimate(flops=flops, bytes_accessed=moved, transcendentals=0)


def swap(size, bit):
    return [(i, i ^ bit) for i in range(size)]


def exchange(sent):
    own = lax.all_to_all(sent, CHIPS, 0, 0)
    return own, lax.ppermute(own, "core", swap(2, 1))


FACES_VMEM = VMEM((FACES, 8, SQUARE), jnp.float32)
SENT = f32(CHIP_COUNT, FACES, 8, SQUARE)


def inner_section(field, coeff, name):
    width = CHUNK * SQUARE
    return pl.pallas_call(
        inner_kernel,
        grid=(SLABS // CHUNK,),
        in_specs=[
            pl.BlockSpec((8, CELLS), lambda i: (0, 0)),
            pl.BlockSpec((1, 7, VARS, VARS, width), lambda i: (0, 0, 0, 0, i)),
        ],
        out_specs=[
            pl.BlockSpec((8, width), lambda i: (0, i)),
            pl.BlockSpec((VARS, 8, width), lambda i: (0, 0, i)),
            pl.BlockSpec((VARS, 8, width), lambda i: (0, 0, i)),
            pl.BlockSpec((2 * PER, VARS, 8, SQUARE), lambda i: (0, 0, 0, 0)),
        ],
        out_shape=[f32(8, CELLS), f32(VARS, 8, CELLS), f32(VARS, 8, CELLS), f32(2 * PER, VARS, 8, SQUARE)],
        compiler_params=params(16),
        cost_estimate=cost(2 * 343 * CELLS, 10 * 2**20),
        name=name,
    )(field, coeff)


def mix(dense):
    parts = [dense] + [lax.ppermute(dense, "z", swap(4, k)) for k in (1, 2, 3)]
    kept, given = pl.pallas_call(
        mix_kernel,
        in_specs=[whole()] * 4,
        out_specs=[whole()] * 2,
        out_shape=[f32(ROWS, LANES)] * 2,
        compiler_params=params(8),
        cost_estimate=cost(16 * ROWS * LANES, 6 * 4 * ROWS * LANES),
        name="mix",
    )(*parts)
    return kept, lax.ppermute(given, "xl", swap(2, 1))


def local(basis, flux, recon, pseudo_time, vol_omega, block_ids, neighbour, orient):
    flat = basis.reshape(KRYLOV * ROWS, LANES)
    sent, padded, dense = pl.pallas_call(
        first_faces_kernel,
        in_specs=[whole(pl.ANY)],
        out_specs=[whole(pl.ANY), whole(), whole()],
        out_shape=[SENT, f32(8, CELLS), f32(ROWS, LANES)],
        scratch_shapes=[VMEM((8 * GROUPS, LANES), jnp.float32), FACES_VMEM, pltpu.SemaphoreType.DMA((CHIP_COUNT,))],
        compiler_params=params(8),
        cost_estimate=cost(10**6, 2 * 2**20),
        name="first_faces",
    )(flat)
    own, swapped = exchange(sent)
    table = pl.pallas_call(
        tables_kernel,
        in_specs=[whole(SMEM)] * 3,
        out_specs=whole(SMEM),
        out_shape=jax.ShapeDtypeStruct((4 * FACES,), jnp.int32),
        scratch_shapes=[SMEM((BLOCKS,), jnp.int32)],
        compiler_params=params(4),
        cost_estimate=cost(10**5, 10**5),
        name="tables",
    )(block_ids, neighbour.T, orient.T)
    kept, returned = mix(dense)
    gram = pl.pallas_call(
        gram_kernel,
        in_specs=[whole()],
        out_specs=whole(),
        out_shape=f32(8, LANES),
        scratch_shapes=[VMEM((KRYLOV * KRYLOV, LANES), jnp.float32)],
        compiler_params=params(8),
        cost_estimate=cost(2 * 36 * VARS * CELLS, 2 * 2**20),
        name="gram",
    )(flat)
    pieces = inner_section(padded, flux, "flux_inner")
    first, sent = pl.pallas_call(
        flux_kernel,
        in_specs=[whole(SMEM)] + [whole()] * 6,
        out_specs=[whole(), whole(pl.ANY)],
        out_shape=[f32(8, CELLS), SENT],
        scratch_shapes=[FACES_VMEM, FACES_VMEM, pltpu.SemaphoreType.DMA((CHIP_COUNT,))],
        compiler_params=params(16),
        cost_estimate=cost(10**6, 4 * 2**20),
        name="flux_outer",
    )(table, own, swapped, *pieces)
    own, swapped = exchange(sent)
    pieces = inner_section(first, recon, "recon_inner")
    image, sums = pl.pallas_call(
        image_kernel,
        in_specs=[whole(SMEM)] + [whole()] * 12,
        out_specs=[whole(), whole()],
        out_shape=[f32(ROWS, LANES), f32(LANES, LANES)],
        scratch_shapes=[FACES_VMEM, VMEM((8 * GROUPS, LANES), jnp.float32)],
        compiler_params=params(16),
        cost_estimate=cost(10**6, 6 * 2**20),
        name="image",
    )(
        table, own, swapped, *pieces,
        flat, pseudo_time.reshape(GROUPS, LANES), vol_omega.reshape(GROUPS, LANES), kept, returned, gram,
    )
    received = lax.all_to_all(sums, ALL, 0, 0)
    following, column = pl.pallas_call(
        finish_kernel,
        in_specs=[whole()] * 3,
        out_specs=[whole(), whole()],
        out_shape=[f32(ROWS, LANES), f32(8, LANES)],
        compiler_params=params(8),
        cost_estimate=cost(10**6, 3 * 2**20),
        name="finish",
    )(received, image, flat)

    def direct(state):
        coeffs = state[1][:KRYLOV]
        ortho = image - jnp.einsum(
            "k,krl->rl", coeffs, flat.reshape(KRYLOV, ROWS, LANES), precision=lax.Precision.HIGHEST
        )
        squares = lax.psum(jnp.sum(ortho * ortho), ALL) / ENTRIES
        norm = jnp.sqrt(squares + 1e-06)
        return (ortho / norm, jnp.concatenate([coeffs, norm[None], jnp.zeros((1,), jnp.float32)]))

    following, hessenberg = lax.while_loop(
        lambda state: state[1][KRYLOV + 1] > 0.5, direct, (following, column[0, : KRYLOV + 2])
    )
    return following.reshape(1, VARS, CELLS), hessenberg[: KRYLOV + 1]


def solution(mesh):
    fine = Mesh(mesh.devices.reshape(4, 2, 2, 4, 2), ALL)
    inst, space = (("z", "xl"), ("xh", "y", "core"))
    placed = (
        P(None, inst, None, space),
        P(inst, None, None, None, space),
        P(inst, None, None, None, space),
        P(space),
        P(space),
        P(),
        P(),
        P(),
    )
    return jax.shard_map(
        local,
        mesh=fine,
        in_specs=placed,
        out_specs=(P(inst, None, space), P()),
        check_vma=False,
    )
```

```python
import jax
import jax.numpy as jnp
import numpy as np
from jax import lax
from jax.experimental import pallas as pl
from jax.experimental.pallas import tpu as pltpu
from jax.sharding import Mesh, PartitionSpec as P

EDGE = 16
SQUARE = EDGE * EDGE
CUBE = EDGE * SQUARE
VARS = 7
KRYLOV = 8
INST = 8
BLOCKS = 32
SPACE = 16
CHIP_COUNT = 8
CELLS = 8192
PER = CELLS // CUBE
FACES = 6 * PER
SLABS = CELLS // SQUARE
ENTRIES = float(INST * VARS * CELLS * SPACE)
LANES = 128
GROUPS = CELLS // LANES
ROWS = VARS * GROUPS
ALL = ("z", "xl", "xh", "y", "core")
CHIPS = ("xh", "y")
VMEM = pltpu.VMEM
SMEM = pltpu.SMEM
GUARD = 0.02
CHUNK = 4
FLUX_INNER = 10**7
INNER_MIB = 50
OUTER_MIB = 16
MIX = 10**6
FLUX_OUTER = 10**6
RECON_INNER = 6 * 10**9


def mixing_weights():
    k = np.arange(1, INST)
    parity = np.where(k % 2 == 0, 1.0, -1.0)
    angle = np.pi * k / INST
    rest = 0.5 * parity / np.tan(angle) - 0.125 * parity / np.sin(angle) ** 2
    return [-0.25 * (INST * INST + 2) / 12.0] + [float(v) for v in rest]


def lanes(shape):
    return lax.broadcasted_iota(jnp.int32, shape, len(shape) - 1)


def sublanes(shape):
    return lax.broadcasted_iota(jnp.int32, shape, len(shape) - 2)


def pick(values, index):
    return jnp.take_along_axis(values, index, axis=1)


def fold(totals):
    row = sublanes(totals[0].shape)
    for width in (1, 2, 4):
        first = row % (2 * width) < width
        totals = [
            jnp.where(first, a, b) + pltpu.roll(jnp.where(first, b, a), width, 0)
            for a, b in zip(totals[::2], totals[1::2])
        ]
    return totals[0]


def strips_of(slab, x, strips):
    lane = lanes((8, LANES))
    low, high = (slab[:, :LANES], slab[:, LANES:])
    own = lane >> 4 == x
    upper = lane & 8 != 0
    z = lane & 15
    source = (lane & 7) << 4
    found = (
        pick(low, z),
        pick(high, z + (LANES - EDGE)),
        jnp.where(upper, pick(high, source), pick(low, source)),
        jnp.where(upper, pick(high, source + 15), pick(low, source + 15)),
    )
    if strips is None:
        return list(found)
    return [jnp.where(own, new, old) for new, old in zip(found, strips)]


def collect_block(field_ref, faces, block):
    start = block * CUBE
    faces[block * 6] = field_ref[:, start : start + SQUARE]
    faces[block * 6 + 1] = field_ref[:, start + CUBE - SQUARE : start + CUBE]
    for half in range(2):
        strips = None
        for inner in range(8):
            place = start + (half * 8 + inner) * SQUARE
            strips = strips_of(field_ref[:, place : place + SQUARE], inner, strips)
        for number, strip in enumerate(strips):
            faces[block * 6 + 2 + number, :, half * LANES : (half + 1) * LANES] = strip


def send_block(faces, sent_ref, arrived, block):
    rows = pl.ds(block * 6, 6)
    copies = [
        pltpu.make_async_copy(faces.at[rows], sent_ref.at[chip, rows], arrived.at[block, chip])
        for chip in range(CHIP_COUNT)
    ]
    for copy in copies:
        copy.start()
    return copies


def first_faces_kernel(basis_ref, sent_ref, padded_ref, dense_ref, field, faces, arrived):
    fetch = pltpu.make_async_copy(
        basis_ref.at[pl.ds((KRYLOV - 1) * ROWS, ROWS)], field.at[pl.ds(0, ROWS)], arrived.at[0, 0]
    )
    fetch.start()
    field[ROWS:] = jnp.zeros((GROUPS, LANES), jnp.float32)
    fetch.wait()
    copies = []
    for block in range(PER):
        for group in range(block * 32, block * 32 + 32):
            padded_ref[:, group * LANES : (group + 1) * LANES] = field[pl.ds(group, 8, stride=GROUPS), :]
        collect_block(padded_ref, faces, block)
        copies += send_block(faces, sent_ref, arrived, block)
    dense_ref[...] = field[:ROWS]
    for copy in copies:
        copy.wait()


def tables_kernel(ids_ref, neighbour_ref, orient_ref, table_ref, position):
    core = lax.axis_index("core")
    rank = (lax.axis_index("xh") * 4 + lax.axis_index("y")) * 2 + core

    def place(slot, carry):
        position[ids_ref[slot]] = slot
        return carry

    lax.fori_loop(0, BLOCKS, place, 0)
    for number in range(FACES):
        owner = ids_ref[rank * PER + number // 6]
        partner = neighbour_ref[number % 6, owner]
        code = orient_ref[number % 6, owner]
        target = jnp.maximum(partner, 0)
        slot = position[target // 6]
        device = slot // PER
        table_ref[number * 4] = device // 2
        table_ref[number * 4 + 1] = jnp.where(device % 2 == core, 1, 0)
        table_ref[number * 4 + 2] = (slot % PER) * 6 + target % 6
        table_ref[number * 4 + 3] = jnp.where(partner < 0, -1, code)


def fetch_halos(table_ref, own_ref, swapped_ref, halos):
    lane = lanes((8, LANES))
    for number in range(FACES):
        chip = table_ref[number * 4]
        here = table_ref[number * 4 + 1] == 1
        row = table_ref[number * 4 + 2]
        code = table_ref[number * 4 + 3]
        wall = code < 0
        code = jnp.maximum(code, 0)
        source = jnp.where(here, own_ref[chip, row], swapped_ref[chip, row])
        source = jnp.where(wall, 0.0, source)
        low, high = (source[:, :LANES], source[:, LANES:])
        transposed = code & 1 == 1
        flip_a = (code >> 1 & 1) * (EDGE - 1)
        flip_b = (code >> 2) * (EDGE - 1)
        for half in range(2):
            a = ((lane >> 4) + half * 8) ^ flip_a
            b = (lane & 15) ^ flip_b
            index = jnp.where(transposed, (b << 4) + a, (a << 4) + b)
            inside = index & (LANES - 1)
            halos[number, :, half * LANES : (half + 1) * LANES] = jnp.where(
                index < LANES, pick(low, inside), pick(high, inside)
            )


def inner_kernel(
    field_ref, coeff_ref, part_ref, across_z_ref, across_y_ref, across_x_ref, token_ref, held, arrived
):
    column = lanes((8, SQUARE))
    z = column & 15
    width = CHUNK * SQUARE
    chunks = SLABS // CHUNK
    copies = [
        pltpu.make_async_copy(coeff_ref.at[0, :, :, :, pl.ds(i * width, width)], held.at[i], arrived.at[i])
        for i in range(chunks)
    ]
    for copy in copies:
        copy.start()

    def load(k):
        return field_ref[:, pl.ds(pl.multiple_of(k * SQUARE, SQUARE), SQUARE)]

    def chunk_step(chunk, carry):
        pltpu.make_async_copy(
            coeff_ref.at[0, :, :, :, pl.ds(0, width)], held.at[chunk], arrived.at[chunk]
        ).wait()
        for inner in range(CHUNK):

            def coeff(s, o):
                value = held[chunk, s, o, :, inner * SQUARE : (inner + 1) * SQUARE].astype(jnp.float32)
                return jnp.concatenate([value, jnp.zeros((1, SQUARE), jnp.float32)], axis=0)

            k = chunk * CHUNK + inner
            block, x = (k // EDGE, k % EDGE)
            place = pl.ds(pl.multiple_of(k * SQUARE, SQUARE), SQUARE)
            centre = load(k)
            below, above = (load(jnp.maximum(k - 1, 0)), load(jnp.minimum(k + 1, SLABS - 1)))
            if inner == 0:
                below = jnp.where(x == 0, 0.0, below)
            if inner == CHUNK - 1:
                above = jnp.where(x == EDGE - 1, 0.0, above)
            operands = [
                centre,
                below,
                above,
                jnp.where(column < EDGE, 0.0, pltpu.roll(centre, EDGE, 1)),
                jnp.where(column >= SQUARE - EDGE, 0.0, pltpu.roll(centre, SQUARE - EDGE, 1)),
                jnp.where(z == 0, 0.0, pltpu.roll(centre, 1, 1)),
                jnp.where(z == EDGE - 1, 0.0, pltpu.roll(centre, SQUARE - 1, 1)),
            ]
            totals = []
            for o in range(VARS):
                values = [coeff(s, o) for s in range(7)]
                total = values[0] * operands[0]
                for s in range(1, 7):
                    total = total + values[s] * operands[s]
                totals.append(total)
                across_z_ref[o, :, place] = jnp.where(
                    z == 0, values[5], jnp.where(z == EDGE - 1, values[6], 0.0)
                ).astype(jnp.bfloat16)
                across_y_ref[o, :, place] = jnp.where(
                    column < EDGE, values[3], jnp.where(column >= SQUARE - EDGE, values[4], 0.0)
                ).astype(jnp.bfloat16)
            part_ref[:, place] = fold(totals + [jnp.zeros((8, SQUARE), jnp.float32)])

            if inner == 0:

                @pl.when(x == 0)
                def _():
                    for o in range(VARS):
                        across_x_ref[block * 2, o] = coeff(1, o).astype(jnp.bfloat16)

            if inner == CHUNK - 1:

                @pl.when(x == EDGE - 1)
                def _():
                    for o in range(VARS):
                        across_x_ref[block * 2 + 1, o] = coeff(2, o).astype(jnp.bfloat16)

        return carry

    lax.fori_loop(0, chunks, chunk_step, 0)
    token_ref[...] = jnp.zeros_like(token_ref)


def outer_slab(part_ref, across_z_ref, across_y_ref, halos, block, half, inner):
    lane = lanes((8, LANES))
    offset = inner * EDGE
    start = block * CUBE + (half * 8 + inner) * SQUARE
    place = slice(start, start + SQUARE)

    def strip(face):
        return halos[block * 6 + face, :, half * LANES : (half + 1) * LANES]

    y = (lane & 15) + offset
    z = (lane >> 4) + offset
    at_low = lane & 15 == 0
    across_y = jnp.concatenate([pick(strip(2), y), pick(strip(3), y)], axis=1)
    z_low, z_high = (strip(4), strip(5))
    across_z = jnp.concatenate(
        [
            jnp.where(at_low, pick(z_low, z), pick(z_high, z)),
            jnp.where(at_low, pick(z_low, z + 8), pick(z_high, z + 8)),
        ],
        axis=1,
    )
    totals = [
        across_z_ref[o, :, place].astype(jnp.float32) * across_z
        + across_y_ref[o, :, place].astype(jnp.float32) * across_y
        for o in range(VARS)
    ]
    return part_ref[:, place] + fold(totals + [jnp.zeros((8, SQUARE), jnp.float32)])


def outer_x(across_x_ref, halos, block, side):
    halo = halos[block * 6 + side]
    totals = [across_x_ref[block * 2 + side, o].astype(jnp.float32) * halo for o in range(VARS)]
    return fold(totals + [jnp.zeros((8, SQUARE), jnp.float32)])


def outer_block(across_x_ref, part_ref, across_z_ref, across_y_ref, halos, block, put):
    for half in range(2):
        for inner in range(8):
            slab = outer_slab(part_ref, across_z_ref, across_y_ref, halos, block, half, inner)
            if half == 0 and inner == 0:
                slab = slab + outer_x(across_x_ref, halos, block, 0)
            if half == 1 and inner == 7:
                slab = slab + outer_x(across_x_ref, halos, block, 1)
            put(block * EDGE + half * 8 + inner, slab)


def flux_kernel(
    table_ref, own_ref, swapped_ref, part_ref, across_z_ref, across_y_ref, across_x_ref, token_ref,
    first_ref, sent_ref, halos, faces, arrived
):
    fetch_halos(table_ref, own_ref, swapped_ref, halos)

    def put(k, slab):
        first_ref[:, k * SQUARE : (k + 1) * SQUARE] = slab

    copies = []
    for block in range(PER):
        outer_block(across_x_ref, part_ref, across_z_ref, across_y_ref, halos, block, put)
        collect_block(first_ref, faces, block)
        copies += send_block(faces, sent_ref, arrived, block)
    for copy in copies:
        copy.wait()


def mix_kernel(own_ref, one_ref, two_ref, three_ref, first_ref, kept_ref, given_ref):
    z = lax.axis_index("z")
    xl = lax.axis_index("xl")
    table = mixing_weights()

    def weight(offset):
        offset = lax.rem(offset + 2 * INST, INST)
        value = jnp.float32(table[0])
        for k in range(1, INST):
            value = jnp.where(offset == k, jnp.float32(table[k]), value)
        return value

    fields = (own_ref, one_ref, two_ref, three_ref)
    sources = [2 * (z ^ k) + xl for k in range(4)]
    kept = [weight(source - (2 * z + xl)) for source in sources]
    given = [weight(source - (2 * z + 1 - xl)) for source in sources]

    def step(k, carry):
        rows = pl.ds(pl.multiple_of(k * 64, 64), 64)
        values = [field[rows] for field in fields]
        kept_ref[rows] = sum(w * v for w, v in zip(kept, values))
        given_ref[rows] = sum(w * v for w, v in zip(given, values))
        return carry

    lax.fori_loop(0, ROWS // 64, step, 0)


def lane_sums(rows, first_lane):
    totals = jnp.broadcast_to(jnp.sum(rows, axis=1, keepdims=True), rows.shape)
    spot = lanes(rows.shape) == sublanes(rows.shape) + first_lane
    return jnp.sum(jnp.where(spot, totals, 0.0), axis=0, keepdims=True)


def gram_kernel(flat_ref, basis_ref, gram_ref, lines, arrived):
    copy = pltpu.make_async_copy(flat_ref, basis_ref, arrived)
    copy.start()
    copy.wait()

    def step(k, totals):
        fields = [
            basis_ref[pl.ds(pl.multiple_of(j * ROWS + k * 8, 8), 8)] for j in range(KRYLOV)
        ]
        out = []
        for i in range(KRYLOV):
            for j in range(i, KRYLOV):
                out.append(totals[len(out)] + fields[i] * fields[j])
        return tuple(out)

    zero = jnp.zeros((8, LANES), jnp.float32)
    totals = lax.fori_loop(0, ROWS // 8, step, (zero,) * (KRYLOV * (KRYLOV + 1) // 2))
    number = 0
    for i in range(KRYLOV):
        for j in range(i, KRYLOV):
            line = jnp.sum(totals[number], axis=0, keepdims=True)
            lines[i * KRYLOV + j : i * KRYLOV + j + 1] = line
            lines[j * KRYLOV + i : j * KRYLOV + i + 1] = line
            number += 1
    gram_ref[...] = jnp.broadcast_to(lane_sums(lines[...], 64), (8, LANES))


def image_kernel(
    table_ref, own_ref, swapped_ref, part_ref, across_z_ref, across_y_ref, across_x_ref,
    basis_ref, pseudo_ref, omega_ref, kept_ref, returned_ref, gram_ref, token_ref,
    image_ref, sums_ref, halos, section
):
    fetch_halos(table_ref, own_ref, swapped_ref, halos)

    def put(k, slab):
        section[pl.ds(2 * k, 8, stride=GROUPS), :] = slab[:, :LANES]
        section[pl.ds(2 * k + 1, 8, stride=GROUPS), :] = slab[:, LANES:]

    for block in range(PER):
        outer_block(across_x_ref, part_ref, across_z_ref, across_y_ref, halos, block, put)

    def step(k, totals):
        start = k * 8
        cells = pl.ds(pl.multiple_of(start % GROUPS, 8), 8)
        rows = pl.ds(pl.multiple_of(start, 8), 8)
        fields = [basis_ref[pl.ds(pl.multiple_of(j * ROWS + start, 8), 8)] for j in range(KRYLOV)]
        spectral = kept_ref[rows] + returned_ref[rows]
        image = pseudo_ref[cells] * fields[KRYLOV - 1] + section[rows] + omega_ref[cells] * spectral
        image_ref[rows] = image
        return tuple(total + field * image for total, field in zip(totals, fields + [image]))

    zero = jnp.zeros((8, LANES), jnp.float32)
    totals = lax.fori_loop(0, ROWS // 8, step, (zero,) * (KRYLOV + 1), unroll=8)
    lines = [jnp.sum(total, axis=0, keepdims=True) for total in totals]
    lines += [jnp.zeros((16 - len(lines), LANES), jnp.float32)]
    sums = jnp.broadcast_to(lane_sums(jnp.concatenate(lines, axis=0), 0), (8, LANES)) + gram_ref[...]
    for group in range(16):
        sums_ref[group * 8 : group * 8 + 8] = sums


def finish_kernel(received_ref, image_ref, basis_ref, next_ref, column_ref, flag_ref, column_held, sent):
    sums = jnp.sum(received_ref[...], axis=0, keepdims=True)
    sums = jnp.broadcast_to(sums, (8, LANES)) / ENTRIES
    lane = lanes((8, LANES))
    left = pick(sums, jnp.maximum(lane - 64, 0) // 8)
    right = pick(sums, lane % 8)
    quadratic = jnp.sum(jnp.where(lane >= 64, sums * left * right, 0.0), axis=1, keepdims=True)
    linear = jnp.sum(jnp.where(lane < KRYLOV, sums * sums, 0.0), axis=1, keepdims=True)
    whole_square = sums[:, KRYLOV : KRYLOV + 1]
    squares = whole_square - 2.0 * linear + quadratic
    size = whole_square + 2.0 * linear + jnp.abs(quadratic)
    norm = jnp.sqrt(jnp.maximum(squares, 0.0) + 1e-06)
    column = jnp.where(lane < KRYLOV, sums, jnp.where(lane == KRYLOV, norm, 0.0))
    column_held[...] = column[:1, : KRYLOV + 1]
    copy = pltpu.make_async_copy(column_held, column_ref, sent)
    copy.start()
    flag_ref[0] = jnp.sum(jnp.where(squares[:1] < GUARD * size[:1], 1.0, 0.0)).astype(jnp.int32)
    coeffs = [jnp.broadcast_to(sums[:, j : j + 1], (8, LANES)) for j in range(KRYLOV)]
    scale = jnp.broadcast_to(1.0 / norm, (8, LANES))

    def step(k, carry):
        start = k * 8
        rows = pl.ds(pl.multiple_of(start, 8), 8)
        ortho = image_ref[rows]
        for j in range(KRYLOV):
            ortho = ortho - coeffs[j] * basis_ref[pl.ds(pl.multiple_of(j * ROWS + start, 8), 8)]
        next_ref[rows] = ortho * scale
        return carry

    lax.fori_loop(0, ROWS // 8, step, 0, unroll=8)
    copy.wait()


def whole(memory=VMEM):
    return pl.BlockSpec(memory_space=memory)


def f32(*shape):
    return jax.ShapeDtypeStruct(shape, jnp.float32)


def bf16(*shape):
    return jax.ShapeDtypeStruct(shape, jnp.bfloat16)


def params(mib):
    return pltpu.CompilerParams(vmem_limit_bytes=mib * 2**20)


def cost(flops, moved):
    return pl.CostEstimate(flops=flops, bytes_accessed=moved, transcendentals=0)


def swap(size, bit):
    return [(i, i ^ bit) for i in range(size)]


def exchange(sent):
    return lax.all_to_all(sent, CHIPS, 0, 0)


def after(value, others):
    return lax.optimization_barrier((value, others))


def swap_cores(own):
    return lax.ppermute(own, "core", swap(2, 1))


FACES_VMEM = VMEM((FACES, 8, SQUARE), jnp.float32)
SENT = f32(CHIP_COUNT, FACES, 8, SQUARE)


def inner_section(field, coeff, name, flops):
    chunks = SLABS // CHUNK
    return pl.pallas_call(
        inner_kernel,
        in_specs=[whole(), whole(pltpu.HBM)],
        out_specs=[whole()] * 5,
        out_shape=[
            f32(8, CELLS), bf16(VARS, 8, CELLS), bf16(VARS, 8, CELLS), bf16(2 * PER, VARS, 8, SQUARE), f32(8, LANES),
        ],
        scratch_shapes=[
            VMEM((chunks, 7, VARS, VARS, CHUNK * SQUARE), jnp.bfloat16),
            pltpu.SemaphoreType.DMA((chunks,)),
        ],
        compiler_params=params(INNER_MIB),
        cost_estimate=cost(flops, 8 * 2**20),
        name=name,
    )(field, coeff)


def mix(parts, first):
    kept, given = pl.pallas_call(
        mix_kernel,
        in_specs=[whole()] * 4 + [whole(pl.ANY)],
        out_specs=[whole()] * 2,
        out_shape=[f32(ROWS, LANES), f32(ROWS, LANES)],
        compiler_params=params(8),
        cost_estimate=cost(MIX, 6 * 4 * ROWS * LANES),
        name="mix",
    )(*parts, first)
    return kept, lax.ppermute(given, "xl", swap(2, 1))


def local(basis, flux, recon, pseudo_time, vol_omega, block_ids, neighbour, orient):
    flat = basis.reshape(KRYLOV * ROWS, LANES)
    sent, padded, dense = pl.pallas_call(
        first_faces_kernel,
        in_specs=[whole(pl.ANY)],
        out_specs=[whole(pl.ANY), whole(), whole()],
        out_shape=[SENT, f32(8, CELLS), f32(ROWS, LANES)],
        scratch_shapes=[VMEM((8 * GROUPS, LANES), jnp.float32), FACES_VMEM, pltpu.SemaphoreType.DMA((PER, CHIP_COUNT))],
        compiler_params=params(8),
        cost_estimate=cost(10**6, 2 * 2**20),
        name="first_faces",
    )(flat)
    own = exchange(sent)
    table = pl.pallas_call(
        tables_kernel,
        in_specs=[whole(SMEM)] * 3,
        out_specs=whole(SMEM),
        out_shape=jax.ShapeDtypeStruct((4 * FACES,), jnp.int32),
        scratch_shapes=[SMEM((BLOCKS,), jnp.int32)],
        compiler_params=params(4),
        cost_estimate=cost(10**5, 10**5),
        name="tables",
    )(block_ids, neighbour.T, orient.T)
    held, gram = pl.pallas_call(
        gram_kernel,
        in_specs=[whole(pl.ANY)],
        out_specs=[whole(), whole()],
        out_shape=[f32(KRYLOV * ROWS, LANES), f32(8, LANES)],
        scratch_shapes=[VMEM((KRYLOV * KRYLOV, LANES), jnp.float32), pltpu.SemaphoreType.DMA],
        compiler_params=params(8),
        cost_estimate=cost(2 * 36 * VARS * CELLS, 2 * 2**20),
        name="gram",
    )(flat)
    *pieces, token = inner_section(padded, flux, "flux_inner", FLUX_INNER)
    one, two, three = [lax.ppermute(dense, "z", swap(4, k)) for k in (1, 2, 3)]
    own, (token, table, one, three) = after(own, (token, table, one, three))
    parts = (dense, one, two, three)
    swapped = swap_cores(own)
    first, sent = pl.pallas_call(
        flux_kernel,
        in_specs=[whole(SMEM)] + [whole()] * 6 + [whole(pl.ANY)],
        out_specs=[whole(), whole(pl.ANY)],
        out_shape=[f32(8, CELLS), SENT],
        scratch_shapes=[FACES_VMEM, FACES_VMEM, pltpu.SemaphoreType.DMA((PER, CHIP_COUNT))],
        compiler_params=params(OUTER_MIB),
        cost_estimate=cost(FLUX_OUTER, 4 * 2**20),
        name="flux_outer",
    )(table, own, swapped, *pieces, token)
    own = exchange(sent)
    kept, returned = mix(parts, first)
    *pieces, token = inner_section(first, recon, "recon_inner", RECON_INNER)
    own, (token, returned) = after(own, (token, returned))
    swapped = swap_cores(own)
    image, sums = pl.pallas_call(
        image_kernel,
        in_specs=[whole(SMEM)] + [whole()] * 12 + [whole(pl.ANY)],
        out_specs=[whole(), whole()],
        out_shape=[f32(ROWS, LANES), f32(LANES, LANES)],
        scratch_shapes=[FACES_VMEM, VMEM((8 * GROUPS, LANES), jnp.float32)],
        compiler_params=params(OUTER_MIB),
        cost_estimate=cost(10**6, 6 * 2**20),
        name="image",
    )(
        table, own, swapped, *pieces,
        held, pseudo_time.reshape(GROUPS, LANES), vol_omega.reshape(GROUPS, LANES), kept, returned, gram, token,
    )
    received = lax.all_to_all(sums, ALL, 0, 0)
    following, column, flag = pl.pallas_call(
        finish_kernel,
        in_specs=[whole()] * 3,
        out_specs=[whole(), whole(pl.ANY), whole(SMEM)],
        out_shape=[f32(ROWS, LANES), f32(1, KRYLOV + 1), jax.ShapeDtypeStruct((1,), jnp.int32)],
        scratch_shapes=[VMEM((1, KRYLOV + 1), jnp.float32), pltpu.SemaphoreType.DMA],
        compiler_params=params(8),
        cost_estimate=cost(10**6, 3 * 2**20),
        name="finish",
    )(received, image, held)

    def direct(state):
        coeffs = state[1][0, :KRYLOV]
        ortho = image - jnp.einsum(
            "k,krl->rl", coeffs, flat.reshape(KRYLOV, ROWS, LANES), precision=lax.Precision.HIGHEST
        )
        squares = lax.psum(jnp.sum(ortho * ortho), ALL) / ENTRIES
        norm = jnp.sqrt(squares + 1e-06)
        return (ortho / norm, jnp.concatenate([coeffs, norm[None]])[None], jnp.zeros((), jnp.int32))

    following, column, _ = lax.while_loop(
        lambda state: state[2] > 0, direct, (following, column, flag[0])
    )
    return following.reshape(1, VARS, CELLS), column[0]


def solution(mesh):
    fine = Mesh(mesh.devices.reshape(4, 2, 2, 4, 2), ALL)
    inst, space = (("z", "xl"), ("xh", "y", "core"))
    placed = (
        P(None, inst, None, space),
        P(inst, None, None, None, space),
        P(inst, None, None, None, space),
        P(space),
        P(space),
        P(),
        P(),
        P(),
    )
    return jax.shard_map(
        local,
        mesh=fine,
        in_specs=placed,
        out_specs=(P(inst, None, space), P()),
        check_vma=False,
    )
```

```python
import jax
import jax.numpy as jnp
import numpy as np
from jax import lax
from jax.experimental import pallas as pl
from jax.experimental.pallas import tpu as pltpu
from jax.sharding import Mesh, PartitionSpec as P

EDGE = 16
SQUARE = EDGE * EDGE
CUBE = EDGE * SQUARE
VARS = 7
KRYLOV = 8
INST = 8
BLOCKS = 32
SPACE = 16
CHIP_COUNT = 8
CELLS = 8192
PER = CELLS // CUBE
FACES = 6 * PER
SLABS = CELLS // SQUARE
ENTRIES = float(INST * VARS * CELLS * SPACE)
LANES = 128
GROUPS = CELLS // LANES
ROWS = VARS * GROUPS
ALL = ("z", "xl", "xh", "y", "core")
CHIPS = ("xh", "y")
VMEM = pltpu.VMEM
SMEM = pltpu.SMEM
GUARD = 0.02
CHUNK = 4
FLUX_INNER = 10**7
INNER_MIB = 46
OUTER_MIB = 16
MIX = 10**6
FLUX_OUTER = 10**6
RECON_INNER = 2 * 10**10


def mixing_weights():
    k = np.arange(1, INST)
    parity = np.where(k % 2 == 0, 1.0, -1.0)
    angle = np.pi * k / INST
    rest = 0.5 * parity / np.tan(angle) - 0.125 * parity / np.sin(angle) ** 2
    return [-0.25 * (INST * INST + 2) / 12.0] + [float(v) for v in rest]


def lanes(shape):
    return lax.broadcasted_iota(jnp.int32, shape, len(shape) - 1)


def sublanes(shape):
    return lax.broadcasted_iota(jnp.int32, shape, len(shape) - 2)


def pick(values, index):
    return jnp.take_along_axis(values, index, axis=1)


def fold(totals):
    row = sublanes(totals[0].shape)
    for width in (1, 2, 4):
        first = row % (2 * width) < width
        totals = [
            jnp.where(first, a, b) + pltpu.roll(jnp.where(first, b, a), width, 0)
            for a, b in zip(totals[::2], totals[1::2])
        ]
    return totals[0]


def strips_of(slab, x, strips):
    lane = lanes((8, LANES))
    low, high = (slab[:, :LANES], slab[:, LANES:])
    own = lane >> 4 == x
    upper = lane & 8 != 0
    z = lane & 15
    source = (lane & 7) << 4
    found = (
        pick(low, z),
        pick(high, z + (LANES - EDGE)),
        jnp.where(upper, pick(high, source), pick(low, source)),
        jnp.where(upper, pick(high, source + 15), pick(low, source + 15)),
    )
    if strips is None:
        return list(found)
    return [jnp.where(own, new, old) for new, old in zip(found, strips)]


def collect_block(field_ref, faces, block):
    start = block * CUBE
    faces[block * 6] = field_ref[:, start : start + SQUARE]
    faces[block * 6 + 1] = field_ref[:, start + CUBE - SQUARE : start + CUBE]
    for half in range(2):
        strips = None
        for inner in range(8):
            place = start + (half * 8 + inner) * SQUARE
            strips = strips_of(field_ref[:, place : place + SQUARE], inner, strips)
        for number, strip in enumerate(strips):
            faces[block * 6 + 2 + number, :, half * LANES : (half + 1) * LANES] = strip


def send_block(faces, sent_ref, arrived, block):
    rows = pl.ds(block * 6, 6)
    copies = [
        pltpu.make_async_copy(faces.at[rows], sent_ref.at[chip, rows], arrived.at[block, chip])
        for chip in range(CHIP_COUNT)
    ]
    for copy in copies:
        copy.start()
    return copies


def first_faces_kernel(basis_ref, sent_ref, padded_ref, dense_ref, field, faces, arrived):
    fetch = pltpu.make_async_copy(
        basis_ref.at[pl.ds((KRYLOV - 1) * ROWS, ROWS)], field.at[pl.ds(0, ROWS)], arrived.at[0, 0]
    )
    fetch.start()
    field[ROWS:] = jnp.zeros((GROUPS, LANES), jnp.float32)
    fetch.wait()
    copies = []
    for block in range(PER):
        for group in range(block * 32, block * 32 + 32):
            padded_ref[:, group * LANES : (group + 1) * LANES] = field[pl.ds(group, 8, stride=GROUPS), :]
        collect_block(padded_ref, faces, block)
        copies += send_block(faces, sent_ref, arrived, block)
    dense_ref[...] = field[:ROWS]
    for copy in copies:
        copy.wait()


PART_OF = (4, 0, 1, 0, 1, 2, 3, 2)
CORE_OF = (0, 0, 0, 1, 1, 0, 0, 1)


def tables_kernel(ids_ref, neighbour_ref, orient_ref, table_ref, later_ref, position):
    core = lax.axis_index("core")
    chip = lax.axis_index("xh") * 4 + lax.axis_index("y")

    def place(slot, carry):
        position[ids_ref[slot]] = slot
        return carry

    lax.fori_loop(0, BLOCKS, place, 0)

    def pick_of(values, index):
        result = jnp.int32(values[0])
        for k in range(1, len(values)):
            result = jnp.where(index == k, jnp.int32(values[k]), result)
        return result

    for mine in (True, False):
        for number in range(FACES):
            rank = chip * 2 + (core if mine else 1 - core)
            owner = ids_ref[rank * PER + number // 6]
            partner = neighbour_ref[number % 6, owner]
            target = jnp.maximum(partner, 0)
            slot = position[target // 6]
            device = slot // PER
            row = (slot % PER) * 6 + target % 6
            source_core = device % 2
            offset = (device // 2) ^ chip
            part = pick_of(PART_OF, offset)
            among = jnp.where(source_core == core, row, row + FACES)
            if mine:
                code = jnp.where(partner < 0, -1, orient_ref[number % 6, owner])
                same = source_core == core
                table_ref[number * 4] = device // 2
                table_ref[number * 4 + 1] = jnp.where(same, 1, 0)
                table_ref[number * 4 + 2] = row
                table_ref[number * 4 + 3] = code
                here = jnp.where(
                    part == 4, True, jnp.where(part == 3, same, pick_of(CORE_OF, offset) == core)
                )
                later_ref[number * 5] = part
                later_ref[number * 5 + 1] = among
                later_ref[number * 5 + 2] = row
                later_ref[number * 5 + 3] = jnp.where(here, 1, 0)
                later_ref[number * 5 + 4] = code
            else:
                later_ref[5 * FACES + number * 3] = part
                later_ref[5 * FACES + number * 3 + 1] = among
                later_ref[5 * FACES + number * 3 + 2] = row


def choose(parts, part, among, row):
    value = parts[4][among]
    for k in range(3):
        value = jnp.where(part == k, parts[k][among], value)
    return jnp.where(part == 3, parts[3][row], value)


def select_kernel(
    later_ref, one_ref, two_ref, three_ref, four_ref, chip_ref, token_ref, wanted_ref
):
    parts = (one_ref, two_ref, three_ref, four_ref, chip_ref)
    for number in range(FACES):
        base = 5 * FACES + number * 3
        wanted_ref[number] = choose(parts, later_ref[base], later_ref[base + 1], later_ref[base + 2])


def turn_face(source, code, halos, number):
    lane = lanes((8, LANES))
    source = jnp.where(code < 0, 0.0, source)
    code = jnp.maximum(code, 0)
    low, high = (source[:, :LANES], source[:, LANES:])
    transposed = code & 1 == 1
    flip_a = (code >> 1 & 1) * (EDGE - 1)
    flip_b = (code >> 2) * (EDGE - 1)
    for half in range(2):
        a = ((lane >> 4) + half * 8) ^ flip_a
        b = (lane & 15) ^ flip_b
        index = jnp.where(transposed, (b << 4) + a, (a << 4) + b)
        inside = index & (LANES - 1)
        halos[number, :, half * LANES : (half + 1) * LANES] = jnp.where(
            index < LANES, pick(low, inside), pick(high, inside)
        )


def fetch_halos(table_ref, own_ref, swapped_ref, halos):
    for number in range(FACES):
        chip = table_ref[number * 4]
        here = table_ref[number * 4 + 1] == 1
        row = table_ref[number * 4 + 2]
        source = jnp.where(here, own_ref[chip, row], swapped_ref[chip, row])
        turn_face(source, table_ref[number * 4 + 3], halos, number)


def fetch_later_halos(later_ref, parts, swapped_ref, halos):
    for number in range(FACES):
        base = number * 5
        source = choose(parts, later_ref[base], later_ref[base + 1], later_ref[base + 2])
        source = jnp.where(later_ref[base + 3] == 1, source, swapped_ref[number])
        turn_face(source, later_ref[base + 4], halos, number)


def inner_kernel(
    field_ref, coeff_ref, part_ref, across_z_ref, across_y_ref, across_x_ref, token_ref, held, arrived
):
    column = lanes((8, SQUARE))
    z = column & 15
    width = CHUNK * SQUARE
    chunks = SLABS // CHUNK
    copies = [
        pltpu.make_async_copy(coeff_ref.at[0, :, :, :, pl.ds(i * width, width)], held.at[i], arrived.at[i])
        for i in range(chunks)
    ]
    for copy in copies:
        copy.start()

    def load(k):
        return field_ref[:, pl.ds(pl.multiple_of(k * SQUARE, SQUARE), SQUARE)]

    def chunk_step(chunk, carry):
        pltpu.make_async_copy(
            coeff_ref.at[0, :, :, :, pl.ds(0, width)], held.at[chunk], arrived.at[chunk]
        ).wait()
        for inner in range(CHUNK):

            def coeff(s, o):
                value = held[chunk, s, o, :, inner * SQUARE : (inner + 1) * SQUARE].astype(jnp.float32)
                return jnp.concatenate([value, jnp.zeros((1, SQUARE), jnp.float32)], axis=0)

            k = chunk * CHUNK + inner
            block, x = (k // EDGE, k % EDGE)
            place = pl.ds(pl.multiple_of(k * SQUARE, SQUARE), SQUARE)
            centre = load(k)
            below, above = (load(jnp.maximum(k - 1, 0)), load(jnp.minimum(k + 1, SLABS - 1)))
            if inner == 0:
                below = jnp.where(x == 0, 0.0, below)
            if inner == CHUNK - 1:
                above = jnp.where(x == EDGE - 1, 0.0, above)
            operands = [
                centre,
                below,
                above,
                jnp.where(column < EDGE, 0.0, pltpu.roll(centre, EDGE, 1)),
                jnp.where(column >= SQUARE - EDGE, 0.0, pltpu.roll(centre, SQUARE - EDGE, 1)),
                jnp.where(z == 0, 0.0, pltpu.roll(centre, 1, 1)),
                jnp.where(z == EDGE - 1, 0.0, pltpu.roll(centre, SQUARE - 1, 1)),
            ]
            totals = []
            for o in range(VARS):
                values = [coeff(s, o) for s in range(7)]
                total = values[0] * operands[0]
                for s in range(1, 7):
                    total = total + values[s] * operands[s]
                totals.append(total)
                across_z_ref[o, :, place] = jnp.where(
                    z == 0, values[5], jnp.where(z == EDGE - 1, values[6], 0.0)
                ).astype(jnp.bfloat16)
                across_y_ref[o, :, place] = jnp.where(
                    column < EDGE, values[3], jnp.where(column >= SQUARE - EDGE, values[4], 0.0)
                ).astype(jnp.bfloat16)
            part_ref[:, place] = fold(totals + [jnp.zeros((8, SQUARE), jnp.float32)])

            if inner == 0:

                @pl.when(x == 0)
                def _():
                    for o in range(VARS):
                        across_x_ref[block * 2, o] = coeff(1, o).astype(jnp.bfloat16)

            if inner == CHUNK - 1:

                @pl.when(x == EDGE - 1)
                def _():
                    for o in range(VARS):
                        across_x_ref[block * 2 + 1, o] = coeff(2, o).astype(jnp.bfloat16)

        return carry

    lax.fori_loop(0, chunks, chunk_step, 0)
    token_ref[...] = jnp.zeros_like(token_ref)


def outer_slab(part_ref, across_z_ref, across_y_ref, halos, block, half, inner):
    lane = lanes((8, LANES))
    offset = inner * EDGE
    start = block * CUBE + (half * 8 + inner) * SQUARE
    place = slice(start, start + SQUARE)

    def strip(face):
        return halos[block * 6 + face, :, half * LANES : (half + 1) * LANES]

    y = (lane & 15) + offset
    z = (lane >> 4) + offset
    at_low = lane & 15 == 0
    across_y = jnp.concatenate([pick(strip(2), y), pick(strip(3), y)], axis=1)
    z_low, z_high = (strip(4), strip(5))
    across_z = jnp.concatenate(
        [
            jnp.where(at_low, pick(z_low, z), pick(z_high, z)),
            jnp.where(at_low, pick(z_low, z + 8), pick(z_high, z + 8)),
        ],
        axis=1,
    )
    totals = [
        across_z_ref[o, :, place].astype(jnp.float32) * across_z
        + across_y_ref[o, :, place].astype(jnp.float32) * across_y
        for o in range(VARS)
    ]
    return part_ref[:, place] + fold(totals + [jnp.zeros((8, SQUARE), jnp.float32)])


def outer_x(across_x_ref, halos, block, side):
    halo = halos[block * 6 + side]
    totals = [across_x_ref[block * 2 + side, o].astype(jnp.float32) * halo for o in range(VARS)]
    return fold(totals + [jnp.zeros((8, SQUARE), jnp.float32)])


def outer_block(across_x_ref, part_ref, across_z_ref, across_y_ref, halos, block, put):
    for half in range(2):
        for inner in range(8):
            slab = outer_slab(part_ref, across_z_ref, across_y_ref, halos, block, half, inner)
            if half == 0 and inner == 0:
                slab = slab + outer_x(across_x_ref, halos, block, 0)
            if half == 1 and inner == 7:
                slab = slab + outer_x(across_x_ref, halos, block, 1)
            put(block * EDGE + half * 8 + inner, slab)


def flux_kernel(
    table_ref, own_ref, swapped_ref, part_ref, across_z_ref, across_y_ref, across_x_ref, token_ref, mixed_ref,
    first_ref, faces_ref, halos
):
    fetch_halos(table_ref, own_ref, swapped_ref, halos)

    def put(k, slab):
        first_ref[:, k * SQUARE : (k + 1) * SQUARE] = slab

    for block in range(PER):
        outer_block(across_x_ref, part_ref, across_z_ref, across_y_ref, halos, block, put)
        collect_block(first_ref, faces_ref, block)


def mix_kernel(own_ref, one_ref, two_ref, three_ref, kept_ref, given_ref, token_ref):
    z = lax.axis_index("z")
    xl = lax.axis_index("xl")
    table = mixing_weights()

    def weight(offset):
        offset = lax.rem(offset + 2 * INST, INST)
        value = jnp.float32(table[0])
        for k in range(1, INST):
            value = jnp.where(offset == k, jnp.float32(table[k]), value)
        return value

    fields = (own_ref, one_ref, two_ref, three_ref)
    sources = [2 * (z ^ k) + xl for k in range(4)]
    kept = [weight(source - (2 * z + xl)) for source in sources]
    given = [weight(source - (2 * z + 1 - xl)) for source in sources]

    def step(k, carry):
        rows = pl.ds(pl.multiple_of(k * 64, 64), 64)
        values = [field[rows] for field in fields]
        kept_ref[rows] = sum(w * v for w, v in zip(kept, values))
        given_ref[rows] = sum(w * v for w, v in zip(given, values))
        return carry

    lax.fori_loop(0, ROWS // 64, step, 0)
    token_ref[...] = jnp.zeros_like(token_ref)


def lane_sums(rows, first_lane):
    totals = jnp.broadcast_to(jnp.sum(rows, axis=1, keepdims=True), rows.shape)
    spot = lanes(rows.shape) == sublanes(rows.shape) + first_lane
    return jnp.sum(jnp.where(spot, totals, 0.0), axis=0, keepdims=True)


def gram_kernel(flat_ref, gram_ref, basis_ref, lines, arrived):
    copy = pltpu.make_async_copy(flat_ref, basis_ref, arrived)
    copy.start()
    copy.wait()

    def step(k, totals):
        fields = [
            basis_ref[pl.ds(pl.multiple_of(j * ROWS + k * 8, 8), 8)] for j in range(KRYLOV)
        ]
        out = []
        for i in range(KRYLOV):
            for j in range(i, KRYLOV):
                out.append(totals[len(out)] + fields[i] * fields[j])
        return tuple(out)

    zero = jnp.zeros((8, LANES), jnp.float32)
    totals = lax.fori_loop(0, ROWS // 8, step, (zero,) * (KRYLOV * (KRYLOV + 1) // 2))
    number = 0
    for i in range(KRYLOV):
        for j in range(i, KRYLOV):
            line = jnp.sum(totals[number], axis=0, keepdims=True)
            lines[i * KRYLOV + j : i * KRYLOV + j + 1] = line
            lines[j * KRYLOV + i : j * KRYLOV + i + 1] = line
            number += 1
    gram_ref[...] = jnp.broadcast_to(lane_sums(lines[...], 64), (8, LANES))


def image_kernel(
    later_ref, one_ref, two_ref, three_ref, four_ref, chip_ref, swapped_ref,
    part_ref, across_z_ref, across_y_ref, across_x_ref,
    flat_ref, pseudo_ref, omega_ref, kept_ref, returned_ref, gram_ref,
    image_ref, sums_ref, basis_ref, halos, section, arrived
):
    copy = pltpu.make_async_copy(flat_ref, basis_ref, arrived)
    copy.start()
    fetch_later_halos(later_ref, (one_ref, two_ref, three_ref, four_ref, chip_ref), swapped_ref, halos)

    def put(k, slab):
        section[pl.ds(2 * k, 8, stride=GROUPS), :] = slab[:, :LANES]
        section[pl.ds(2 * k + 1, 8, stride=GROUPS), :] = slab[:, LANES:]

    for block in range(PER):
        outer_block(across_x_ref, part_ref, across_z_ref, across_y_ref, halos, block, put)
    copy.wait()

    def step(k, totals):
        start = k * 8
        cells = pl.ds(pl.multiple_of(start % GROUPS, 8), 8)
        rows = pl.ds(pl.multiple_of(start, 8), 8)
        fields = [basis_ref[pl.ds(pl.multiple_of(j * ROWS + start, 8), 8)] for j in range(KRYLOV)]
        spectral = kept_ref[rows] + returned_ref[rows]
        image = pseudo_ref[cells] * fields[KRYLOV - 1] + section[rows] + omega_ref[cells] * spectral
        image_ref[rows] = image
        return tuple(total + field * image for total, field in zip(totals, fields + [image]))

    zero = jnp.zeros((8, LANES), jnp.float32)
    totals = lax.fori_loop(0, ROWS // 8, step, (zero,) * (KRYLOV + 1), unroll=8)
    lines = [jnp.sum(total, axis=0, keepdims=True) for total in totals]
    lines += [jnp.zeros((16 - len(lines), LANES), jnp.float32)]
    sums = jnp.broadcast_to(lane_sums(jnp.concatenate(lines, axis=0), 0), (8, LANES)) + gram_ref[...]
    for group in range(16):
        sums_ref[group * 8 : group * 8 + 8] = sums


def finish_kernel(received_ref, image_ref, basis_ref, next_ref, column_ref, flag_ref, column_held, sent):
    sums = jnp.sum(received_ref[...], axis=0, keepdims=True)
    sums = jnp.broadcast_to(sums, (8, LANES)) / ENTRIES
    lane = lanes((8, LANES))
    left = pick(sums, jnp.maximum(lane - 64, 0) // 8)
    right = pick(sums, lane % 8)
    quadratic = jnp.sum(jnp.where(lane >= 64, sums * left * right, 0.0), axis=1, keepdims=True)
    linear = jnp.sum(jnp.where(lane < KRYLOV, sums * sums, 0.0), axis=1, keepdims=True)
    whole_square = sums[:, KRYLOV : KRYLOV + 1]
    squares = whole_square - 2.0 * linear + quadratic
    size = whole_square + 2.0 * linear + jnp.abs(quadratic)
    norm = jnp.sqrt(jnp.maximum(squares, 0.0) + 1e-06)
    column = jnp.where(lane < KRYLOV, sums, jnp.where(lane == KRYLOV, norm, 0.0))
    column_held[...] = column[:1, : KRYLOV + 1]
    copy = pltpu.make_async_copy(column_held, column_ref, sent)
    copy.start()
    flag_ref[0] = jnp.sum(jnp.where(squares[:1] < GUARD * size[:1], 1.0, 0.0)).astype(jnp.int32)
    coeffs = [jnp.broadcast_to(sums[:, j : j + 1], (8, LANES)) for j in range(KRYLOV)]
    scale = jnp.broadcast_to(1.0 / norm, (8, LANES))

    def step(k, carry):
        start = k * 8
        rows = pl.ds(pl.multiple_of(start, 8), 8)
        ortho = image_ref[rows]
        for j in range(KRYLOV):
            ortho = ortho - coeffs[j] * basis_ref[pl.ds(pl.multiple_of(j * ROWS + start, 8), 8)]
        next_ref[rows] = ortho * scale
        return carry

    lax.fori_loop(0, ROWS // 8, step, 0, unroll=8)
    copy.wait()


def whole(memory=VMEM):
    return pl.BlockSpec(memory_space=memory)


def f32(*shape):
    return jax.ShapeDtypeStruct(shape, jnp.float32)


def bf16(*shape):
    return jax.ShapeDtypeStruct(shape, jnp.bfloat16)


def params(mib):
    return pltpu.CompilerParams(vmem_limit_bytes=mib * 2**20)


def cost(flops, moved):
    return pl.CostEstimate(flops=flops, bytes_accessed=moved, transcendentals=0)


def swap(size, bit):
    return [(i, i ^ bit) for i in range(size)]


def exchange(sent):
    return lax.all_to_all(sent, CHIPS, 0, 0)


def after(value, others):
    return lax.optimization_barrier((value, others))


def split_pairs(first, second):
    pairs = []
    for chip in range(CHIP_COUNT):
        pairs.append((chip * 2, (chip ^ first) * 2))
        pairs.append((chip * 2 + 1, (chip ^ second) * 2 + 1))
    return pairs


def second_exchange(faces):
    space = ("xh", "y", "core")
    chip = jnp.concatenate([faces, swap_cores(faces)])
    return (
        lax.ppermute(chip, space, split_pairs(1, 3)),
        lax.ppermute(chip, space, split_pairs(2, 4)),
        lax.ppermute(chip, space, split_pairs(5, 7)),
        lax.ppermute(faces, space, split_pairs(6, 6)),
        chip,
    )


def swap_cores(own):
    return lax.ppermute(own, "core", swap(2, 1))


FACES_VMEM = VMEM((FACES, 8, SQUARE), jnp.float32)
SENT = f32(CHIP_COUNT, FACES, 8, SQUARE)


def inner_section(field, coeff, name, flops):
    chunks = SLABS // CHUNK
    return pl.pallas_call(
        inner_kernel,
        in_specs=[whole(), whole(pltpu.HBM)],
        out_specs=[whole()] * 5,
        out_shape=[
            f32(8, CELLS), bf16(VARS, 8, CELLS), bf16(VARS, 8, CELLS), bf16(2 * PER, VARS, 8, SQUARE), f32(8, LANES),
        ],
        scratch_shapes=[
            VMEM((chunks, 7, VARS, VARS, CHUNK * SQUARE), jnp.bfloat16),
            pltpu.SemaphoreType.DMA((chunks,)),
        ],
        compiler_params=params(INNER_MIB),
        cost_estimate=cost(flops, 8 * 2**20),
        name=name,
    )(field, coeff)


def mix(parts):
    return pl.pallas_call(
        mix_kernel,
        in_specs=[whole()] * 4,
        out_specs=[whole()] * 3,
        out_shape=[f32(ROWS, LANES), f32(ROWS, LANES), f32(8, LANES)],
        compiler_params=params(8),
        cost_estimate=cost(MIX, 6 * 4 * ROWS * LANES),
        name="mix",
    )(*parts)


def local(basis, flux, recon, pseudo_time, vol_omega, block_ids, neighbour, orient):
    flat = basis.reshape(KRYLOV * ROWS, LANES)
    sent, padded, dense = pl.pallas_call(
        first_faces_kernel,
        in_specs=[whole(pl.ANY)],
        out_specs=[whole(pl.ANY), whole(), whole()],
        out_shape=[SENT, f32(8, CELLS), f32(ROWS, LANES)],
        scratch_shapes=[VMEM((8 * GROUPS, LANES), jnp.float32), FACES_VMEM, pltpu.SemaphoreType.DMA((PER, CHIP_COUNT))],
        compiler_params=params(8),
        cost_estimate=cost(10**6, 2 * 2**20),
        name="first_faces",
    )(flat)
    own = exchange(sent)
    table, later = pl.pallas_call(
        tables_kernel,
        in_specs=[whole(SMEM)] * 3,
        out_specs=[whole(SMEM), whole(SMEM)],
        out_shape=[
            jax.ShapeDtypeStruct((4 * FACES,), jnp.int32),
            jax.ShapeDtypeStruct((8 * FACES,), jnp.int32),
        ],
        scratch_shapes=[SMEM((BLOCKS,), jnp.int32)],
        compiler_params=params(4),
        cost_estimate=cost(10**5, 10**5),
        name="tables",
    )(block_ids, neighbour.T, orient.T)
    *pieces, token = inner_section(padded, flux, "flux_inner", FLUX_INNER)
    gram = pl.pallas_call(
        gram_kernel,
        in_specs=[whole(pl.ANY)],
        out_specs=whole(),
        out_shape=f32(8, LANES),
        scratch_shapes=[
            VMEM((KRYLOV * ROWS, LANES), jnp.float32),
            VMEM((KRYLOV * KRYLOV, LANES), jnp.float32),
            pltpu.SemaphoreType.DMA,
        ],
        compiler_params=params(8),
        cost_estimate=cost(2 * 36 * VARS * CELLS, 2 * 2**20),
        name="gram",
    )(flat)
    kept, given, mixed = mix([dense] + [lax.ppermute(dense, "z", swap(4, k)) for k in (1, 2, 3)])
    own, (token, table, mixed, gram) = after(own, (token, table, mixed, gram))
    swapped = swap_cores(own)
    first, faces = pl.pallas_call(
        flux_kernel,
        in_specs=[whole(SMEM)] + [whole()] * 6 + [whole(pl.ANY)] * 2,
        out_specs=[whole(), whole()],
        out_shape=[f32(8, CELLS), f32(FACES, 8, SQUARE)],
        scratch_shapes=[FACES_VMEM],
        compiler_params=params(OUTER_MIB),
        cost_estimate=cost(FLUX_OUTER, 4 * 2**20),
        name="flux_outer",
    )(table, own, swapped, *pieces, token, mixed)
    returned = lax.ppermute(given, "xl", swap(2, 1))
    *pieces, token = inner_section(first, recon, "recon_inner", RECON_INNER)
    parts = second_exchange(faces)
    wanted = pl.pallas_call(
        select_kernel,
        in_specs=[whole(SMEM)] + [whole()] * 5 + [whole(pl.ANY)],
        out_specs=whole(),
        out_shape=f32(FACES, 8, SQUARE),
        compiler_params=params(4),
        cost_estimate=cost(10**5, 10**6),
        name="select",
    )(later, *parts, token)
    swapped = swap_cores(wanted)
    image, sums, held = pl.pallas_call(
        image_kernel,
        in_specs=[whole(SMEM)] + [whole()] * 10 + [whole(pl.ANY)] + [whole()] * 5,
        out_specs=[whole(), whole(), whole()],
        out_shape=[f32(ROWS, LANES), f32(LANES, LANES), f32(KRYLOV * ROWS, LANES)],
        scratch_shapes=[FACES_VMEM, VMEM((8 * GROUPS, LANES), jnp.float32), pltpu.SemaphoreType.DMA],
        compiler_params=params(OUTER_MIB),
        cost_estimate=cost(10**6, 6 * 2**20),
        name="image",
    )(
        later, *parts, swapped, *pieces,
        flat, pseudo_time.reshape(GROUPS, LANES), vol_omega.reshape(GROUPS, LANES), kept, returned, gram,
    )
    received = lax.all_to_all(sums, ALL, 0, 0)
    following, column, flag = pl.pallas_call(
        finish_kernel,
        in_specs=[whole()] * 3,
        out_specs=[whole(), whole(pl.ANY), whole(SMEM)],
        out_shape=[f32(ROWS, LANES), f32(1, KRYLOV + 1), jax.ShapeDtypeStruct((1,), jnp.int32)],
        scratch_shapes=[VMEM((1, KRYLOV + 1), jnp.float32), pltpu.SemaphoreType.DMA],
        compiler_params=params(8),
        cost_estimate=cost(10**6, 3 * 2**20),
        name="finish",
    )(received, image, held)

    def direct(state):
        coeffs = state[1][0, :KRYLOV]
        ortho = image - jnp.einsum(
            "k,krl->rl", coeffs, flat.reshape(KRYLOV, ROWS, LANES), precision=lax.Precision.HIGHEST
        )
        squares = lax.psum(jnp.sum(ortho * ortho), ALL) / ENTRIES
        norm = jnp.sqrt(squares + 1e-06)
        return (ortho / norm, jnp.concatenate([coeffs, norm[None]])[None], jnp.zeros((), jnp.int32))

    following, column, _ = lax.while_loop(
        lambda state: state[2] > 0, direct, (following, column, flag[0])
    )
    return following.reshape(1, VARS, CELLS), column[0]


def solution(mesh):
    fine = Mesh(mesh.devices.reshape(4, 2, 2, 4, 2), ALL)
    inst, space = (("z", "xl"), ("xh", "y", "core"))
    placed = (
        P(None, inst, None, space),
        P(inst, None, None, None, space),
        P(inst, None, None, None, space),
        P(space),
        P(space),
        P(),
        P(),
        P(),
    )
    return jax.shard_map(
        local,
        mesh=fine,
        in_specs=placed,
        out_specs=(P(inst, None, space), P()),
        check_vma=False,
    )
```

```python
import jax
import jax.numpy as jnp
import numpy as np
from jax import lax
from jax.experimental import pallas as pl
from jax.experimental.pallas import tpu as pltpu
from jax.sharding import Mesh, PartitionSpec as P

EDGE = 16
SQUARE = EDGE * EDGE
CUBE = EDGE * SQUARE
VARS = 7
KRYLOV = 8
INST = 8
BLOCKS = 32
SPACE = 16
CHIP_COUNT = 8
CELLS = 8192
PER = CELLS // CUBE
FACES = 6 * PER
SLABS = CELLS // SQUARE
ENTRIES = float(INST * VARS * CELLS * SPACE)
LANES = 128
GROUPS = CELLS // LANES
ROWS = VARS * GROUPS
ALL = ("z", "xl", "xh", "y", "core")
CHIPS = ("xh", "y")
VMEM = pltpu.VMEM
SMEM = pltpu.SMEM
GUARD = 0.02
CHUNK = 4
FLUX_INNER = 10**6
INNER_MIB = 46
OUTER_MIB = 16
MIX = 10**6
FLUX_OUTER = 10**6
RECON_INNER = 2 * 10**10


def mixing_weights():
    k = np.arange(1, INST)
    parity = np.where(k % 2 == 0, 1.0, -1.0)
    angle = np.pi * k / INST
    rest = 0.5 * parity / np.tan(angle) - 0.125 * parity / np.sin(angle) ** 2
    return [-0.25 * (INST * INST + 2) / 12.0] + [float(v) for v in rest]


def lanes(shape):
    return lax.broadcasted_iota(jnp.int32, shape, len(shape) - 1)


def sublanes(shape):
    return lax.broadcasted_iota(jnp.int32, shape, len(shape) - 2)


def pick(values, index):
    return jnp.take_along_axis(values, index, axis=1)


def fold(totals):
    row = sublanes(totals[0].shape)
    for width in (1, 2, 4):
        first = row % (2 * width) < width
        totals = [
            jnp.where(first, a, b) + pltpu.roll(jnp.where(first, b, a), width, 0)
            for a, b in zip(totals[::2], totals[1::2])
        ]
    return totals[0]


def strips_of(slab, x, strips):
    lane = lanes((8, LANES))
    low, high = (slab[:, :LANES], slab[:, LANES:])
    own = lane >> 4 == x
    upper = lane & 8 != 0
    z = lane & 15
    source = (lane & 7) << 4
    found = (
        pick(low, z),
        pick(high, z + (LANES - EDGE)),
        jnp.where(upper, pick(high, source), pick(low, source)),
        jnp.where(upper, pick(high, source + 15), pick(low, source + 15)),
    )
    if strips is None:
        return list(found)
    return [jnp.where(own, new, old) for new, old in zip(found, strips)]


def collect_block(field_ref, faces, block):
    start = block * CUBE
    faces[block * 6] = field_ref[:, start : start + SQUARE]
    faces[block * 6 + 1] = field_ref[:, start + CUBE - SQUARE : start + CUBE]
    for half in range(2):
        strips = None
        for inner in range(8):
            place = start + (half * 8 + inner) * SQUARE
            strips = strips_of(field_ref[:, place : place + SQUARE], inner, strips)
        for number, strip in enumerate(strips):
            faces[block * 6 + 2 + number, :, half * LANES : (half + 1) * LANES] = strip


def send_block(faces, sent_ref, arrived, block):
    rows = pl.ds(block * 6, 6)
    copies = [
        pltpu.make_async_copy(faces.at[rows], sent_ref.at[chip, rows], arrived.at[block, chip])
        for chip in range(CHIP_COUNT)
    ]
    for copy in copies:
        copy.start()
    return copies


def first_faces_kernel(basis_ref, sent_ref, padded_ref, dense_ref, field, faces, arrived):
    fetch = pltpu.make_async_copy(
        basis_ref.at[pl.ds((KRYLOV - 1) * ROWS, ROWS)], field.at[pl.ds(0, ROWS)], arrived.at[0, 0]
    )
    fetch.start()
    field[ROWS:] = jnp.zeros((GROUPS, LANES), jnp.float32)
    fetch.wait()
    copies = []
    for block in range(PER):
        for group in range(block * 32, block * 32 + 32):
            padded_ref[:, group * LANES : (group + 1) * LANES] = field[pl.ds(group, 8, stride=GROUPS), :]
        collect_block(padded_ref, faces, block)
        copies += send_block(faces, sent_ref, arrived, block)
    dense_ref[...] = field[:ROWS]
    for copy in copies:
        copy.wait()


PART_OF = (4, 0, 1, 0, 1, 2, 3, 2)
CORE_OF = (0, 0, 0, 1, 1, 0, 0, 1)


def tables_kernel(ids_ref, neighbour_ref, orient_ref, table_ref, later_ref, position):
    core = lax.axis_index("core")
    chip = lax.axis_index("xh") * 4 + lax.axis_index("y")

    def place(slot, carry):
        position[ids_ref[slot]] = slot
        return carry

    lax.fori_loop(0, BLOCKS, place, 0)

    def pick_of(values, index):
        result = jnp.int32(values[0])
        for k in range(1, len(values)):
            result = jnp.where(index == k, jnp.int32(values[k]), result)
        return result

    for mine in (True, False):
        for number in range(FACES):
            rank = chip * 2 + (core if mine else 1 - core)
            owner = ids_ref[rank * PER + number // 6]
            partner = neighbour_ref[number % 6, owner]
            target = jnp.maximum(partner, 0)
            slot = position[target // 6]
            device = slot // PER
            row = (slot % PER) * 6 + target % 6
            source_core = device % 2
            offset = (device // 2) ^ chip
            part = pick_of(PART_OF, offset)
            among = jnp.where(source_core == core, row, row + FACES)
            if mine:
                code = jnp.where(partner < 0, -1, orient_ref[number % 6, owner])
                same = source_core == core
                table_ref[number * 4] = device // 2
                table_ref[number * 4 + 1] = jnp.where(same, 1, 0)
                table_ref[number * 4 + 2] = row
                table_ref[number * 4 + 3] = code
                here = jnp.where(
                    part == 4, True, jnp.where(part == 3, jnp.logical_not(same), pick_of(CORE_OF, offset) == core)
                )
                later_ref[number * 5] = part
                later_ref[number * 5 + 1] = among
                later_ref[number * 5 + 2] = row
                later_ref[number * 5 + 3] = jnp.where(here, 1, 0)
                later_ref[number * 5 + 4] = code
            else:
                table_ref[4 * FACES + number * 2] = device // 2
                table_ref[4 * FACES + number * 2 + 1] = row
                later_ref[5 * FACES + number * 3] = part
                later_ref[5 * FACES + number * 3 + 1] = among
                later_ref[5 * FACES + number * 3 + 2] = row


def choose(parts, part, among, row):
    value = parts[4][among]
    for k in range(3):
        value = jnp.where(part == k, parts[k][among], value)
    return jnp.where(part == 3, parts[3][row], value)


def select_kernel(
    later_ref, one_ref, two_ref, three_ref, four_ref, chip_ref, token_ref, wanted_ref
):
    parts = (one_ref, two_ref, three_ref, four_ref, chip_ref)
    for number in range(FACES):
        base = 5 * FACES + number * 3
        wanted_ref[number] = choose(parts, later_ref[base], later_ref[base + 1], later_ref[base + 2])


def select_near_kernel(table_ref, own_ref, token_ref, gram_ref, wanted_ref):
    for number in range(FACES):
        base = 4 * FACES + number * 2
        wanted_ref[number] = own_ref[table_ref[base], table_ref[base + 1]]


def turn_face(source, code, halos, number):
    lane = lanes((8, LANES))
    source = jnp.where(code < 0, 0.0, source)
    code = jnp.maximum(code, 0)
    low, high = (source[:, :LANES], source[:, LANES:])
    transposed = code & 1 == 1
    flip_a = (code >> 1 & 1) * (EDGE - 1)
    flip_b = (code >> 2) * (EDGE - 1)
    for half in range(2):
        a = ((lane >> 4) + half * 8) ^ flip_a
        b = (lane & 15) ^ flip_b
        index = jnp.where(transposed, (b << 4) + a, (a << 4) + b)
        inside = index & (LANES - 1)
        halos[number, :, half * LANES : (half + 1) * LANES] = jnp.where(
            index < LANES, pick(low, inside), pick(high, inside)
        )


def fetch_halos(table_ref, own_ref, swapped_ref, halos):
    for number in range(FACES):
        chip = table_ref[number * 4]
        here = table_ref[number * 4 + 1] == 1
        row = table_ref[number * 4 + 2]
        source = jnp.where(here, own_ref[chip, row], swapped_ref[number])
        turn_face(source, table_ref[number * 4 + 3], halos, number)


def fetch_later_halos(later_ref, parts, swapped_ref, halos):
    for number in range(FACES):
        base = number * 5
        source = choose(parts, later_ref[base], later_ref[base + 1], later_ref[base + 2])
        source = jnp.where(later_ref[base + 3] == 1, source, swapped_ref[number])
        turn_face(source, later_ref[base + 4], halos, number)


def inner_kernel(
    field_ref, coeff_ref, part_ref, across_z_ref, across_y_ref, across_x_ref, token_ref, held, arrived
):
    column = lanes((8, SQUARE))
    z = column & 15
    width = CHUNK * SQUARE
    chunks = SLABS // CHUNK
    copies = [
        pltpu.make_async_copy(coeff_ref.at[0, :, :, :, pl.ds(i * width, width)], held.at[i], arrived.at[i])
        for i in range(chunks)
    ]
    for copy in copies:
        copy.start()

    def load(k):
        return field_ref[:, pl.ds(pl.multiple_of(k * SQUARE, SQUARE), SQUARE)]

    def chunk_step(chunk, carry):
        pltpu.make_async_copy(
            coeff_ref.at[0, :, :, :, pl.ds(0, width)], held.at[chunk], arrived.at[chunk]
        ).wait()
        for inner in range(CHUNK):

            def coeff(s, o):
                value = held[chunk, s, o, :, inner * SQUARE : (inner + 1) * SQUARE].astype(jnp.float32)
                return jnp.concatenate([value, jnp.zeros((1, SQUARE), jnp.float32)], axis=0)

            k = chunk * CHUNK + inner
            block, x = (k // EDGE, k % EDGE)
            place = pl.ds(pl.multiple_of(k * SQUARE, SQUARE), SQUARE)
            centre = load(k)
            below, above = (load(jnp.maximum(k - 1, 0)), load(jnp.minimum(k + 1, SLABS - 1)))
            if inner == 0:
                below = jnp.where(x == 0, 0.0, below)
            if inner == CHUNK - 1:
                above = jnp.where(x == EDGE - 1, 0.0, above)
            operands = [
                centre,
                below,
                above,
                jnp.where(column < EDGE, 0.0, pltpu.roll(centre, EDGE, 1)),
                jnp.where(column >= SQUARE - EDGE, 0.0, pltpu.roll(centre, SQUARE - EDGE, 1)),
                jnp.where(z == 0, 0.0, pltpu.roll(centre, 1, 1)),
                jnp.where(z == EDGE - 1, 0.0, pltpu.roll(centre, SQUARE - 1, 1)),
            ]
            totals = []
            for o in range(VARS):
                values = [coeff(s, o) for s in range(7)]
                total = values[0] * operands[0]
                for s in range(1, 7):
                    total = total + values[s] * operands[s]
                totals.append(total)
                across_z_ref[o, :, place] = jnp.where(
                    z == 0, values[5], jnp.where(z == EDGE - 1, values[6], 0.0)
                ).astype(jnp.bfloat16)
                across_y_ref[o, :, place] = jnp.where(
                    column < EDGE, values[3], jnp.where(column >= SQUARE - EDGE, values[4], 0.0)
                ).astype(jnp.bfloat16)
            part_ref[:, place] = fold(totals + [jnp.zeros((8, SQUARE), jnp.float32)])

            if inner == 0:

                @pl.when(x == 0)
                def _():
                    for o in range(VARS):
                        across_x_ref[block * 2, o] = coeff(1, o).astype(jnp.bfloat16)

            if inner == CHUNK - 1:

                @pl.when(x == EDGE - 1)
                def _():
                    for o in range(VARS):
                        across_x_ref[block * 2 + 1, o] = coeff(2, o).astype(jnp.bfloat16)

        return carry

    lax.fori_loop(0, chunks, chunk_step, 0)
    token_ref[...] = jnp.zeros_like(token_ref)


def outer_slab(part_ref, across_z_ref, across_y_ref, halos, block, half, inner):
    lane = lanes((8, LANES))
    offset = inner * EDGE
    start = block * CUBE + (half * 8 + inner) * SQUARE
    place = slice(start, start + SQUARE)

    def strip(face):
        return halos[block * 6 + face, :, half * LANES : (half + 1) * LANES]

    y = (lane & 15) + offset
    z = (lane >> 4) + offset
    at_low = lane & 15 == 0
    across_y = jnp.concatenate([pick(strip(2), y), pick(strip(3), y)], axis=1)
    z_low, z_high = (strip(4), strip(5))
    across_z = jnp.concatenate(
        [
            jnp.where(at_low, pick(z_low, z), pick(z_high, z)),
            jnp.where(at_low, pick(z_low, z + 8), pick(z_high, z + 8)),
        ],
        axis=1,
    )
    totals = [
        across_z_ref[o, :, place].astype(jnp.float32) * across_z
        + across_y_ref[o, :, place].astype(jnp.float32) * across_y
        for o in range(VARS)
    ]
    return part_ref[:, place] + fold(totals + [jnp.zeros((8, SQUARE), jnp.float32)])


def outer_x(across_x_ref, halos, block, side):
    halo = halos[block * 6 + side]
    totals = [across_x_ref[block * 2 + side, o].astype(jnp.float32) * halo for o in range(VARS)]
    return fold(totals + [jnp.zeros((8, SQUARE), jnp.float32)])


def outer_block(across_x_ref, part_ref, across_z_ref, across_y_ref, halos, block, put):
    for half in range(2):
        for inner in range(8):
            slab = outer_slab(part_ref, across_z_ref, across_y_ref, halos, block, half, inner)
            if half == 0 and inner == 0:
                slab = slab + outer_x(across_x_ref, halos, block, 0)
            if half == 1 and inner == 7:
                slab = slab + outer_x(across_x_ref, halos, block, 1)
            put(block * EDGE + half * 8 + inner, slab)


def flux_kernel(
    table_ref, own_ref, swapped_ref, part_ref, across_z_ref, across_y_ref, across_x_ref, mixed_ref,
    first_ref, faces_ref, halos
):
    fetch_halos(table_ref, own_ref, swapped_ref, halos)

    def put(k, slab):
        first_ref[:, k * SQUARE : (k + 1) * SQUARE] = slab

    for block in range(PER):
        outer_block(across_x_ref, part_ref, across_z_ref, across_y_ref, halos, block, put)
        collect_block(first_ref, faces_ref, block)


def mix_kernel(own_ref, one_ref, two_ref, three_ref, kept_ref, given_ref, token_ref):
    z = lax.axis_index("z")
    xl = lax.axis_index("xl")
    table = mixing_weights()

    def weight(offset):
        offset = lax.rem(offset + 2 * INST, INST)
        value = jnp.float32(table[0])
        for k in range(1, INST):
            value = jnp.where(offset == k, jnp.float32(table[k]), value)
        return value

    fields = (own_ref, one_ref, two_ref, three_ref)
    sources = [2 * (z ^ k) + xl for k in range(4)]
    kept = [weight(source - (2 * z + xl)) for source in sources]
    given = [weight(source - (2 * z + 1 - xl)) for source in sources]

    def step(k, carry):
        rows = pl.ds(pl.multiple_of(k * 64, 64), 64)
        values = [field[rows] for field in fields]
        kept_ref[rows] = sum(w * v for w, v in zip(kept, values))
        given_ref[rows] = sum(w * v for w, v in zip(given, values))
        return carry

    lax.fori_loop(0, ROWS // 64, step, 0)
    token_ref[...] = jnp.zeros_like(token_ref)


def lane_sums(rows, first_lane):
    totals = jnp.broadcast_to(jnp.sum(rows, axis=1, keepdims=True), rows.shape)
    spot = lanes(rows.shape) == sublanes(rows.shape) + first_lane
    return jnp.sum(jnp.where(spot, totals, 0.0), axis=0, keepdims=True)


def gram_kernel(flat_ref, gram_ref, basis_ref, lines, arrived):
    copy = pltpu.make_async_copy(flat_ref, basis_ref, arrived)
    copy.start()
    copy.wait()

    def step(k, totals):
        fields = [
            basis_ref[pl.ds(pl.multiple_of(j * ROWS + k * 8, 8), 8)] for j in range(KRYLOV)
        ]
        out = []
        for i in range(KRYLOV):
            for j in range(i, KRYLOV):
                out.append(totals[len(out)] + fields[i] * fields[j])
        return tuple(out)

    zero = jnp.zeros((8, LANES), jnp.float32)
    totals = lax.fori_loop(0, ROWS // 8, step, (zero,) * (KRYLOV * (KRYLOV + 1) // 2))
    number = 0
    for i in range(KRYLOV):
        for j in range(i, KRYLOV):
            line = jnp.sum(totals[number], axis=0, keepdims=True)
            lines[i * KRYLOV + j : i * KRYLOV + j + 1] = line
            lines[j * KRYLOV + i : j * KRYLOV + i + 1] = line
            number += 1
    gram_ref[...] = jnp.broadcast_to(lane_sums(lines[...], 64), (8, LANES))


def image_kernel(
    later_ref, one_ref, two_ref, three_ref, four_ref, chip_ref, swapped_ref,
    part_ref, across_z_ref, across_y_ref, across_x_ref,
    flat_ref, pseudo_ref, omega_ref, kept_ref, returned_ref, gram_ref,
    image_ref, sums_ref, basis_ref, halos, section, arrived
):
    copy = pltpu.make_async_copy(flat_ref, basis_ref, arrived)
    copy.start()
    fetch_later_halos(later_ref, (one_ref, two_ref, three_ref, four_ref, chip_ref), swapped_ref, halos)

    def put(k, slab):
        section[pl.ds(2 * k, 8, stride=GROUPS), :] = slab[:, :LANES]
        section[pl.ds(2 * k + 1, 8, stride=GROUPS), :] = slab[:, LANES:]

    for block in range(PER):
        outer_block(across_x_ref, part_ref, across_z_ref, across_y_ref, halos, block, put)
    copy.wait()

    def step(k, totals):
        start = k * 8
        cells = pl.ds(pl.multiple_of(start % GROUPS, 8), 8)
        rows = pl.ds(pl.multiple_of(start, 8), 8)
        fields = [basis_ref[pl.ds(pl.multiple_of(j * ROWS + start, 8), 8)] for j in range(KRYLOV)]
        spectral = kept_ref[rows] + returned_ref[rows]
        image = pseudo_ref[cells] * fields[KRYLOV - 1] + section[rows] + omega_ref[cells] * spectral
        image_ref[rows] = image
        return tuple(total + field * image for total, field in zip(totals, fields + [image]))

    zero = jnp.zeros((8, LANES), jnp.float32)
    totals = lax.fori_loop(0, ROWS // 8, step, (zero,) * (KRYLOV + 1), unroll=8)
    lines = [jnp.sum(total, axis=0, keepdims=True) for total in totals]
    lines += [jnp.zeros((16 - len(lines), LANES), jnp.float32)]
    sums = jnp.broadcast_to(lane_sums(jnp.concatenate(lines, axis=0), 0), (8, LANES)) + gram_ref[...]
    for group in range(16):
        sums_ref[group * 8 : group * 8 + 8] = sums


def finish_kernel(received_ref, image_ref, basis_ref, next_ref, column_ref, flag_ref, column_held, sent):
    sums = jnp.sum(received_ref[...], axis=0, keepdims=True)
    sums = jnp.broadcast_to(sums, (8, LANES)) / ENTRIES
    lane = lanes((8, LANES))
    left = pick(sums, jnp.maximum(lane - 64, 0) // 8)
    right = pick(sums, lane % 8)
    quadratic = jnp.sum(jnp.where(lane >= 64, sums * left * right, 0.0), axis=1, keepdims=True)
    linear = jnp.sum(jnp.where(lane < KRYLOV, sums * sums, 0.0), axis=1, keepdims=True)
    whole_square = sums[:, KRYLOV : KRYLOV + 1]
    squares = whole_square - 2.0 * linear + quadratic
    size = whole_square + 2.0 * linear + jnp.abs(quadratic)
    norm = jnp.sqrt(jnp.maximum(squares, 0.0) + 1e-06)
    column = jnp.where(lane < KRYLOV, sums, jnp.where(lane == KRYLOV, norm, 0.0))
    column_held[...] = column[:1, : KRYLOV + 1]
    copy = pltpu.make_async_copy(column_held, column_ref, sent)
    copy.start()
    flag_ref[0] = jnp.sum(jnp.where(squares[:1] < GUARD * size[:1], 1.0, 0.0)).astype(jnp.int32)
    coeffs = [jnp.broadcast_to(sums[:, j : j + 1], (8, LANES)) for j in range(KRYLOV)]
    scale = jnp.broadcast_to(1.0 / norm, (8, LANES))

    def step(k, carry):
        start = k * 8
        rows = pl.ds(pl.multiple_of(start, 8), 8)
        ortho = image_ref[rows]
        for j in range(KRYLOV):
            ortho = ortho - coeffs[j] * basis_ref[pl.ds(pl.multiple_of(j * ROWS + start, 8), 8)]
        next_ref[rows] = ortho * scale
        return carry

    lax.fori_loop(0, ROWS // 8, step, 0, unroll=8)
    copy.wait()


def whole(memory=VMEM):
    return pl.BlockSpec(memory_space=memory)


def f32(*shape):
    return jax.ShapeDtypeStruct(shape, jnp.float32)


def bf16(*shape):
    return jax.ShapeDtypeStruct(shape, jnp.bfloat16)


def params(mib):
    return pltpu.CompilerParams(vmem_limit_bytes=mib * 2**20)


def cost(flops, moved):
    return pl.CostEstimate(flops=flops, bytes_accessed=moved, transcendentals=0)


def swap(size, bit):
    return [(i, i ^ bit) for i in range(size)]


def exchange(sent):
    return lax.all_to_all(sent, CHIPS, 0, 0)


def split_pairs(first, second):
    pairs = []
    for chip in range(CHIP_COUNT):
        pairs.append((chip * 2, (chip ^ first) * 2))
        pairs.append((chip * 2 + 1, (chip ^ second) * 2 + 1))
    return pairs


def second_exchange(faces):
    space = ("xh", "y", "core")
    chip = jnp.concatenate([faces, swap_cores(faces)])
    return (
        lax.ppermute(chip, space, split_pairs(1, 3)),
        lax.ppermute(chip, space, split_pairs(2, 4)),
        lax.ppermute(chip, space, split_pairs(5, 7)),
        lax.ppermute(chip[FACES:], space, split_pairs(6, 6)),
        chip,
    )


def swap_cores(own):
    return lax.ppermute(own, "core", swap(2, 1))


FACES_VMEM = VMEM((FACES, 8, SQUARE), jnp.float32)
SENT = f32(CHIP_COUNT, FACES, 8, SQUARE)


def inner_section(field, coeff, name, flops):
    chunks = SLABS // CHUNK
    return pl.pallas_call(
        inner_kernel,
        in_specs=[whole(), whole(pltpu.HBM)],
        out_specs=[whole()] * 5,
        out_shape=[
            f32(8, CELLS), bf16(VARS, 8, CELLS), bf16(VARS, 8, CELLS), bf16(2 * PER, VARS, 8, SQUARE), f32(8, LANES),
        ],
        scratch_shapes=[
            VMEM((chunks, 7, VARS, VARS, CHUNK * SQUARE), jnp.bfloat16),
            pltpu.SemaphoreType.DMA((chunks,)),
        ],
        compiler_params=params(INNER_MIB),
        cost_estimate=cost(flops, 8 * 2**20),
        name=name,
    )(field, coeff)


def mix(parts):
    return pl.pallas_call(
        mix_kernel,
        in_specs=[whole()] * 4,
        out_specs=[whole()] * 3,
        out_shape=[f32(ROWS, LANES), f32(ROWS, LANES), f32(8, LANES)],
        compiler_params=params(8),
        cost_estimate=cost(MIX, 6 * 4 * ROWS * LANES),
        name="mix",
    )(*parts)


def local(basis, flux, recon, pseudo_time, vol_omega, block_ids, neighbour, orient):
    flat = basis.reshape(KRYLOV * ROWS, LANES)
    sent, padded, dense = pl.pallas_call(
        first_faces_kernel,
        in_specs=[whole(pl.ANY)],
        out_specs=[whole(pl.ANY), whole(), whole()],
        out_shape=[SENT, f32(8, CELLS), f32(ROWS, LANES)],
        scratch_shapes=[VMEM((8 * GROUPS, LANES), jnp.float32), FACES_VMEM, pltpu.SemaphoreType.DMA((PER, CHIP_COUNT))],
        compiler_params=params(8),
        cost_estimate=cost(10**6, 2 * 2**20),
        name="first_faces",
    )(flat)
    own = exchange(sent)
    table, later = pl.pallas_call(
        tables_kernel,
        in_specs=[whole(SMEM)] * 3,
        out_specs=[whole(SMEM), whole(SMEM)],
        out_shape=[
            jax.ShapeDtypeStruct((6 * FACES,), jnp.int32),
            jax.ShapeDtypeStruct((8 * FACES,), jnp.int32),
        ],
        scratch_shapes=[SMEM((BLOCKS,), jnp.int32)],
        compiler_params=params(4),
        cost_estimate=cost(10**5, 10**5),
        name="tables",
    )(block_ids, neighbour.T, orient.T)
    *pieces, token = inner_section(padded, flux, "flux_inner", FLUX_INNER)
    gram = pl.pallas_call(
        gram_kernel,
        in_specs=[whole(pl.ANY)],
        out_specs=whole(),
        out_shape=f32(8, LANES),
        scratch_shapes=[
            VMEM((KRYLOV * ROWS, LANES), jnp.float32),
            VMEM((KRYLOV * KRYLOV, LANES), jnp.float32),
            pltpu.SemaphoreType.DMA,
        ],
        compiler_params=params(8),
        cost_estimate=cost(2 * 36 * VARS * CELLS, 2 * 2**20),
        name="gram",
    )(flat)
    kept, given, mixed = mix([dense] + [lax.ppermute(dense, "z", swap(4, k)) for k in (1, 2, 3)])
    wanted = pl.pallas_call(
        select_near_kernel,
        in_specs=[whole(SMEM), whole(), whole(pl.ANY), whole(pl.ANY)],
        out_specs=whole(),
        out_shape=f32(FACES, 8, SQUARE),
        compiler_params=params(4),
        cost_estimate=cost(10**5, 10**6),
        name="select_near",
    )(table, own, token, gram)
    swapped = swap_cores(wanted)
    first, faces = pl.pallas_call(
        flux_kernel,
        in_specs=[whole(SMEM)] + [whole()] * 6 + [whole(pl.ANY)],
        out_specs=[whole(), whole()],
        out_shape=[f32(8, CELLS), f32(FACES, 8, SQUARE)],
        scratch_shapes=[FACES_VMEM],
        compiler_params=params(OUTER_MIB),
        cost_estimate=cost(FLUX_OUTER, 4 * 2**20),
        name="flux_outer",
    )(table, own, swapped, *pieces, mixed)
    returned = lax.ppermute(given, "xl", swap(2, 1))
    *pieces, token = inner_section(first, recon, "recon_inner", RECON_INNER)
    parts = second_exchange(faces)
    wanted = pl.pallas_call(
        select_kernel,
        in_specs=[whole(SMEM)] + [whole()] * 5 + [whole(pl.ANY)],
        out_specs=whole(),
        out_shape=f32(FACES, 8, SQUARE),
        compiler_params=params(4),
        cost_estimate=cost(10**5, 10**6),
        name="select",
    )(later, *parts, token)
    swapped = swap_cores(wanted)
    image, sums, held = pl.pallas_call(
        image_kernel,
        in_specs=[whole(SMEM)] + [whole()] * 10 + [whole(pl.ANY)] + [whole()] * 5,
        out_specs=[whole(), whole(), whole()],
        out_shape=[f32(ROWS, LANES), f32(LANES, LANES), f32(KRYLOV * ROWS, LANES)],
        scratch_shapes=[FACES_VMEM, VMEM((8 * GROUPS, LANES), jnp.float32), pltpu.SemaphoreType.DMA],
        compiler_params=params(OUTER_MIB),
        cost_estimate=cost(10**6, 6 * 2**20),
        name="image",
    )(
        later, *parts, swapped, *pieces,
        flat, pseudo_time.reshape(GROUPS, LANES), vol_omega.reshape(GROUPS, LANES), kept, returned, gram,
    )
    received = lax.all_to_all(sums, ALL, 0, 0)
    following, column, flag = pl.pallas_call(
        finish_kernel,
        in_specs=[whole()] * 3,
        out_specs=[whole(), whole(pl.ANY), whole(SMEM)],
        out_shape=[f32(ROWS, LANES), f32(1, KRYLOV + 1), jax.ShapeDtypeStruct((1,), jnp.int32)],
        scratch_shapes=[VMEM((1, KRYLOV + 1), jnp.float32), pltpu.SemaphoreType.DMA],
        compiler_params=params(8),
        cost_estimate=cost(10**6, 3 * 2**20),
        name="finish",
    )(received, image, held)

    def direct(state):
        coeffs = state[1][0, :KRYLOV]
        ortho = image - jnp.einsum(
            "k,krl->rl", coeffs, flat.reshape(KRYLOV, ROWS, LANES), precision=lax.Precision.HIGHEST
        )
        squares = lax.psum(jnp.sum(ortho * ortho), ALL) / ENTRIES
        norm = jnp.sqrt(squares + 1e-06)
        return (ortho / norm, jnp.concatenate([coeffs, norm[None]])[None], jnp.zeros((), jnp.int32))

    following, column, _ = lax.while_loop(
        lambda state: state[2] > 0, direct, (following, column, flag[0])
    )
    return following.reshape(1, VARS, CELLS), column[0]


def solution(mesh):
    fine = Mesh(mesh.devices.reshape(4, 2, 2, 4, 2), ALL)
    inst, space = (("z", "xl"), ("xh", "y", "core"))
    placed = (
        P(None, inst, None, space),
        P(inst, None, None, None, space),
        P(inst, None, None, None, space),
        P(space),
        P(space),
        P(),
        P(),
        P(),
    )
    return jax.shard_map(
        local,
        mesh=fine,
        in_specs=placed,
        out_specs=(P(inst, None, space), P()),
        check_vma=False,
    )
```

```python
import jax
import jax.numpy as jnp
import numpy as np
from jax import lax
from jax.experimental import pallas as pl
from jax.experimental.pallas import tpu as pltpu
from jax.sharding import Mesh, PartitionSpec as P

EDGE = 16
SQUARE = EDGE * EDGE
CUBE = EDGE * SQUARE
VARS = 7
KRYLOV = 8
INST = 8
BLOCKS = 32
SPACE = 16
CHIP_COUNT = 8
CELLS = 8192
PER = CELLS // CUBE
FACES = 6 * PER
SLABS = CELLS // SQUARE
ENTRIES = float(INST * VARS * CELLS * SPACE)
LANES = 128
GROUPS = CELLS // LANES
ROWS = VARS * GROUPS
ALL = ("z", "xl", "xh", "y", "core")
CHIPS = ("xh", "y")
VMEM = pltpu.VMEM
SMEM = pltpu.SMEM
GUARD = 0.02
CHUNK = 4
FLUX_INNER = 10**6
INNER_MIB = 50
OUTER_MIB = 16
MIX = 5 * 10**9
GRAM = 10**9
FLUX_OUTER = 10**6
RECON_INNER = 10**6


def mixing_weights():
    k = np.arange(1, INST)
    parity = np.where(k % 2 == 0, 1.0, -1.0)
    angle = np.pi * k / INST
    rest = 0.5 * parity / np.tan(angle) - 0.125 * parity / np.sin(angle) ** 2
    return [-0.25 * (INST * INST + 2) / 12.0] + [float(v) for v in rest]


def lanes(shape):
    return lax.broadcasted_iota(jnp.int32, shape, len(shape) - 1)


def sublanes(shape):
    return lax.broadcasted_iota(jnp.int32, shape, len(shape) - 2)


def pick(values, index):
    return jnp.take_along_axis(values, index, axis=1)


def fold(totals):
    row = sublanes(totals[0].shape)
    for width in (1, 2, 4):
        first = row % (2 * width) < width
        totals = [
            jnp.where(first, a, b) + pltpu.roll(jnp.where(first, b, a), width, 0)
            for a, b in zip(totals[::2], totals[1::2])
        ]
    return totals[0]


def strips_of(slab, x, strips):
    lane = lanes((8, LANES))
    low, high = (slab[:, :LANES], slab[:, LANES:])
    own = lane >> 4 == x
    upper = lane & 8 != 0
    z = lane & 15
    source = (lane & 7) << 4
    found = (
        pick(low, z),
        pick(high, z + (LANES - EDGE)),
        jnp.where(upper, pick(high, source), pick(low, source)),
        jnp.where(upper, pick(high, source + 15), pick(low, source + 15)),
    )
    if strips is None:
        return list(found)
    return [jnp.where(own, new, old) for new, old in zip(found, strips)]


def collect_block(field_ref, faces, block):
    start = block * CUBE
    faces[block * 6] = field_ref[:, start : start + SQUARE]
    faces[block * 6 + 1] = field_ref[:, start + CUBE - SQUARE : start + CUBE]
    for half in range(2):
        strips = None
        for inner in range(8):
            place = start + (half * 8 + inner) * SQUARE
            strips = strips_of(field_ref[:, place : place + SQUARE], inner, strips)
        for number, strip in enumerate(strips):
            faces[block * 6 + 2 + number, :, half * LANES : (half + 1) * LANES] = strip


def send_block(faces, sent_ref, arrived, block):
    rows = pl.ds(block * 6, 6)
    copies = [
        pltpu.make_async_copy(faces.at[rows], sent_ref.at[chip, rows], arrived.at[block, chip])
        for chip in range(CHIP_COUNT)
    ]
    for copy in copies:
        copy.start()
    return copies


def first_faces_kernel(basis_ref, sent_ref, padded_ref, dense_ref, field, faces, arrived):
    fetch = pltpu.make_async_copy(
        basis_ref.at[pl.ds((KRYLOV - 1) * ROWS, ROWS)], field.at[pl.ds(0, ROWS)], arrived.at[0, 0]
    )
    fetch.start()
    field[ROWS:] = jnp.zeros((GROUPS, LANES), jnp.float32)
    fetch.wait()
    copies = [pltpu.make_async_copy(field.at[pl.ds(0, ROWS)], dense_ref, arrived.at[PER, 0])]
    copies[0].start()
    for block in range(PER):
        for group in range(block * 32, block * 32 + 32):
            padded_ref[:, group * LANES : (group + 1) * LANES] = field[pl.ds(group, 8, stride=GROUPS), :]
        collect_block(padded_ref, faces, block)
        copies += send_block(faces, sent_ref, arrived, block)
    for copy in copies:
        copy.wait()


def tables_kernel(ids_ref, neighbour_ref, orient_ref, table_ref, later_ref, position):
    core = lax.axis_index("core")
    chip = lax.axis_index("xh") * 4 + lax.axis_index("y")

    def place(slot, carry):
        position[ids_ref[slot]] = slot
        return carry

    lax.fori_loop(0, BLOCKS, place, 0)

    for mine in (True, False):
        for number in range(FACES):
            rank = chip * 2 + (core if mine else 1 - core)
            owner = ids_ref[rank * PER + number // 6]
            partner = neighbour_ref[number % 6, owner]
            target = jnp.maximum(partner, 0)
            slot = position[target // 6]
            device = slot // PER
            row = (slot % PER) * 6 + target % 6
            source_core = device % 2
            offset = (device // 2) ^ chip
            part = offset & 3
            among = (offset >> 2) * FACES + row
            if mine:
                code = jnp.where(partner < 0, -1, orient_ref[number % 6, owner])
                same = source_core == core
                table_ref[number * 4] = device // 2
                table_ref[number * 4 + 1] = jnp.where(same, 1, 0)
                table_ref[number * 4 + 2] = row
                table_ref[number * 4 + 3] = code
                later_ref[number * 4] = part
                later_ref[number * 4 + 1] = among
                later_ref[number * 4 + 2] = jnp.where(same, 1, 0)
                later_ref[number * 4 + 3] = code
            else:
                table_ref[4 * FACES + number * 2] = device // 2
                table_ref[4 * FACES + number * 2 + 1] = row
                later_ref[4 * FACES + number * 2] = part
                later_ref[4 * FACES + number * 2 + 1] = among


def choose(parts, part, among):
    value = parts[0][among]
    for k in range(1, 4):
        value = jnp.where(part == k, parts[k][among], value)
    return value


def select_kernel(
    later_ref, pair_ref, one_ref, two_ref, three_ref, token_ref, mixed_ref, gram_ref, wanted_ref
):
    parts = (pair_ref, one_ref, two_ref, three_ref)
    for number in range(FACES):
        base = 4 * FACES + number * 2
        wanted_ref[number] = choose(parts, later_ref[base], later_ref[base + 1])


def select_near_kernel(table_ref, own_ref, token_ref, wanted_ref):
    for number in range(FACES):
        base = 4 * FACES + number * 2
        wanted_ref[number] = own_ref[table_ref[base], table_ref[base + 1]]


def turn_face(source, code, halos, number):
    lane = lanes((8, LANES))
    source = jnp.where(code < 0, 0.0, source)
    code = jnp.maximum(code, 0)
    low, high = (source[:, :LANES], source[:, LANES:])
    transposed = code & 1 == 1
    flip_a = (code >> 1 & 1) * (EDGE - 1)
    flip_b = (code >> 2) * (EDGE - 1)
    for half in range(2):
        a = ((lane >> 4) + half * 8) ^ flip_a
        b = (lane & 15) ^ flip_b
        index = jnp.where(transposed, (b << 4) + a, (a << 4) + b)
        inside = index & (LANES - 1)
        halos[number, :, half * LANES : (half + 1) * LANES] = jnp.where(
            index < LANES, pick(low, inside), pick(high, inside)
        )


def fetch_halos(table_ref, own_ref, swapped_ref, halos):
    for number in range(FACES):
        chip = table_ref[number * 4]
        here = table_ref[number * 4 + 1] == 1
        row = table_ref[number * 4 + 2]
        source = jnp.where(here, own_ref[chip, row], swapped_ref[number])
        turn_face(source, table_ref[number * 4 + 3], halos, number)


def fetch_later_halos(later_ref, parts, swapped_ref, halos):
    for number in range(FACES):
        base = number * 4
        source = choose(parts, later_ref[base], later_ref[base + 1])
        source = jnp.where(later_ref[base + 2] == 1, source, swapped_ref[number])
        turn_face(source, later_ref[base + 3], halos, number)


def inner_kernel(
    field_ref, coeff_ref, part_ref, across_z_ref, across_y_ref, across_x_ref, token_ref, held, arrived
):
    column = lanes((8, SQUARE))
    z = column & 15
    width = CHUNK * SQUARE
    chunks = SLABS // CHUNK
    copies = [
        pltpu.make_async_copy(coeff_ref.at[0, :, :, :, pl.ds(i * width, width)], held.at[i], arrived.at[i])
        for i in range(chunks)
    ]
    for copy in copies:
        copy.start()

    def load(k):
        return field_ref[:, pl.ds(pl.multiple_of(k * SQUARE, SQUARE), SQUARE)]

    def chunk_step(chunk, carry):
        pltpu.make_async_copy(
            coeff_ref.at[0, :, :, :, pl.ds(0, width)], held.at[chunk], arrived.at[chunk]
        ).wait()
        for inner in range(CHUNK):

            def coeff(s, o):
                value = held[chunk, s, o, :, inner * SQUARE : (inner + 1) * SQUARE].astype(jnp.float32)
                return jnp.concatenate([value, jnp.zeros((1, SQUARE), jnp.float32)], axis=0)

            k = chunk * CHUNK + inner
            block, x = (k // EDGE, k % EDGE)
            place = pl.ds(pl.multiple_of(k * SQUARE, SQUARE), SQUARE)
            centre = load(k)
            below, above = (load(jnp.maximum(k - 1, 0)), load(jnp.minimum(k + 1, SLABS - 1)))
            if inner == 0:
                below = jnp.where(x == 0, 0.0, below)
            if inner == CHUNK - 1:
                above = jnp.where(x == EDGE - 1, 0.0, above)
            operands = [
                centre,
                below,
                above,
                jnp.where(column < EDGE, 0.0, pltpu.roll(centre, EDGE, 1)),
                jnp.where(column >= SQUARE - EDGE, 0.0, pltpu.roll(centre, SQUARE - EDGE, 1)),
                jnp.where(z == 0, 0.0, pltpu.roll(centre, 1, 1)),
                jnp.where(z == EDGE - 1, 0.0, pltpu.roll(centre, SQUARE - 1, 1)),
            ]
            totals = []
            for o in range(VARS):
                values = [coeff(s, o) for s in range(7)]
                total = values[0] * operands[0]
                for s in range(1, 7):
                    total = total + values[s] * operands[s]
                totals.append(total)
                across_z_ref[o, :, place] = jnp.where(
                    z == 0, values[5], jnp.where(z == EDGE - 1, values[6], 0.0)
                ).astype(jnp.bfloat16)
                across_y_ref[o, :, place] = jnp.where(
                    column < EDGE, values[3], jnp.where(column >= SQUARE - EDGE, values[4], 0.0)
                ).astype(jnp.bfloat16)
            part_ref[:, place] = fold(totals + [jnp.zeros((8, SQUARE), jnp.float32)])

            if inner == 0:

                @pl.when(x == 0)
                def _():
                    for o in range(VARS):
                        across_x_ref[block * 2, o] = coeff(1, o).astype(jnp.bfloat16)

            if inner == CHUNK - 1:

                @pl.when(x == EDGE - 1)
                def _():
                    for o in range(VARS):
                        across_x_ref[block * 2 + 1, o] = coeff(2, o).astype(jnp.bfloat16)

        return carry

    lax.fori_loop(0, chunks, chunk_step, 0)
    token_ref[...] = jnp.zeros_like(token_ref)


def outer_slab(part_ref, across_z_ref, across_y_ref, halos, block, half, inner):
    lane = lanes((8, LANES))
    offset = inner * EDGE
    start = block * CUBE + (half * 8 + inner) * SQUARE
    place = slice(start, start + SQUARE)

    def strip(face):
        return halos[block * 6 + face, :, half * LANES : (half + 1) * LANES]

    y = (lane & 15) + offset
    z = (lane >> 4) + offset
    at_low = lane & 15 == 0
    across_y = jnp.concatenate([pick(strip(2), y), pick(strip(3), y)], axis=1)
    z_low, z_high = (strip(4), strip(5))
    across_z = jnp.concatenate(
        [
            jnp.where(at_low, pick(z_low, z), pick(z_high, z)),
            jnp.where(at_low, pick(z_low, z + 8), pick(z_high, z + 8)),
        ],
        axis=1,
    )
    totals = [
        across_z_ref[o, :, place].astype(jnp.float32) * across_z
        + across_y_ref[o, :, place].astype(jnp.float32) * across_y
        for o in range(VARS)
    ]
    return part_ref[:, place] + fold(totals + [jnp.zeros((8, SQUARE), jnp.float32)])


def outer_x(across_x_ref, halos, block, side):
    halo = halos[block * 6 + side]
    totals = [across_x_ref[block * 2 + side, o].astype(jnp.float32) * halo for o in range(VARS)]
    return fold(totals + [jnp.zeros((8, SQUARE), jnp.float32)])


def outer_block(across_x_ref, part_ref, across_z_ref, across_y_ref, halos, block, put):
    for half in range(2):
        for inner in range(8):
            slab = outer_slab(part_ref, across_z_ref, across_y_ref, halos, block, half, inner)
            if half == 0 and inner == 0:
                slab = slab + outer_x(across_x_ref, halos, block, 0)
            if half == 1 and inner == 7:
                slab = slab + outer_x(across_x_ref, halos, block, 1)
            put(block * EDGE + half * 8 + inner, slab)


def flux_kernel(
    table_ref, own_ref, swapped_ref, part_ref, across_z_ref, across_y_ref, across_x_ref,
    z_one_ref, z_two_ref, z_three_ref, first_ref, faces_ref, halos
):
    fetch_halos(table_ref, own_ref, swapped_ref, halos)

    def put(k, slab):
        first_ref[:, k * SQUARE : (k + 1) * SQUARE] = slab

    for block in range(PER):
        outer_block(across_x_ref, part_ref, across_z_ref, across_y_ref, halos, block, put)
        collect_block(first_ref, faces_ref, block)


def mix_kernel(own_ref, one_ref, two_ref, three_ref, pair_ref, kept_ref, given_ref, token_ref):
    z = lax.axis_index("z")
    xl = lax.axis_index("xl")
    table = mixing_weights()

    def weight(offset):
        offset = lax.rem(offset + 2 * INST, INST)
        value = jnp.float32(table[0])
        for k in range(1, INST):
            value = jnp.where(offset == k, jnp.float32(table[k]), value)
        return value

    fields = (own_ref, one_ref, two_ref, three_ref)
    sources = [2 * (z ^ k) + xl for k in range(4)]
    kept = [weight(source - (2 * z + xl)) for source in sources]
    given = [weight(source - (2 * z + 1 - xl)) for source in sources]

    def step(k, carry):
        rows = pl.ds(pl.multiple_of(k * 64, 64), 64)
        values = [field[rows] for field in fields]
        kept_ref[rows] = sum(w * v for w, v in zip(kept, values))
        given_ref[rows] = sum(w * v for w, v in zip(given, values))
        return carry

    lax.fori_loop(0, ROWS // 64, step, 0)
    token_ref[...] = jnp.zeros_like(token_ref)


def lane_sums(rows, first_lane):
    totals = jnp.broadcast_to(jnp.sum(rows, axis=1, keepdims=True), rows.shape)
    spot = lanes(rows.shape) == sublanes(rows.shape) + first_lane
    return jnp.sum(jnp.where(spot, totals, 0.0), axis=0, keepdims=True)


def gram_kernel(flat_ref, pair_ref, gram_ref, basis_ref, lines, arrived):
    copy = pltpu.make_async_copy(flat_ref, basis_ref, arrived)
    copy.start()
    copy.wait()

    def step(k, totals):
        fields = [
            basis_ref[pl.ds(pl.multiple_of(j * ROWS + k * 8, 8), 8)] for j in range(KRYLOV)
        ]
        out = []
        for i in range(KRYLOV):
            for j in range(i, KRYLOV):
                out.append(totals[len(out)] + fields[i] * fields[j])
        return tuple(out)

    zero = jnp.zeros((8, LANES), jnp.float32)
    totals = lax.fori_loop(0, ROWS // 8, step, (zero,) * (KRYLOV * (KRYLOV + 1) // 2))
    number = 0
    for i in range(KRYLOV):
        for j in range(i, KRYLOV):
            line = jnp.sum(totals[number], axis=0, keepdims=True)
            lines[i * KRYLOV + j : i * KRYLOV + j + 1] = line
            lines[j * KRYLOV + i : j * KRYLOV + i + 1] = line
            number += 1
    gram_ref[...] = jnp.broadcast_to(lane_sums(lines[...], 64), (8, LANES))


def image_kernel(
    later_ref, pair_ref, one_ref, two_ref, three_ref, swapped_ref,
    part_ref, across_z_ref, across_y_ref, across_x_ref,
    flat_ref, pseudo_ref, omega_ref, kept_ref, returned_ref, gram_ref,
    image_ref, sums_ref, basis_ref, halos, section, arrived
):
    copy = pltpu.make_async_copy(flat_ref, basis_ref, arrived)
    copy.start()
    fetch_later_halos(later_ref, (pair_ref, one_ref, two_ref, three_ref), swapped_ref, halos)

    def put(k, slab):
        section[pl.ds(2 * k, 8, stride=GROUPS), :] = slab[:, :LANES]
        section[pl.ds(2 * k + 1, 8, stride=GROUPS), :] = slab[:, LANES:]

    for block in range(PER):
        outer_block(across_x_ref, part_ref, across_z_ref, across_y_ref, halos, block, put)
    copy.wait()

    def step(k, totals):
        start = k * 8
        cells = pl.ds(pl.multiple_of(start % GROUPS, 8), 8)
        rows = pl.ds(pl.multiple_of(start, 8), 8)
        fields = [basis_ref[pl.ds(pl.multiple_of(j * ROWS + start, 8), 8)] for j in range(KRYLOV)]
        spectral = kept_ref[rows] + returned_ref[rows]
        image = pseudo_ref[cells] * fields[KRYLOV - 1] + section[rows] + omega_ref[cells] * spectral
        image_ref[rows] = image
        return tuple(total + field * image for total, field in zip(totals, fields + [image]))

    zero = jnp.zeros((8, LANES), jnp.float32)
    totals = lax.fori_loop(0, ROWS // 8, step, (zero,) * (KRYLOV + 1), unroll=8)
    lines = [jnp.sum(total, axis=0, keepdims=True) for total in totals]
    lines += [jnp.zeros((16 - len(lines), LANES), jnp.float32)]
    sums = jnp.broadcast_to(lane_sums(jnp.concatenate(lines, axis=0), 0), (8, LANES)) + gram_ref[...]
    for group in range(16):
        sums_ref[group * 8 : group * 8 + 8] = sums


def finish_kernel(received_ref, image_ref, basis_ref, next_ref, column_ref, flag_ref, column_held, sent):
    sums = jnp.sum(received_ref[...], axis=0, keepdims=True)
    sums = jnp.broadcast_to(sums, (8, LANES)) / ENTRIES
    lane = lanes((8, LANES))
    left = pick(sums, jnp.maximum(lane - 64, 0) // 8)
    right = pick(sums, lane % 8)
    quadratic = jnp.sum(jnp.where(lane >= 64, sums * left * right, 0.0), axis=1, keepdims=True)
    linear = jnp.sum(jnp.where(lane < KRYLOV, sums * sums, 0.0), axis=1, keepdims=True)
    whole_square = sums[:, KRYLOV : KRYLOV + 1]
    squares = whole_square - 2.0 * linear + quadratic
    size = whole_square + 2.0 * linear + jnp.abs(quadratic)
    norm = jnp.sqrt(jnp.maximum(squares, 0.0) + 1e-06)
    column = jnp.where(lane < KRYLOV, sums, jnp.where(lane == KRYLOV, norm, 0.0))
    column_held[...] = column[:1, : KRYLOV + 1]
    copy = pltpu.make_async_copy(column_held, column_ref, sent)
    copy.start()
    flag_ref[0] = jnp.sum(jnp.where(squares[:1] < GUARD * size[:1], 1.0, 0.0)).astype(jnp.int32)
    coeffs = [jnp.broadcast_to(sums[:, j : j + 1], (8, LANES)) for j in range(KRYLOV)]
    scale = jnp.broadcast_to(1.0 / norm, (8, LANES))

    def step(k, carry):
        start = k * 8
        rows = pl.ds(pl.multiple_of(start, 8), 8)
        ortho = image_ref[rows]
        for j in range(KRYLOV):
            ortho = ortho - coeffs[j] * basis_ref[pl.ds(pl.multiple_of(j * ROWS + start, 8), 8)]
        next_ref[rows] = ortho * scale
        return carry

    lax.fori_loop(0, ROWS // 8, step, 0, unroll=8)
    copy.wait()


def whole(memory=VMEM):
    return pl.BlockSpec(memory_space=memory)


def f32(*shape):
    return jax.ShapeDtypeStruct(shape, jnp.float32)


def bf16(*shape):
    return jax.ShapeDtypeStruct(shape, jnp.bfloat16)


def params(mib):
    return pltpu.CompilerParams(vmem_limit_bytes=mib * 2**20)


def cost(flops, moved):
    return pl.CostEstimate(flops=flops, bytes_accessed=moved, transcendentals=0)


def swap(size, bit):
    return [(i, i ^ bit) for i in range(size)]


def exchange(sent):
    return lax.all_to_all(sent, CHIPS, 0, 0)


def chip_pairs(offset):
    return [(rank, rank ^ (2 * offset)) for rank in range(SPACE)]


def second_exchange(faces, token):
    space = ("xh", "y", "core")
    other, token = lax.optimization_barrier((lax.ppermute(faces, space, chip_pairs(4)), token))
    pair = jnp.concatenate([faces, other])
    return token, [pair] + [lax.ppermute(pair, space, chip_pairs(offset)) for offset in (1, 2, 3)]


def swap_cores(own):
    return lax.ppermute(own, "core", swap(2, 1))


FACES_VMEM = VMEM((FACES, 8, SQUARE), jnp.float32)
SENT = f32(CHIP_COUNT, FACES, 8, SQUARE)


def inner_section(field, coeff, name, flops):
    chunks = SLABS // CHUNK
    return pl.pallas_call(
        inner_kernel,
        in_specs=[whole(), whole(pltpu.HBM)],
        out_specs=[whole()] * 5,
        out_shape=[
            f32(8, CELLS), bf16(VARS, 8, CELLS), bf16(VARS, 8, CELLS), bf16(2 * PER, VARS, 8, SQUARE), f32(8, LANES),
        ],
        scratch_shapes=[
            VMEM((chunks, 7, VARS, VARS, CHUNK * SQUARE), jnp.bfloat16),
            pltpu.SemaphoreType.DMA((chunks,)),
        ],
        compiler_params=params(INNER_MIB),
        cost_estimate=cost(flops, 2**10),
        name=name,
    )(field, coeff)


def mix(parts, pair):
    return pl.pallas_call(
        mix_kernel,
        in_specs=[whole()] * 4 + [whole(pl.ANY)],
        out_specs=[whole()] * 3,
        out_shape=[f32(ROWS, LANES), f32(ROWS, LANES), f32(8, LANES)],
        compiler_params=params(8),
        cost_estimate=cost(MIX, 6 * 4 * ROWS * LANES),
        name="mix",
    )(*parts, pair)


def local(basis, flux, recon, pseudo_time, vol_omega, block_ids, neighbour, orient):
    flat = basis.reshape(KRYLOV * ROWS, LANES)
    sent, padded, dense = pl.pallas_call(
        first_faces_kernel,
        in_specs=[whole(pl.ANY)],
        out_specs=[whole(pl.ANY), whole(), whole(pl.ANY)],
        out_shape=[SENT, f32(8, CELLS), f32(ROWS, LANES)],
        scratch_shapes=[VMEM((8 * GROUPS, LANES), jnp.float32), FACES_VMEM, pltpu.SemaphoreType.DMA((PER + 1, CHIP_COUNT))],
        compiler_params=params(8),
        cost_estimate=cost(10**6, 2 * 2**20),
        name="first_faces",
    )(flat)
    own = exchange(sent)
    table, later = pl.pallas_call(
        tables_kernel,
        in_specs=[whole(SMEM)] * 3,
        out_specs=[whole(SMEM), whole(SMEM)],
        out_shape=[
            jax.ShapeDtypeStruct((6 * FACES,), jnp.int32),
            jax.ShapeDtypeStruct((6 * FACES,), jnp.int32),
        ],
        scratch_shapes=[SMEM((BLOCKS,), jnp.int32)],
        compiler_params=params(4),
        cost_estimate=cost(10**5, 10**5),
        name="tables",
    )(block_ids, neighbour.T, orient.T)
    *pieces, token = inner_section(padded, flux, "flux_inner", FLUX_INNER)
    others = [lax.ppermute(dense, "z", swap(4, k)) for k in (1, 2, 3)]
    wanted = pl.pallas_call(
        select_near_kernel,
        in_specs=[whole(SMEM), whole(), whole(pl.ANY)],
        out_specs=whole(),
        out_shape=f32(FACES, 8, SQUARE),
        compiler_params=params(4),
        cost_estimate=cost(10**5, 10**6),
        name="select_near",
    )(table, own, token)
    swapped = swap_cores(wanted)
    first, faces = pl.pallas_call(
        flux_kernel,
        in_specs=[whole(SMEM)] + [whole()] * 6 + [whole(pl.ANY)] * 3,
        out_specs=[whole(), whole()],
        out_shape=[f32(8, CELLS), f32(FACES, 8, SQUARE)],
        scratch_shapes=[FACES_VMEM],
        compiler_params=params(OUTER_MIB),
        cost_estimate=cost(1, 1),
        name="flux_outer",
    )(table, own, swapped, *pieces, *others)
    *pieces, token = inner_section(first, recon, "recon_inner", RECON_INNER)
    token, parts = second_exchange(faces, token)
    kept, given, mixed = mix([dense] + others, parts[0])
    returned = lax.ppermute(given, "xl", swap(2, 1))
    gram = pl.pallas_call(
        gram_kernel,
        in_specs=[whole(pl.ANY)] * 2,
        out_specs=whole(),
        out_shape=f32(8, LANES),
        scratch_shapes=[
            VMEM((KRYLOV * ROWS, LANES), jnp.float32),
            VMEM((KRYLOV * KRYLOV, LANES), jnp.float32),
            pltpu.SemaphoreType.DMA,
        ],
        compiler_params=params(8),
        cost_estimate=cost(GRAM, 2 * 2**20),
        name="gram",
    )(flat, parts[0])
    wanted = pl.pallas_call(
        select_kernel,
        in_specs=[whole(SMEM)] + [whole()] * 4 + [whole(pl.ANY)] * 3,
        out_specs=whole(),
        out_shape=f32(FACES, 8, SQUARE),
        compiler_params=params(4),
        cost_estimate=cost(10**5, 10**6),
        name="select",
    )(later, *parts, token, mixed, gram)
    swapped = swap_cores(wanted)
    image, sums, held = pl.pallas_call(
        image_kernel,
        in_specs=[whole(SMEM)] + [whole()] * 9 + [whole(pl.ANY)] + [whole()] * 5,
        out_specs=[whole(), whole(), whole()],
        out_shape=[f32(ROWS, LANES), f32(LANES, LANES), f32(KRYLOV * ROWS, LANES)],
        scratch_shapes=[FACES_VMEM, VMEM((8 * GROUPS, LANES), jnp.float32), pltpu.SemaphoreType.DMA],
        compiler_params=params(OUTER_MIB),
        cost_estimate=cost(10**6, 6 * 2**20),
        name="image",
    )(
        later, *parts, swapped, *pieces,
        flat, pseudo_time.reshape(GROUPS, LANES), vol_omega.reshape(GROUPS, LANES), kept, returned, gram,
    )
    received = lax.all_to_all(sums, ALL, 0, 0)
    following, column, flag = pl.pallas_call(
        finish_kernel,
        in_specs=[whole()] * 3,
        out_specs=[whole(), whole(pl.ANY), whole(SMEM)],
        out_shape=[f32(ROWS, LANES), f32(1, KRYLOV + 1), jax.ShapeDtypeStruct((1,), jnp.int32)],
        scratch_shapes=[VMEM((1, KRYLOV + 1), jnp.float32), pltpu.SemaphoreType.DMA],
        compiler_params=params(8),
        cost_estimate=cost(10**6, 3 * 2**20),
        name="finish",
    )(received, image, held)

    def direct(state):
        coeffs = state[1][0, :KRYLOV]
        ortho = image - jnp.einsum(
            "k,krl->rl", coeffs, flat.reshape(KRYLOV, ROWS, LANES), precision=lax.Precision.HIGHEST
        )
        squares = lax.psum(jnp.sum(ortho * ortho), ALL) / ENTRIES
        norm = jnp.sqrt(squares + 1e-06)
        return (ortho / norm, jnp.concatenate([coeffs, norm[None]])[None], jnp.zeros((), jnp.int32))

    following, column, _ = lax.while_loop(
        lambda state: state[2] > 0, direct, (following, column, flag[0])
    )
    return following.reshape(1, VARS, CELLS), column[0]


def solution(mesh):
    fine = Mesh(mesh.devices.reshape(4, 2, 2, 4, 2), ALL)
    inst, space = (("z", "xl"), ("xh", "y", "core"))
    placed = (
        P(None, inst, None, space),
        P(inst, None, None, None, space),
        P(inst, None, None, None, space),
        P(space),
        P(space),
        P(),
        P(),
        P(),
    )
    return jax.shard_map(
        local,
        mesh=fine,
        in_specs=placed,
        out_specs=(P(inst, None, space), P()),
        check_vma=False,
    )
```

```python
import jax
import jax.numpy as jnp
import numpy as np
from jax import lax
from jax.experimental import pallas as pl
from jax.experimental.pallas import tpu as pltpu
from jax.sharding import Mesh, PartitionSpec as P

EDGE = 16
SQUARE = EDGE * EDGE
CUBE = EDGE * SQUARE
VARS = 7
KRYLOV = 8
INST = 8
BLOCKS = 32
SPACE = 16
CHIP_COUNT = 8
CELLS = 8192
PER = CELLS // CUBE
FACES = 6 * PER
SLABS = CELLS // SQUARE
ENTRIES = float(INST * VARS * CELLS * SPACE)
LANES = 128
GROUPS = CELLS // LANES
ROWS = VARS * GROUPS
ALL = ("z", "xl", "xh", "y", "core")
CHIPS = ("xh", "y")
VMEM = pltpu.VMEM
SMEM = pltpu.SMEM
GUARD = 0.02
CHUNK = 4
FLUX_INNER = 10**6
INNER_MIB = 50
OUTER_MIB = 16
MIX = 5 * 10**9
GRAM = 10**9
FLUX_OUTER = 10**6
RECON_INNER = 10**6


def mixing_weights():
    k = np.arange(1, INST)
    parity = np.where(k % 2 == 0, 1.0, -1.0)
    angle = np.pi * k / INST
    rest = 0.5 * parity / np.tan(angle) - 0.125 * parity / np.sin(angle) ** 2
    return [-0.25 * (INST * INST + 2) / 12.0] + [float(v) for v in rest]


def lanes(shape):
    return lax.broadcasted_iota(jnp.int32, shape, len(shape) - 1)


def sublanes(shape):
    return lax.broadcasted_iota(jnp.int32, shape, len(shape) - 2)


def pick(values, index):
    return jnp.take_along_axis(values, index, axis=1)


def fold(totals):
    row = sublanes(totals[0].shape)
    for width in (1, 2, 4):
        first = row % (2 * width) < width
        totals = [
            jnp.where(first, a, b) + pltpu.roll(jnp.where(first, b, a), width, 0)
            for a, b in zip(totals[::2], totals[1::2])
        ]
    return totals[0]


def strips_of(slab, x, strips):
    lane = lanes((8, LANES))
    low, high = (slab[:, :LANES], slab[:, LANES:])
    own = lane >> 4 == x
    upper = lane & 8 != 0
    z = lane & 15
    source = (lane & 7) << 4
    found = (
        pick(low, z),
        pick(high, z + (LANES - EDGE)),
        jnp.where(upper, pick(high, source), pick(low, source)),
        jnp.where(upper, pick(high, source + 15), pick(low, source + 15)),
    )
    if strips is None:
        return list(found)
    return [jnp.where(own, new, old) for new, old in zip(found, strips)]


def collect_block(field_ref, faces, block):
    start = block * CUBE
    faces[block * 6] = field_ref[:, start : start + SQUARE]
    faces[block * 6 + 1] = field_ref[:, start + CUBE - SQUARE : start + CUBE]
    for half in range(2):
        strips = None
        for inner in range(8):
            place = start + (half * 8 + inner) * SQUARE
            strips = strips_of(field_ref[:, place : place + SQUARE], inner, strips)
        for number, strip in enumerate(strips):
            faces[block * 6 + 2 + number, :, half * LANES : (half + 1) * LANES] = strip


def send_block(faces, sent_ref, arrived, block):
    rows = pl.ds(block * 6, 6)
    copies = [
        pltpu.make_async_copy(faces.at[rows], sent_ref.at[chip, rows], arrived.at[block, chip])
        for chip in range(CHIP_COUNT)
    ]
    for copy in copies:
        copy.start()
    return copies


def first_faces_kernel(basis_ref, sent_ref, padded_ref, dense_ref, field, faces, arrived):
    fetch = pltpu.make_async_copy(
        basis_ref.at[pl.ds((KRYLOV - 1) * ROWS, ROWS)], field.at[pl.ds(0, ROWS)], arrived.at[0, 0]
    )
    fetch.start()
    field[ROWS:] = jnp.zeros((GROUPS, LANES), jnp.float32)
    fetch.wait()
    copies = [pltpu.make_async_copy(field.at[pl.ds(0, ROWS)], dense_ref, arrived.at[PER, 0])]
    copies[0].start()
    for block in range(PER):
        for group in range(block * 32, block * 32 + 32):
            padded_ref[:, group * LANES : (group + 1) * LANES] = field[pl.ds(group, 8, stride=GROUPS), :]
        collect_block(padded_ref, faces, block)
        copies += send_block(faces, sent_ref, arrived, block)
    for copy in copies:
        copy.wait()


def tables_kernel(ids_ref, neighbour_ref, orient_ref, table_ref, later_ref, position):
    core = lax.axis_index("core")
    chip = lax.axis_index("xh") * 4 + lax.axis_index("y")

    def place(slot, carry):
        position[ids_ref[slot]] = slot
        return carry

    lax.fori_loop(0, BLOCKS, place, 0)

    for mine in (True, False):
        for number in range(FACES):
            rank = chip * 2 + (core if mine else 1 - core)
            owner = ids_ref[rank * PER + number // 6]
            partner = neighbour_ref[number % 6, owner]
            target = jnp.maximum(partner, 0)
            slot = position[target // 6]
            device = slot // PER
            row = (slot % PER) * 6 + target % 6
            source_core = device % 2
            offset = (device // 2) ^ chip
            part = offset & 3
            among = (offset >> 2) * FACES + row
            if mine:
                code = jnp.where(partner < 0, -1, orient_ref[number % 6, owner])
                same = source_core == core
                table_ref[number * 4] = device // 2
                table_ref[number * 4 + 1] = jnp.where(same, 1, 0)
                table_ref[number * 4 + 2] = row
                table_ref[number * 4 + 3] = code
                later_ref[number * 4] = part
                later_ref[number * 4 + 1] = among
                later_ref[number * 4 + 2] = jnp.where(same, 1, 0)
                later_ref[number * 4 + 3] = code
            else:
                table_ref[4 * FACES + number * 2] = device // 2
                table_ref[4 * FACES + number * 2 + 1] = row
                later_ref[4 * FACES + number * 2] = part
                later_ref[4 * FACES + number * 2 + 1] = among


def choose(parts, part, among):
    value = parts[0][among]
    for k in range(1, 4):
        value = jnp.where(part == k, parts[k][among], value)
    return value


def select_kernel(
    later_ref, pair_ref, one_ref, two_ref, three_ref, token_ref, mixed_ref, gram_ref, wanted_ref
):
    parts = (pair_ref, one_ref, two_ref, three_ref)
    for number in range(FACES):
        base = 4 * FACES + number * 2
        wanted_ref[number] = choose(parts, later_ref[base], later_ref[base + 1])


def select_near_kernel(table_ref, own_ref, token_ref, wanted_ref):
    for number in range(FACES):
        base = 4 * FACES + number * 2
        wanted_ref[number] = own_ref[table_ref[base], table_ref[base + 1]]


def turn_face(source, code, halos, number):
    lane = lanes((8, LANES))
    source = jnp.where(code < 0, 0.0, source)
    code = jnp.maximum(code, 0)
    low, high = (source[:, :LANES], source[:, LANES:])
    transposed = code & 1 == 1
    flip_a = (code >> 1 & 1) * (EDGE - 1)
    flip_b = (code >> 2) * (EDGE - 1)
    for half in range(2):
        a = ((lane >> 4) + half * 8) ^ flip_a
        b = (lane & 15) ^ flip_b
        index = jnp.where(transposed, (b << 4) + a, (a << 4) + b)
        inside = index & (LANES - 1)
        halos[number, :, half * LANES : (half + 1) * LANES] = jnp.where(
            index < LANES, pick(low, inside), pick(high, inside)
        )


def fetch_halos(table_ref, own_ref, swapped_ref, halos):
    for number in range(FACES):
        chip = table_ref[number * 4]
        here = table_ref[number * 4 + 1] == 1
        row = table_ref[number * 4 + 2]
        source = jnp.where(here, own_ref[chip, row], swapped_ref[number])
        turn_face(source, table_ref[number * 4 + 3], halos, number)


def fetch_later_halos(later_ref, parts, swapped_ref, halos):
    for number in range(FACES):
        base = number * 4
        source = choose(parts, later_ref[base], later_ref[base + 1])
        source = jnp.where(later_ref[base + 2] == 1, source, swapped_ref[number])
        turn_face(source, later_ref[base + 3], halos, number)


def inner_kernel(
    field_ref, coeff_ref, part_ref, across_z_ref, across_y_ref, across_x_ref, token_ref, held, arrived
):
    column = lanes((8, SQUARE))
    z = column & 15
    width = CHUNK * SQUARE
    chunks = SLABS // CHUNK
    copies = [
        pltpu.make_async_copy(coeff_ref.at[0, :, :, :, pl.ds(i * width, width)], held.at[i], arrived.at[i])
        for i in range(chunks)
    ]
    for copy in copies:
        copy.start()

    def load(k):
        return field_ref[:, pl.ds(pl.multiple_of(k * SQUARE, SQUARE), SQUARE)]

    def chunk_step(chunk, carry):
        pltpu.make_async_copy(
            coeff_ref.at[0, :, :, :, pl.ds(0, width)], held.at[chunk], arrived.at[chunk]
        ).wait()
        for inner in range(CHUNK):

            def coeff(s, o):
                value = held[chunk, s, o, :, inner * SQUARE : (inner + 1) * SQUARE].astype(jnp.float32)
                return jnp.concatenate([value, jnp.zeros((1, SQUARE), jnp.float32)], axis=0)

            k = chunk * CHUNK + inner
            block, x = (k // EDGE, k % EDGE)
            place = pl.ds(pl.multiple_of(k * SQUARE, SQUARE), SQUARE)
            centre = load(k)
            below, above = (load(jnp.maximum(k - 1, 0)), load(jnp.minimum(k + 1, SLABS - 1)))
            if inner == 0:
                below = jnp.where(x == 0, 0.0, below)
            if inner == CHUNK - 1:
                above = jnp.where(x == EDGE - 1, 0.0, above)
            operands = [
                centre,
                below,
                above,
                jnp.where(column < EDGE, 0.0, pltpu.roll(centre, EDGE, 1)),
                jnp.where(column >= SQUARE - EDGE, 0.0, pltpu.roll(centre, SQUARE - EDGE, 1)),
                jnp.where(z == 0, 0.0, pltpu.roll(centre, 1, 1)),
                jnp.where(z == EDGE - 1, 0.0, pltpu.roll(centre, SQUARE - 1, 1)),
            ]
            totals = []
            for o in range(VARS):
                values = [coeff(s, o) for s in range(7)]
                total = values[0] * operands[0]
                for s in range(1, 7):
                    total = total + values[s] * operands[s]
                totals.append(total)
                across_z_ref[o, :, place] = jnp.where(
                    z == 0, values[5], jnp.where(z == EDGE - 1, values[6], 0.0)
                ).astype(jnp.bfloat16)
                across_y_ref[o, :, place] = jnp.where(
                    column < EDGE, values[3], jnp.where(column >= SQUARE - EDGE, values[4], 0.0)
                ).astype(jnp.bfloat16)
            part_ref[:, place] = fold(totals + [jnp.zeros((8, SQUARE), jnp.float32)])

            if inner == 0:

                @pl.when(x == 0)
                def _():
                    for o in range(VARS):
                        across_x_ref[block * 2, o] = coeff(1, o).astype(jnp.bfloat16)

            if inner == CHUNK - 1:

                @pl.when(x == EDGE - 1)
                def _():
                    for o in range(VARS):
                        across_x_ref[block * 2 + 1, o] = coeff(2, o).astype(jnp.bfloat16)

        return carry

    lax.fori_loop(0, chunks, chunk_step, 0)
    token_ref[...] = jnp.zeros_like(token_ref)


def outer_slab(part_ref, across_z_ref, across_y_ref, halos, block, half, inner):
    lane = lanes((8, LANES))
    offset = inner * EDGE
    start = block * CUBE + (half * 8 + inner) * SQUARE
    place = slice(start, start + SQUARE)

    def strip(face):
        return halos[block * 6 + face, :, half * LANES : (half + 1) * LANES]

    y = (lane & 15) + offset
    z = (lane >> 4) + offset
    at_low = lane & 15 == 0
    across_y = jnp.concatenate([pick(strip(2), y), pick(strip(3), y)], axis=1)
    z_low, z_high = (strip(4), strip(5))
    across_z = jnp.concatenate(
        [
            jnp.where(at_low, pick(z_low, z), pick(z_high, z)),
            jnp.where(at_low, pick(z_low, z + 8), pick(z_high, z + 8)),
        ],
        axis=1,
    )
    totals = [
        across_z_ref[o, :, place].astype(jnp.float32) * across_z
        + across_y_ref[o, :, place].astype(jnp.float32) * across_y
        for o in range(VARS)
    ]
    return part_ref[:, place] + fold(totals + [jnp.zeros((8, SQUARE), jnp.float32)])


def outer_x(across_x_ref, halos, block, side):
    halo = halos[block * 6 + side]
    totals = [across_x_ref[block * 2 + side, o].astype(jnp.float32) * halo for o in range(VARS)]
    return fold(totals + [jnp.zeros((8, SQUARE), jnp.float32)])


def outer_block(across_x_ref, part_ref, across_z_ref, across_y_ref, halos, block, put):
    for half in range(2):
        for inner in range(8):
            slab = outer_slab(part_ref, across_z_ref, across_y_ref, halos, block, half, inner)
            if half == 0 and inner == 0:
                slab = slab + outer_x(across_x_ref, halos, block, 0)
            if half == 1 and inner == 7:
                slab = slab + outer_x(across_x_ref, halos, block, 1)
            put(block * EDGE + half * 8 + inner, slab)


def flux_kernel(
    table_ref, own_ref, swapped_ref, part_ref, across_z_ref, across_y_ref, across_x_ref,
    z_one_ref, z_two_ref, z_three_ref, first_ref, faces_ref, halos
):
    fetch_halos(table_ref, own_ref, swapped_ref, halos)

    def put(k, slab):
        first_ref[:, k * SQUARE : (k + 1) * SQUARE] = slab

    for block in range(PER):
        outer_block(across_x_ref, part_ref, across_z_ref, across_y_ref, halos, block, put)
        collect_block(first_ref, faces_ref, block)


def mix_kernel(own_ref, one_ref, two_ref, three_ref, pair_ref, kept_ref, given_ref, token_ref):
    z = lax.axis_index("z")
    xl = lax.axis_index("xl")
    table = mixing_weights()

    def weight(offset):
        offset = lax.rem(offset + 2 * INST, INST)
        value = jnp.float32(table[0])
        for k in range(1, INST):
            value = jnp.where(offset == k, jnp.float32(table[k]), value)
        return value

    fields = (own_ref, one_ref, two_ref, three_ref)
    sources = [2 * (z ^ k) + xl for k in range(4)]
    kept = [weight(source - (2 * z + xl)) for source in sources]
    given = [weight(source - (2 * z + 1 - xl)) for source in sources]

    def step(k, carry):
        rows = pl.ds(pl.multiple_of(k * 64, 64), 64)
        values = [field[rows] for field in fields]
        kept_ref[rows] = sum(w * v for w, v in zip(kept, values))
        given_ref[rows] = sum(w * v for w, v in zip(given, values))
        return carry

    lax.fori_loop(0, ROWS // 64, step, 0)
    token_ref[...] = jnp.zeros_like(token_ref)


def lane_sums(rows, first_lane):
    totals = jnp.broadcast_to(jnp.sum(rows, axis=1, keepdims=True), rows.shape)
    spot = lanes(rows.shape) == sublanes(rows.shape) + first_lane
    return jnp.sum(jnp.where(spot, totals, 0.0), axis=0, keepdims=True)


def gram_kernel(flat_ref, pair_ref, gram_ref, basis_ref, lines, arrived):
    copy = pltpu.make_async_copy(flat_ref, basis_ref, arrived)
    copy.start()
    copy.wait()

    def step(k, totals):
        fields = [
            basis_ref[pl.ds(pl.multiple_of(j * ROWS + k * 8, 8), 8)] for j in range(KRYLOV)
        ]
        out = []
        for i in range(KRYLOV):
            for j in range(i, KRYLOV):
                out.append(totals[len(out)] + fields[i] * fields[j])
        return tuple(out)

    zero = jnp.zeros((8, LANES), jnp.float32)
    totals = lax.fori_loop(0, ROWS // 8, step, (zero,) * (KRYLOV * (KRYLOV + 1) // 2))
    number = 0
    for i in range(KRYLOV):
        for j in range(i, KRYLOV):
            line = jnp.sum(totals[number], axis=0, keepdims=True)
            lines[i * KRYLOV + j : i * KRYLOV + j + 1] = line
            lines[j * KRYLOV + i : j * KRYLOV + i + 1] = line
            number += 1
    gram_ref[...] = jnp.broadcast_to(lane_sums(lines[...], 64), (8, LANES))


def image_kernel(
    later_ref, pair_ref, one_ref, two_ref, three_ref, swapped_ref,
    part_ref, across_z_ref, across_y_ref, across_x_ref,
    flat_ref, pseudo_ref, omega_ref, kept_ref, returned_ref, gram_ref,
    image_ref, sums_ref, basis_ref, halos, section, arrived
):
    copy = pltpu.make_async_copy(flat_ref, basis_ref, arrived)
    copy.start()
    fetch_later_halos(later_ref, (pair_ref, one_ref, two_ref, three_ref), swapped_ref, halos)

    def put(k, slab):
        section[pl.ds(2 * k, 8, stride=GROUPS), :] = slab[:, :LANES]
        section[pl.ds(2 * k + 1, 8, stride=GROUPS), :] = slab[:, LANES:]

    for block in range(PER):
        outer_block(across_x_ref, part_ref, across_z_ref, across_y_ref, halos, block, put)
    copy.wait()

    def step(k, totals):
        start = k * 8
        cells = pl.ds(pl.multiple_of(start % GROUPS, 8), 8)
        rows = pl.ds(pl.multiple_of(start, 8), 8)
        fields = [basis_ref[pl.ds(pl.multiple_of(j * ROWS + start, 8), 8)] for j in range(KRYLOV)]
        spectral = kept_ref[rows] + returned_ref[rows]
        image = pseudo_ref[cells] * fields[KRYLOV - 1] + section[rows] + omega_ref[cells] * spectral
        image_ref[rows] = image
        return tuple(total + field * image for total, field in zip(totals, fields + [image]))

    zero = jnp.zeros((8, LANES), jnp.float32)
    totals = lax.fori_loop(0, ROWS // 8, step, (zero,) * (KRYLOV + 1), unroll=8)
    lines = [jnp.sum(total, axis=0, keepdims=True) for total in totals]
    lines += [jnp.zeros((16 - len(lines), LANES), jnp.float32)]
    sums = jnp.broadcast_to(lane_sums(jnp.concatenate(lines, axis=0), 0), (8, LANES)) + gram_ref[...]
    for group in range(16):
        sums_ref[group * 8 : group * 8 + 8] = sums


def finish_kernel(received_ref, image_ref, basis_ref, next_ref, column_ref, flag_ref, column_held, sent):
    sums = jnp.sum(received_ref[...], axis=0, keepdims=True)
    sums = jnp.broadcast_to(sums, (8, LANES)) / ENTRIES
    lane = lanes((8, LANES))
    left = pick(sums, jnp.maximum(lane - 64, 0) // 8)
    right = pick(sums, lane % 8)
    quadratic = jnp.sum(jnp.where(lane >= 64, sums * left * right, 0.0), axis=1, keepdims=True)
    linear = jnp.sum(jnp.where(lane < KRYLOV, sums * sums, 0.0), axis=1, keepdims=True)
    whole_square = sums[:, KRYLOV : KRYLOV + 1]
    squares = whole_square - 2.0 * linear + quadratic
    size = whole_square + 2.0 * linear + jnp.abs(quadratic)
    norm = jnp.sqrt(jnp.maximum(squares, 0.0) + 1e-06)
    column = jnp.where(lane < KRYLOV, sums, jnp.where(lane == KRYLOV, norm, 0.0))
    column_held[...] = column[:1, : KRYLOV + 1]
    copy = pltpu.make_async_copy(column_held, column_ref, sent)
    copy.start()
    flag_ref[0] = jnp.sum(jnp.where(squares[:1] < GUARD * size[:1], 1.0, 0.0)).astype(jnp.int32)
    coeffs = [jnp.broadcast_to(sums[:, j : j + 1], (8, LANES)) for j in range(KRYLOV)]
    scale = jnp.broadcast_to(1.0 / norm, (8, LANES))

    def step(k, carry):
        start = k * 8
        rows = pl.ds(pl.multiple_of(start, 8), 8)
        ortho = image_ref[rows]
        for j in range(KRYLOV):
            ortho = ortho - coeffs[j] * basis_ref[pl.ds(pl.multiple_of(j * ROWS + start, 8), 8)]
        next_ref[rows] = ortho * scale
        return carry

    lax.fori_loop(0, ROWS // 8, step, 0, unroll=8)
    copy.wait()


def whole(memory=VMEM):
    return pl.BlockSpec(memory_space=memory)


def f32(*shape):
    return jax.ShapeDtypeStruct(shape, jnp.float32)


def bf16(*shape):
    return jax.ShapeDtypeStruct(shape, jnp.bfloat16)


def params(mib):
    return pltpu.CompilerParams(vmem_limit_bytes=mib * 2**20)


def cost(flops, moved):
    return pl.CostEstimate(flops=flops, bytes_accessed=moved, transcendentals=0)


def swap(size, bit):
    return [(i, i ^ bit) for i in range(size)]


def exchange(sent):
    return lax.all_to_all(sent, CHIPS, 0, 0)


def chip_pairs(offset):
    return [(rank, rank ^ (2 * offset)) for rank in range(SPACE)]


def second_exchange(faces, token):
    space = ("xh", "y", "core")
    other, token = lax.optimization_barrier((lax.ppermute(faces, space, chip_pairs(4)), token))
    pair = jnp.concatenate([faces, other])
    one, three, two = [lax.ppermute(pair, space, chip_pairs(offset)) for offset in (1, 3, 2)]
    return token, [pair, one, two, three]


def swap_cores(own):
    return lax.ppermute(own, "core", swap(2, 1))


FACES_VMEM = VMEM((FACES, 8, SQUARE), jnp.float32)
SENT = f32(CHIP_COUNT, FACES, 8, SQUARE)


def inner_section(field, coeff, name, flops):
    chunks = SLABS // CHUNK
    return pl.pallas_call(
        inner_kernel,
        in_specs=[whole(), whole(pltpu.HBM)],
        out_specs=[whole()] * 5,
        out_shape=[
            f32(8, CELLS), bf16(VARS, 8, CELLS), bf16(VARS, 8, CELLS), bf16(2 * PER, VARS, 8, SQUARE), f32(8, LANES),
        ],
        scratch_shapes=[
            VMEM((chunks, 7, VARS, VARS, CHUNK * SQUARE), jnp.bfloat16),
            pltpu.SemaphoreType.DMA((chunks,)),
        ],
        compiler_params=params(INNER_MIB),
        cost_estimate=cost(flops, 2**10),
        name=name,
    )(field, coeff)


def mix(parts, pair):
    return pl.pallas_call(
        mix_kernel,
        in_specs=[whole()] * 4 + [whole(pl.ANY)],
        out_specs=[whole()] * 3,
        out_shape=[f32(ROWS, LANES), f32(ROWS, LANES), f32(8, LANES)],
        compiler_params=params(8),
        cost_estimate=cost(MIX, 6 * 4 * ROWS * LANES),
        name="mix",
    )(*parts, pair)


def local(basis, flux, recon, pseudo_time, vol_omega, block_ids, neighbour, orient):
    flat = basis.reshape(KRYLOV * ROWS, LANES)
    sent, padded, dense = pl.pallas_call(
        first_faces_kernel,
        in_specs=[whole(pl.ANY)],
        out_specs=[whole(pl.ANY), whole(), whole(pl.ANY)],
        out_shape=[SENT, f32(8, CELLS), f32(ROWS, LANES)],
        scratch_shapes=[VMEM((8 * GROUPS, LANES), jnp.float32), FACES_VMEM, pltpu.SemaphoreType.DMA((PER + 1, CHIP_COUNT))],
        compiler_params=params(8),
        cost_estimate=cost(10**6, 2 * 2**20),
        name="first_faces",
    )(flat)
    own = exchange(sent)
    table, later = pl.pallas_call(
        tables_kernel,
        in_specs=[whole(SMEM)] * 3,
        out_specs=[whole(SMEM), whole(SMEM)],
        out_shape=[
            jax.ShapeDtypeStruct((6 * FACES,), jnp.int32),
            jax.ShapeDtypeStruct((6 * FACES,), jnp.int32),
        ],
        scratch_shapes=[SMEM((BLOCKS,), jnp.int32)],
        compiler_params=params(4),
        cost_estimate=cost(10**5, 10**5),
        name="tables",
    )(block_ids, neighbour.T, orient.T)
    *pieces, token = inner_section(padded, flux, "flux_inner", FLUX_INNER)
    others = [lax.ppermute(dense, "z", swap(4, k)) for k in (1, 2, 3)]
    wanted = pl.pallas_call(
        select_near_kernel,
        in_specs=[whole(SMEM), whole(), whole(pl.ANY)],
        out_specs=whole(),
        out_shape=f32(FACES, 8, SQUARE),
        compiler_params=params(4),
        cost_estimate=cost(10**5, 10**6),
        name="select_near",
    )(table, own, token)
    swapped = swap_cores(wanted)
    first, faces = pl.pallas_call(
        flux_kernel,
        in_specs=[whole(SMEM)] + [whole()] * 6 + [whole(pl.ANY)] * 3,
        out_specs=[whole(), whole()],
        out_shape=[f32(8, CELLS), f32(FACES, 8, SQUARE)],
        scratch_shapes=[FACES_VMEM],
        compiler_params=params(OUTER_MIB),
        cost_estimate=cost(1, 1),
        name="flux_outer",
    )(table, own, swapped, *pieces, *others)
    *pieces, token = inner_section(first, recon, "recon_inner", RECON_INNER)
    token, parts = second_exchange(faces, token)
    kept, given, mixed = mix([dense] + others, parts[0])
    returned = lax.ppermute(given, "xl", swap(2, 1))
    gram = pl.pallas_call(
        gram_kernel,
        in_specs=[whole(pl.ANY)] * 2,
        out_specs=whole(),
        out_shape=f32(8, LANES),
        scratch_shapes=[
            VMEM((KRYLOV * ROWS, LANES), jnp.float32),
            VMEM((KRYLOV * KRYLOV, LANES), jnp.float32),
            pltpu.SemaphoreType.DMA,
        ],
        compiler_params=params(8),
        cost_estimate=cost(GRAM, 2 * 2**20),
        name="gram",
    )(flat, parts[0])
    wanted = pl.pallas_call(
        select_kernel,
        in_specs=[whole(SMEM)] + [whole()] * 4 + [whole(pl.ANY)] * 3,
        out_specs=whole(),
        out_shape=f32(FACES, 8, SQUARE),
        compiler_params=params(4),
        cost_estimate=cost(10**5, 10**6),
        name="select",
    )(later, *parts, token, mixed, gram)
    swapped = swap_cores(wanted)
    image, sums, held = pl.pallas_call(
        image_kernel,
        in_specs=[whole(SMEM)] + [whole()] * 9 + [whole(pl.ANY)] + [whole()] * 5,
        out_specs=[whole(), whole(), whole()],
        out_shape=[f32(ROWS, LANES), f32(LANES, LANES), f32(KRYLOV * ROWS, LANES)],
        scratch_shapes=[FACES_VMEM, VMEM((8 * GROUPS, LANES), jnp.float32), pltpu.SemaphoreType.DMA],
        compiler_params=params(OUTER_MIB),
        cost_estimate=cost(10**6, 6 * 2**20),
        name="image",
    )(
        later, *parts, swapped, *pieces,
        flat, pseudo_time.reshape(GROUPS, LANES), vol_omega.reshape(GROUPS, LANES), kept, returned, gram,
    )
    received = lax.all_to_all(sums, ALL, 0, 0)
    following, column, flag = pl.pallas_call(
        finish_kernel,
        in_specs=[whole()] * 3,
        out_specs=[whole(), whole(pl.ANY), whole(SMEM)],
        out_shape=[f32(ROWS, LANES), f32(1, KRYLOV + 1), jax.ShapeDtypeStruct((1,), jnp.int32)],
        scratch_shapes=[VMEM((1, KRYLOV + 1), jnp.float32), pltpu.SemaphoreType.DMA],
        compiler_params=params(8),
        cost_estimate=cost(10**6, 3 * 2**20),
        name="finish",
    )(received, image, held)

    def direct(state):
        coeffs = state[1][0, :KRYLOV]
        ortho = image - jnp.einsum(
            "k,krl->rl", coeffs, flat.reshape(KRYLOV, ROWS, LANES), precision=lax.Precision.HIGHEST
        )
        squares = lax.psum(jnp.sum(ortho * ortho), ALL) / ENTRIES
        norm = jnp.sqrt(squares + 1e-06)
        return (ortho / norm, jnp.concatenate([coeffs, norm[None]])[None], jnp.zeros((), jnp.int32))

    following, column, _ = lax.while_loop(
        lambda state: state[2] > 0, direct, (following, column, flag[0])
    )
    return following.reshape(1, VARS, CELLS), column[0]


def solution(mesh):
    fine = Mesh(mesh.devices.reshape(4, 2, 2, 4, 2), ALL)
    inst, space = (("z", "xl"), ("xh", "y", "core"))
    placed = (
        P(None, inst, None, space),
        P(inst, None, None, None, space),
        P(inst, None, None, None, space),
        P(space),
        P(space),
        P(),
        P(),
        P(),
    )
    return jax.shard_map(
        local,
        mesh=fine,
        in_specs=placed,
        out_specs=(P(inst, None, space), P()),
        check_vma=False,
    )
```
